128 devices in a mesh: dp: 2 (over core), pipe: 4 (over x), height: 16 (over z, y).
Axes of the slice: x: 4, y: 4, z: 4, core: 2. Of those that a mesh axis runs over, the one named last changes fastest.
Arguments:
- video: bfloat16 [2, 12, 64, 16, 256], P('dp', None, 'height'), may hold values from -48 to 48
- kernels: bfloat16 [4, 6912, 256], P('pipe'), may hold values from -0.078125 to 0.078125
- gains: float32 [4, 256], P('pipe'), may hold values from 0.1 to 1.9
- shifts: float32 [4, 256], P('pipe'), may hold values from -3 to 3
- out_grad: bfloat16 [2, 12, 64, 16, 256], P('dp', None, 'height'), may hold values from -0.48 to 0.48
Outputs:
- kernel_grad: float32 [4, 6912, 256], P('pipe', ('dp', 'height'))
- norm_grad: float32 [4, 2, 256], P('pipe')
The draws below stay inside these ranges and needn't reach their ends.
All inputs are finite; a program needn't handle non-finite values.
Results may differ from the reference program's by a relative error of at most 0.0067.
Values may be sent and summed in bfloat16 or wider, within the bound.
A program may use at most 64 MiB of HBM per device.

```python
import math
import jax
import jax.numpy as jnp
from jax import lax

C = 256
GROUPS = 32
COLS = 16
FRAMES = 4
SPANS = 3
CLIPS = 2
SECTIONS = 4
H = 64
TIME = 12


def scaled_field(key, scale, direction, level_step, offset_size):
    keys = jax.random.split(key, 7)
    shape = (CLIPS, TIME, H, COLS, C)
    heights = jnp.arange(H, dtype=jnp.float32) / max(H - 1, 1)
    oriented = 0.5 + direction * (heights - 0.5)
    row_scale = 0.3 * jnp.exp(oriented * math.log(10.0))
    col_scale = jnp.exp(jax.random.uniform(keys[0], (COLS,), jnp.float32, math.log(0.5), math.log(2.0)))
    chan_scale = jnp.exp(jax.random.uniform(keys[1], (C,), jnp.float32, math.log(0.5), math.log(2.0)))
    values = jnp.clip(jax.random.normal(keys[3], shape, jnp.float32), -4.0, 4.0)
    ranks = jax.random.permutation(keys[4], SPANS).astype(jnp.float32)
    jitter = jax.random.uniform(keys[5], (SPANS,), jnp.float32, 0.0, 0.2)
    block_level = jnp.exp(-level_step * (ranks + jitter * jnp.minimum(ranks, 1.0)))
    block_offset = jax.random.uniform(keys[6], (SPANS, C), jnp.float32, -1.0, 1.0) * offset_size
    frame_block = jnp.arange(TIME) // FRAMES
    frame_level = block_level[frame_block]
    frame_offset = block_offset[frame_block]
    scaled = values * row_scale[None, None, :, None, None] * col_scale[None, None, None, :, None] * chan_scale
    scaled = scale * scaled * frame_level[None, :, None, None, None] + frame_offset[None, :, None, None, :]
    return scaled.astype(jnp.bfloat16)


def draw_video(key, part):
    key = jax.random.fold_in(key, 3)
    return scaled_field(key, 0.85, 1.0, 0.7, 4.0)


def draw_out_grad(key, part):
    key = jax.random.fold_in(key, 7)
    return scaled_field(key, 0.01, -1.0, 0.0, 0.0)


def block_scale(rng, dims, cuts, least, largest):
    level, own = 1.0, jax.random.fold_in(rng, 6)
    for position, blocks in cuts:
        draws = jnp.exp(jax.random.uniform(jax.random.fold_in(own, position), (blocks,), jnp.float32, least / len(cuts), largest / len(cuts)))
        level = level * jnp.repeat(draws, dims[position] // blocks).reshape([-1 if axis == position else 1 for axis in range(len(dims))])
    return level


def normal_values(key, shape, deviation, reach, cuts=(), kind=jnp.bfloat16):
    array = jax.random.normal(key, shape, jnp.float32) * deviation
    if len(cuts) > 0:
        array = block_scale(key, shape, cuts, -0.22, 0.18) * array
    return jnp.clip(array, min=-reach, max=reach).astype(kind)


def setup_inputs(seed: int = 0) -> dict:
    streams_of = jax.random.split(jax.random.key(seed), 6)
    return {
        "video": draw_video(jax.random.fold_in(streams_of[5], 71), 0),
        "kernels": normal_values(streams_of[1], (SECTIONS, 27 * C, C), (27 * C) ** -0.5, 0.078125, ((0, 4),)),
        "gains": jnp.clip(1.0 + 0.18 * jax.random.normal(streams_of[2], (SECTIONS, C), jnp.float32), 0.1, 1.9),
        "shifts": normal_values(streams_of[3], (SECTIONS, C), 0.5, 3.0, ((0, 4),), jnp.float32),
        "out_grad": draw_out_grad(jax.random.fold_in(streams_of[5], 71), 0),
    }


eps = 1e-05

def tap_patches(padded):
    frames = padded.shape[1] - 2
    band_rows = padded.shape[2] - 2
    columns = padded.shape[3] - 2
    pieces = []
    for tap_time in range(3):
        for tap_row in range(3):
            for tap_col in range(3):
                pieces.append(padded[:, tap_time:tap_time + frames, tap_row:tap_row + band_rows, tap_col:tap_col + columns, :])
    stacked = jnp.concatenate(pieces, axis=-1)
    return stacked.reshape(-1, stacked.shape[-1])

def spatial_pad(time_ext):
    return jnp.pad(time_ext, ((0, 0), (0, 0), (1, 1), (1, 1), (0, 0)))

def flipped(kernel):
    channels = kernel.shape[1]
    taps = kernel.reshape(3, 3, 3, channels, channels)[::-1, ::-1, ::-1]
    return jnp.transpose(taps, (0, 1, 2, 4, 3)).reshape(27 * channels, channels)

def silu_slope(pre_act):
    sigmoid_z = jax.nn.sigmoid(pre_act)
    return sigmoid_z * (1.0 + pre_act * (1.0 - sigmoid_z))

def group_norm(conv_out, per_group, group_size):
    grouped = conv_out.reshape(conv_out.shape[0], conv_out.shape[1], GROUPS, per_group)
    mean_value = lax.optimization_barrier(jnp.sum(grouped, axis=(1, 3))) / group_size
    centered = grouped - mean_value[:, None, :, None]
    variance = lax.optimization_barrier(jnp.sum(centered * centered, axis=(1, 3))) / group_size
    inv_std = lax.rsqrt(variance + eps)
    normed = (centered * inv_std[:, None, :, None]).reshape(conv_out.shape)
    return (normed, inv_std)

def reference(video, kernels, gains, shifts, out_grad):
    clips = video.shape[0]
    channels = video.shape[4]
    frames = FRAMES
    per_group = channels // GROUPS
    positions = frames * video.shape[2] * video.shape[3]
    group_size = float(positions * per_group)
    frame_shape = (clips, frames) + video.shape[2:]
    edge_shape = (clips, 2) + video.shape[2:]
    records = []
    layer_in = video
    for section_index in range(SECTIONS):
        kernel = kernels[section_index]
        time_tail = jnp.zeros(edge_shape, jnp.bfloat16)
        outputs = []
        section_records = []
        for span_index in range(SPANS):
            current = layer_in[:, span_index * frames:(span_index + 1) * frames]
            padded = spatial_pad(jnp.concatenate([time_tail, current], axis=1))
            conv_out = jnp.dot(tap_patches(padded), kernel, preferred_element_type=jnp.float32).reshape(clips, positions, channels)
            normed, inv_std = group_norm(conv_out, per_group, group_size)
            pre_act = normed * gains[section_index] + shifts[section_index]
            result = (current.reshape(clips, positions, channels).astype(jnp.float32) + jax.nn.silu(pre_act)).astype(jnp.bfloat16)
            outputs.append(result.reshape(frame_shape))
            section_records.append((padded, normed, inv_std))
            time_tail = current[:, frames - 2:]
        layer_in = jnp.concatenate(outputs, axis=1)
        records.append(section_records)
    kernel_grads = []
    norm_grads = []
    upstream_all = out_grad
    for section_index in reversed(range(SECTIONS)):
        kernel = kernels[section_index]
        back_kernel = flipped(kernel)
        gain_vec = gains[section_index]
        time_head = jnp.zeros(edge_shape, jnp.bfloat16)
        kernel_total = jnp.zeros((27 * channels, channels), jnp.float32)
        gain_total = jnp.zeros((channels,), jnp.float32)
        shift_total = jnp.zeros((channels,), jnp.float32)
        grad_spans = [None] * SPANS
        for span_index in reversed(range(SPANS)):
            padded, normed, inv_std = records[section_index][span_index]
            upstream = upstream_all[:, span_index * frames:(span_index + 1) * frames].reshape(clips, positions, channels).astype(jnp.float32)
            pre_act = normed * gain_vec + shifts[section_index]
            grad_pre = upstream * silu_slope(pre_act)
            gain_total = gain_total + lax.optimization_barrier(jnp.sum(grad_pre * normed, axis=(0, 1)))
            shift_total = shift_total + lax.optimization_barrier(jnp.sum(grad_pre, axis=(0, 1)))
            grad_normed = (grad_pre * gain_vec).reshape(clips, positions, GROUPS, per_group)
            normed_groups = normed.reshape(clips, positions, GROUPS, per_group)
            first_mean = lax.optimization_barrier(jnp.sum(grad_normed, axis=(1, 3))) / group_size
            second_mean = lax.optimization_barrier(jnp.sum(grad_normed * normed_groups, axis=(1, 3))) / group_size
            grad_conv_out = ((grad_normed - first_mean[:, None, :, None] - normed_groups * second_mean[:, None, :, None]) * inv_std[:, None, :, None]).astype(jnp.bfloat16).reshape(clips * positions, channels)
            kernel_total = kernel_total + lax.dot_general(tap_patches(padded), grad_conv_out, (((0,), (0,)), ((), ())), preferred_element_type=jnp.float32)
            grad_frames = grad_conv_out.reshape(frame_shape)
            if section_index > 0:
                padded_grad = spatial_pad(jnp.concatenate([grad_frames, time_head], axis=1))
                grad_input = jnp.dot(tap_patches(padded_grad), back_kernel, preferred_element_type=jnp.float32).reshape(clips, positions, channels)
                grad_spans[span_index] = (upstream + grad_input).astype(jnp.bfloat16).reshape(frame_shape)
            time_head = grad_frames[:, :2]
        if section_index > 0:
            upstream_all = jnp.concatenate(grad_spans, axis=1)
        kernel_grads.insert(0, kernel_total)
        norm_grads.insert(0, jnp.stack([gain_total, shift_total]))
    return (jnp.stack(kernel_grads), jnp.stack(norm_grads))
```

```python
import functools

import jax
import jax.numpy as jnp
from jax import lax
from jax.experimental import pallas as pl
from jax.experimental.pallas import tpu as pltpu
from jax.sharding import PartitionSpec as P

GROUPS = 32
F = 4
SPANS = 3
NB = 16
LAYERS = 4
R = 4
W16 = 16
C = 256
POS = F * R * W16
GSIZE = float(POS * NB * (C // GROUPS))
HALF = 3456
SHARE = 216
EPS = 1e-05
f32 = jnp.float32
bf16 = jnp.bfloat16
MESH = pl.DeviceIdType.MESH


def group_sum(x):
    lane = lax.broadcasted_iota(jnp.int32, x.shape, 1)
    for d in (1, 2, 4):
        x = x + jnp.where((lane & d) != 0, pltpu.roll(x, d, 1), pltpu.roll(x, C - d, 1))
    return x


def combine(table):
    sums = jnp.sum(table, axis=0)
    mean_c = sums[0:1] * (1.0 / NB)
    between = jnp.sum((table - mean_c[None]) ** 2, axis=0)[0:1]
    dev_c = sums[1:2] + POS * between
    per = C // GROUPS
    mu = group_sum(mean_c) * (1.0 / per)
    var = group_sum(dev_c + (POS * NB) * (mean_c - mu) ** 2) * (1.0 / GSIZE)
    return mu, lax.rsqrt(var + EPS)


def sigmoid(v):
    return 1.0 / (1.0 + jnp.exp(-v))


def put_shifted(dst, frame, x):
    v = x.reshape(F * 6, W16, C)
    col = lax.broadcasted_iota(jnp.int32, v.shape, 1)
    left = jnp.where(col == 0, 0.0, pltpu.roll(v, 1, 1))
    right = jnp.where(col == W16 - 1, 0.0, pltpu.roll(v, W16 - 1, 1))
    dst[frame : frame + F, :, :, 0:C] = left.astype(bf16).reshape(F, 6, W16, C)
    dst[frame : frame + F, :, :, C : 2 * C] = v.astype(bf16).reshape(F, 6, W16, C)
    dst[frame : frame + F, :, :, 2 * C : 3 * C] = right.astype(bf16).reshape(F, 6, W16, C)


def kernel(
    video, kern, gains, shifts, ograd, out_k, out_n,
    W, XP, XR, CP, CO, CF, S, PX, PS, G, GG, UR, UO, STP, STO, SB, SBO, GO, GP, NP, LP, NO, LO,
    WG, RSS, RSR, NG,
    w_sem, l_sem, xpc, xph, cp, stp, sto, cfh, ur, sb, px, pg, rr, ngs, gps,
    s_x, s_xr, s_c, s_ch, s_sto, s_stn, s_px, s_pg, s_ur, s_og, s_sb, s_sbo, s_rs, s_ng, s_gp,
):
    dp, s, h = lax.axis_index("dp"), lax.axis_index("pipe"), lax.axis_index("height")
    nxt, prv = lax.rem(s + 1, LAYERS), lax.rem(s + LAYERS - 1, LAYERS)
    up, dn = lax.rem(h + NB - 1, NB), lax.rem(h + 1, NB)
    other = 1 - dp

    def remote(src, dst, ssem, rsem, dev):
        pltpu.make_async_remote_copy(
            src_ref=src, dst_ref=dst, send_sem=ssem, recv_sem=rsem, device_id=dev, device_id_type=MESH
        ).start()

    def await_bytes(ref, sem):
        pltpu.make_async_copy(ref, ref, sem).wait()

    def fr(k):
        return pl.ds(F * k, F)

    wcopy = pltpu.make_async_copy(kern.at[0], W, w_sem)
    wcopy.start()
    barrier = pltpu.get_barrier_semaphore()
    for j in range(1, NB):
        pl.semaphore_signal(barrier, inc=1, device_id=(dp, s, lax.rem(h + j, NB)), device_id_type=MESH)
    for j in range(NB):
        b = lax.rem(h + j, NB)
        pl.semaphore_signal(barrier, inc=1, device_id=(dp, nxt, b), device_id_type=MESH)
        pl.semaphore_signal(barrier, inc=1, device_id=(dp, prv, b), device_id_type=MESH)
    pl.semaphore_signal(barrier, inc=1, device_id=(other, s, h), device_id_type=MESH)

    @pl.when(s <= 1)
    def _():
        for k in range(SPANS):
            pltpu.make_async_copy(video.at[0, fr(k)], XP.at[fr(k), pl.ds(1, R)], xpc.at[k]).start()

    @pl.when(s == LAYERS - 1)
    def _():
        for k in range(SPANS):
            pltpu.make_async_copy(ograd.at[0, fr(k)], UR.at[fr(k), pl.ds(1, R)], ur.at[k]).start()

    S[0:2] = jnp.zeros((2, 6, W16, 3 * C), bf16)
    PS[0:2] = jnp.zeros((2, 6, W16, 3 * C), bf16)
    G[12:14] = jnp.zeros((2, 6, W16, 3 * C), bf16)
    GO[0:1] = gains[...]
    GO[1:2] = shifts[...]
    pl.semaphore_wait(barrier, 3 * NB)

    @pl.when(s <= 1)
    def _():
        for k in range(SPANS):
            remote(video.at[0, fr(k), pl.ds(0, 1)], XP.at[fr(k), pl.ds(5, 1)], s_xr.at[k], xph.at[k], (dp, s, up))
            remote(video.at[0, fr(k), pl.ds(3, 1)], XP.at[fr(k), pl.ds(0, 1)], s_xr.at[k], xph.at[k], (dp, s, dn))

    @pl.when(s == LAYERS - 1)
    def _():
        for k in reversed(range(SPANS)):
            remote(ograd.at[0, fr(k), pl.ds(0, 1)], UR.at[fr(k), pl.ds(5, 1)], s_og.at[k], ur.at[k], (dp, s, up))
            remote(ograd.at[0, fr(k), pl.ds(3, 1)], UR.at[fr(k), pl.ds(0, 1)], s_og.at[k], ur.at[k], (dp, s, dn))

    @pl.when(s < LAYERS - 1)
    def _():
        remote(GO, GP, s_gp, gps, (dp, nxt, h))

    @pl.when(s > 0)
    def _():
        await_bytes(GP, gps)

    row = lax.broadcasted_iota(jnp.int32, (1, 6, 1, 1), 1)
    valid = jnp.where(row == 0, (h > 0).astype(f32), jnp.where(row == 5, (h < NB - 1).astype(f32), 1.0))

    def normalized(conv, table_ref, k):
        mu, inv = combine(table_ref[k])
        own = (table_ref[k, h][0:1] - mu).reshape(1, 1, 1, C)
        above = (table_ref[k, up][0:1] - mu).reshape(1, 1, 1, C)
        below = (table_ref[k, dn][0:1] - mu).reshape(1, 1, 1, C)
        off = jnp.concatenate([above, own, own, own, own, below], axis=1)
        return (conv + off) * inv.reshape(1, 1, 1, C), inv

    for k in range(SPANS):
        await_bytes(XP.at[fr(k), pl.ds(1, R)], xpc.at[k])

        @pl.when(s >= 2)
        def _():
            remote(XP.at[fr(k), pl.ds(1, 1)], XP.at[fr(k), pl.ds(5, 1)], s_xr.at[k], xph.at[k], (dp, s, up))
            remote(XP.at[fr(k), pl.ds(4, 1)], XP.at[fr(k), pl.ds(0, 1)], s_xr.at[k], xph.at[k], (dp, s, dn))

        await_bytes(XP.at[fr(k), pl.ds(0, 2)], xph.at[k])

        @pl.when(s == 0)
        def _():
            x = XP[F * k : F * k + F].astype(f32) * valid
            XR[F * k : F * k + F] = x.astype(bf16)
            put_shifted(S, 2 + F * k, x)

        @pl.when(s > 0)
        def _():
            await_bytes(STP.at[k], stp.at[k])
            await_bytes(CP.at[fr(k)], cp.at[k])
            normed, _ = normalized(CP[F * k : F * k + F].astype(f32), STP, k)
            pre = normed * GP[0:1].reshape(1, 1, 1, C) + GP[1:2].reshape(1, 1, 1, C)
            sig = sigmoid(pre)
            x = XP[F * k : F * k + F].astype(f32) + pre * sig
            x16 = (x * valid).astype(bf16)
            XR[F * k : F * k + F] = x16

            @pl.when(s < LAYERS - 1)
            def _():
                remote(XR.at[fr(k), pl.ds(1, R)], XP.at[fr(k), pl.ds(1, R)], s_x.at[k], xpc.at[k], (dp, nxt, h))

            put_shifted(S, 2 + F * k, x16.astype(f32))
            NP[k] = normed[:, 1:5].reshape(POS, C)
            LP[k] = (sig * (1.0 + pre * (1.0 - sig)))[:, 1:5].reshape(POS, C)

        if k == 0:
            wcopy.wait()
        acc = None
        for ab in range(9):
            a, b = divmod(ab, 3)
            lhs = S[F * k + a : F * k + a + F, b : b + R].reshape(POS, 3 * C)
            d = jnp.dot(lhs, W[ab * 768 : ab * 768 + 768, :], preferred_element_type=f32)
            acc = d if acc is None else acc + d
        mean = jnp.sum(acc, axis=0, keepdims=True) * (1.0 / POS)
        cen = acc - mean
        STO[k, h] = jnp.concatenate([mean, jnp.sum(cen * cen, axis=0, keepdims=True)], axis=0)
        CF[F * k : F * k + F, 1:5] = cen.reshape(F, R, W16, C)
        CO[F * k : F * k + F] = cen.astype(bf16).reshape(F, R, W16, C)

        @pl.when(s < LAYERS - 1)
        def _():
            for j in range(NB):
                remote(STO.at[k, h], STP.at[k, h], s_stn.at[k], stp.at[k], (dp, nxt, lax.rem(h + j, NB)))
            remote(CO.at[fr(k), pl.ds(0, 1)], CP.at[fr(k), pl.ds(5, 1)], s_c.at[k], cp.at[k], (dp, nxt, up))
            remote(CO.at[fr(k), pl.ds(3, 1)], CP.at[fr(k), pl.ds(0, 1)], s_c.at[k], cp.at[k], (dp, nxt, dn))
            remote(CO.at[fr(k)], CP.at[fr(k), pl.ds(1, R)], s_c.at[k], cp.at[k], (dp, nxt, h))

        for j in range(1, NB):
            remote(STO.at[k, h], STO.at[k, h], s_sto.at[k], sto.at[k], (dp, s, lax.rem(h + j, NB)))
        remote(CF.at[fr(k), pl.ds(1, 1)], CF.at[fr(k), pl.ds(5, 1)], s_ch.at[k], cfh.at[k], (dp, s, up))
        remote(CF.at[fr(k), pl.ds(4, 1)], CF.at[fr(k), pl.ds(0, 1)], s_ch.at[k], cfh.at[k], (dp, s, dn))
        remote(XR.at[fr(k)], PX.at[fr(k)], s_px.at[k], px.at[k], (other, s, h))

    inv_own = [None] * SPANS
    for k in reversed(range(SPANS)):
        await_bytes(STO.at[k, pl.ds(0, NB - 1)], sto.at[k])
        await_bytes(CF.at[fr(k), pl.ds(0, 2)], cfh.at[k])
        normed, inv_own[k] = normalized(CF[F * k : F * k + F], STO, k)
        gain = GO[0:1].reshape(1, 1, 1, C)
        pre = normed * gain + GO[1:2].reshape(1, 1, 1, C)
        sig = sigmoid(pre)
        slope = sig * (1.0 + pre * (1.0 - sig))
        NO[F * k : F * k + F] = normed
        LO[F * k : F * k + F] = slope

        @pl.when(s == LAYERS - 1)
        def _():
            await_bytes(UR.at[fr(k)], ur.at[k])
            gpre = UR[F * k : F * k + F, 1:5].astype(f32) * LO[F * k : F * k + F, 1:5]
            gpre = gpre.reshape(POS, C)
            nn = NO[F * k : F * k + F, 1:5].reshape(POS, C)
            SB[k, h] = jnp.concatenate(
                [jnp.sum(gpre * nn, axis=0, keepdims=True), jnp.sum(gpre, axis=0, keepdims=True)], axis=0
            )
            for j in range(1, NB):
                remote(SB.at[k, h], SB.at[k, h], s_sbo.at[k], sb.at[k], (dp, s, lax.rem(h + j, NB)))

    for k in range(SPANS):
        await_bytes(PX.at[fr(k)], px.at[k])
        put_shifted(PS, 2 + F * k, PX[F * k : F * k + F].astype(f32))

    def weight_grad(k):
        await_bytes(GG.at[1, k], pg.at[k])

        def part(q, carry):
            ab = q + dp * (8 - 2 * q)
            a, b = lax.div(ab, 3), lax.rem(ab, 3)
            off = pl.multiple_of(ab * 768 - HALF * dp, 128)
            total = None
            for src, side in ((S, 0), (PS, 1)):
                lhs = src[pl.ds(F * k + a, F), pl.ds(b, R)].reshape(POS, 3 * C)
                d = lax.dot_general(lhs, GG[side, k], (((0,), (0,)), ((), ())), preferred_element_type=f32)
                total = d if total is None else total + d
            if k == SPANS - 1:
                WG[pl.ds(off, 768), :] = total
            else:
                WG[pl.ds(off, 768), :] += total
            return carry

        lax.fori_loop(0, 4, part, 0)
        off = pl.multiple_of((HALF - 384) * (1 - dp), 128)
        total = None
        for src, side in ((S, 0), (PS, 1)):
            full = src[F * k + 1 : F * k + 1 + F, 1 : 1 + R].reshape(POS, 3 * C)
            lhs = jnp.where(dp == 0, full[:, 0:384], full[:, 384:768])
            d = lax.dot_general(lhs, GG[side, k], (((0,), (0,)), ((), ())), preferred_element_type=f32)
            total = d if total is None else total + d
        if k == SPANS - 1:
            WG[pl.ds(off, 384), :] = total
        else:
            WG[pl.ds(off, 384), :] += total

    norm_sum = jnp.zeros((2, C), f32)
    for k in reversed(range(SPANS)):

        @pl.when(s < LAYERS - 1)
        def _():
            await_bytes(SB.at[k], sb.at[k])
            await_bytes(UR.at[fr(k)], ur.at[k])

        @pl.when(s == LAYERS - 1)
        def _():
            await_bytes(SB.at[k, pl.ds(0, NB - 1)], sb.at[k])

        sums = jnp.sum(SB[k], axis=0)
        norm_sum = norm_sum + sums
        gain = GO[0:1]
        m2 = group_sum(sums[0:1] * gain) * (1.0 / GSIZE)
        m1 = group_sum(sums[1:2] * gain) * (1.0 / GSIZE)
        upstream = UR[F * k : F * k + F].astype(f32)
        gn = upstream * LO[F * k : F * k + F] * gain.reshape(1, 1, 1, C)
        nn = NO[F * k : F * k + F]
        inv = inv_own[k]
        gc = (gn - m1.reshape(1, 1, 1, C) - nn * m2.reshape(1, 1, 1, C)) * inv.reshape(1, 1, 1, C)
        gc16 = jnp.where(valid > 0, gc, 0.0).astype(bf16)
        GG[0, k] = gc16[:, 1:5].reshape(POS, C)
        remote(GG.at[0, k], GG.at[1, k], s_pg.at[k], pg.at[k], (other, s, h))

        @pl.when(s > 0)
        def _():
            put_shifted(G, F * k, gc16.astype(f32))
            acc = None
            for ab in range(9):
                a, b = divmod(ab, 3)
                for c in range(3):
                    lhs = G[F * k + a : F * k + a + F, b : b + R, :, C * c : C * c + C].reshape(POS, C)
                    t = 9 * (2 - a) + 3 * (2 - b) + 2 - c
                    d = lax.dot_general(
                        lhs, W[t * C : t * C + C, :], (((1,), (1,)), ((), ())), preferred_element_type=f32
                    )
                    acc = d if acc is None else acc + d
            u16 = (UR[F * k : F * k + F, 1:5].astype(f32).reshape(POS, C) + acc).astype(bf16)
            UO[F * k : F * k + F] = u16.reshape(F, R, W16, C)
            remote(UO.at[fr(k), pl.ds(0, 1)], UR.at[fr(k), pl.ds(5, 1)], s_ur.at[k], ur.at[k], (dp, prv, up))
            remote(UO.at[fr(k), pl.ds(3, 1)], UR.at[fr(k), pl.ds(0, 1)], s_ur.at[k], ur.at[k], (dp, prv, dn))
            remote(UO.at[fr(k)], UR.at[fr(k), pl.ds(1, R)], s_ur.at[k], ur.at[k], (dp, prv, h))
            gpre = u16.astype(f32) * LP[k]
            SBO[k] = jnp.concatenate(
                [jnp.sum(gpre * NP[k], axis=0, keepdims=True), jnp.sum(gpre, axis=0, keepdims=True)], axis=0
            )
            for j in range(NB):
                remote(SBO.at[k], SB.at[k, h], s_sb.at[k], sb.at[k], (dp, prv, lax.rem(h + j, NB)))

        @pl.when(s == 0)
        def _():
            weight_grad(k)

    NG[0] = norm_sum
    remote(NG.at[0], NG.at[1], s_ng, ngs, (other, s, h))

    @pl.when(s > 0)
    def _():
        for k in reversed(range(SPANS)):
            weight_grad(k)

    for j in range(1, NB):
        t = lax.rem(h + j, NB)
        v = WG[pl.ds(pl.multiple_of(t * SHARE, 8), SHARE), :].reshape(27, 8, C)
        RSS[j - 1] = jnp.concatenate([v[:, :, 0:128], v[:, :, 128:256]], axis=1).astype(bf16)
        remote(RSS.at[j - 1], RSR.at[j - 1], s_rs, rr, (dp, s, t))
    await_bytes(NG.at[1], ngs)
    out_n[0] = NG[0] + NG[1]
    await_bytes(RSR, rr)
    total = None
    for j in range(NB - 1):
        v = RSR[j].astype(f32)
        total = v if total is None else total + v
    mine = WG[pl.ds(pl.multiple_of(h * SHARE, 8), SHARE), :].reshape(27, 8, C)
    out_k[0] = (mine + jnp.concatenate([total[:, 0:8], total[:, 8:16]], axis=2)).reshape(SHARE, C)

    for k in range(SPANS):
        await_bytes(XP.at[fr(k), pl.ds(0, 2)], s_xr.at[k])
        await_bytes(STO.at[k, pl.ds(0, NB - 1)], s_sto.at[k])
        await_bytes(CF.at[fr(k), pl.ds(0, 2)], s_ch.at[k])
        await_bytes(PX.at[fr(k)], s_px.at[k])
        await_bytes(GG.at[0, k], s_pg.at[k])

        @pl.when(s < LAYERS - 1)
        def _():
            await_bytes(STP.at[k], s_stn.at[k])
            await_bytes(CP.at[fr(k)], s_c.at[k])

        @pl.when((s > 0) & (s < LAYERS - 1))
        def _():
            await_bytes(CO.at[fr(k)], s_x.at[k])

        @pl.when(s > 0)
        def _():
            await_bytes(UR.at[fr(k)], s_ur.at[k])
            await_bytes(SB.at[k], s_sb.at[k])

        @pl.when(s == LAYERS - 1)
        def _():
            await_bytes(UR.at[fr(k), pl.ds(0, 2)], s_og.at[k])
            await_bytes(SB.at[k, pl.ds(0, NB - 1)], s_sbo.at[k])

    @pl.when(s < LAYERS - 1)
    def _():
        await_bytes(GO, s_gp)

    await_bytes(NG.at[0], s_ng)
    await_bytes(RSS, s_rs)


def per_device(video, kernels, gains, shifts, out_grad):
    dma = pltpu.SemaphoreType.DMA
    six = (F * SPANS, 6, W16, C)
    four = (F * SPANS, R, W16, C)
    wide = (F * SPANS + 2, 6, W16, 3 * C)
    table = (SPANS, NB, 2, C)
    scratch = [
        pltpu.VMEM((27 * C, C), bf16),
        pltpu.VMEM(six, bf16),
        pltpu.VMEM(six, bf16),
        pltpu.VMEM(six, bf16),
        pltpu.VMEM(four, bf16),
        pltpu.VMEM(six, f32),
        pltpu.VMEM(wide, bf16),
        pltpu.VMEM(six, bf16),
        pltpu.VMEM(wide, bf16),
        pltpu.VMEM(wide, bf16),
        pltpu.VMEM((2, SPANS, POS, C), bf16),
        pltpu.VMEM(six, bf16),
        pltpu.VMEM(four, bf16),
        pltpu.VMEM(table, f32),
        pltpu.VMEM(table, f32),
        pltpu.VMEM(table, f32),
        pltpu.VMEM((SPANS, 2, C), f32),
        pltpu.VMEM((2, C), f32),
        pltpu.VMEM((2, C), f32),
        pltpu.VMEM((SPANS, POS, C), f32),
        pltpu.VMEM((SPANS, POS, C), f32),
        pltpu.VMEM(six, f32),
        pltpu.VMEM(six, f32),
        pltpu.VMEM((HALF, C), f32),
        pltpu.VMEM((NB - 1, 27, 16, 128), bf16),
        pltpu.VMEM((NB - 1, 27, 16, 128), bf16),
        pltpu.VMEM((2, 2, C), f32),
    ]
    k3 = dma((SPANS,))
    sems = [dma, dma] + [k3] * 10 + [dma, dma, dma]
    sems += [k3] * 12 + [dma, dma, dma]
    anyspec = pl.BlockSpec(memory_space=pl.ANY)
    vm = pl.BlockSpec(memory_space=pltpu.VMEM)
    return pl.pallas_call(
        kernel,
        out_shape=(
            jax.ShapeDtypeStruct((1, SHARE, C), f32),
            jax.ShapeDtypeStruct((1, 2, C), f32),
        ),
        in_specs=[anyspec, anyspec, vm, vm, anyspec],
        out_specs=(vm, vm),
        scratch_shapes=scratch + sems,
        compiler_params=pltpu.CompilerParams(
            collective_id=0, has_side_effects=True, vmem_limit_bytes=60 * 2**20
        ),
    )(video, kernels, gains, shifts, out_grad)


def solution(mesh):
    return jax.shard_map(
        per_device,
        mesh=mesh,
        in_specs=(
            P("dp", None, "height", None, None),
            P("pipe", None, None),
            P("pipe", None),
            P("pipe", None),
            P("dp", None, "height", None, None),
        ),
        out_specs=(P("pipe", ("dp", "height"), None), P("pipe", None, None)),
        check_vma=False,
    )
```

```python
import functools

import jax
import jax.numpy as jnp
from jax import lax
from jax.experimental import pallas as pl
from jax.experimental.pallas import tpu as pltpu
from jax.sharding import PartitionSpec as P

GROUPS = 32
F = 4
SPANS = 3
NB = 16
LAYERS = 4
R = 4
W16 = 16
C = 256
POS = F * R * W16
GSIZE = float(POS * NB * (C // GROUPS))
HALF = 3456
SHARE = 216
EPS = 1e-05
f32 = jnp.float32
bf16 = jnp.bfloat16
MESH = pl.DeviceIdType.MESH


def group_sum(x):
    lane = lax.broadcasted_iota(jnp.int32, x.shape, 1)
    for d in (1, 2, 4):
        x = x + jnp.where((lane & d) != 0, pltpu.roll(x, d, 1), pltpu.roll(x, C - d, 1))
    return x


def combine(table):
    sums = jnp.sum(table, axis=0)
    mean_c = sums[0:1] * (1.0 / NB)
    between = jnp.sum((table - mean_c[None]) ** 2, axis=0)[0:1]
    dev_c = sums[1:2] + POS * between
    per = C // GROUPS
    mu = group_sum(mean_c) * (1.0 / per)
    var = group_sum(dev_c + (POS * NB) * (mean_c - mu) ** 2) * (1.0 / GSIZE)
    return mu, lax.rsqrt(var + EPS)


def sigmoid(v):
    return 1.0 / (1.0 + jnp.exp(-v))


def put_shifted(dst, frame, x):
    v = x.reshape(F * 6, W16, C)
    col = lax.broadcasted_iota(jnp.int32, v.shape, 1)
    left = jnp.where(col == 0, 0.0, pltpu.roll(v, 1, 1))
    right = jnp.where(col == W16 - 1, 0.0, pltpu.roll(v, W16 - 1, 1))
    dst[frame : frame + F, :, :, 0:C] = left.astype(bf16).reshape(F, 6, W16, C)
    dst[frame : frame + F, :, :, C : 2 * C] = v.astype(bf16).reshape(F, 6, W16, C)
    dst[frame : frame + F, :, :, 2 * C : 3 * C] = right.astype(bf16).reshape(F, 6, W16, C)


def kernel(
    video, kern, gains, shifts, ograd, out_k, out_n,
    W, XP, XR, XN, RL, CP, CO, CF, S, PX, PS, G, GG, UR, UO, STP, STO, SB, SBO, GO, GP, NP, LP, NO, LO,
    WG, A1S, A1R, B1S, B1R, A2S, A2R, B2S, B2R, NG,
    w_sem, xpc, xph, rl, cp, stp, sto, cfh, ur, sb, px, pg, a1, b1, a2, b2, ngs, gps,
    s_x, s_xn, s_xr, s_rl, s_c, s_ch, s_sto, s_stn, s_px, s_pg, s_ur, s_og, s_sb, s_sbo, s_a1, s_b1, s_a2, s_b2, s_ng, s_gp,
):
    dp, s, h = lax.axis_index("dp"), lax.axis_index("pipe"), lax.axis_index("height")
    nxt, prv = lax.rem(s + 1, LAYERS), lax.rem(s + LAYERS - 1, LAYERS)
    up, dn = lax.rem(h + NB - 1, NB), lax.rem(h + 1, NB)
    other = 1 - dp
    zz, yy = lax.div(h, 4), lax.rem(h, 4)
    steps = [(i, j) for i in range(4) for j in range(4)]
    steps.sort(key=lambda o: -(min(o[0], 4 - o[0]) + min(o[1], 4 - o[1])))
    bands = [lax.rem(zz + i, 4) * 4 + lax.rem(yy + j, 4) for i, j in steps]

    def remote(src, dst, ssem, rsem, dev):
        pltpu.make_async_remote_copy(
            src_ref=src, dst_ref=dst, send_sem=ssem, recv_sem=rsem, device_id=dev, device_id_type=MESH
        ).start()

    def await_bytes(ref, sem):
        pltpu.make_async_copy(ref, ref, sem).wait()

    def fr(k):
        return pl.ds(F * k, F)

    wcopy = pltpu.make_async_copy(kern.at[0], W, w_sem)
    wcopy.start()
    barrier = pltpu.get_barrier_semaphore()
    for j, b in enumerate(bands):
        pl.semaphore_signal(barrier, inc=1, device_id=(dp, nxt, b), device_id_type=MESH)
        pl.semaphore_signal(barrier, inc=1, device_id=(dp, prv, b), device_id_type=MESH)
        if j < NB - 1:
            pl.semaphore_signal(barrier, inc=1, device_id=(dp, s, b), device_id_type=MESH)
    far = lax.rem(s + 2, LAYERS)
    for b in (h, up, dn):
        pl.semaphore_signal(barrier, inc=1, device_id=(dp, far, b), device_id_type=MESH)
    pl.semaphore_signal(barrier, inc=1, device_id=(other, s, h), device_id_type=MESH)

    @pl.when(s <= 1)
    def _():
        for k in range(SPANS):
            pltpu.make_async_copy(video.at[0, fr(k)], XP.at[fr(k), pl.ds(1, R)], xpc.at[k]).start()

    @pl.when(s == LAYERS - 1)
    def _():
        for k in range(SPANS):
            pltpu.make_async_copy(ograd.at[0, fr(k)], UR.at[fr(k), pl.ds(1, R)], ur.at[k]).start()

    S[0:2] = jnp.zeros((2, 6, W16, 3 * C), bf16)
    PS[0:2] = jnp.zeros((2, 6, W16, 3 * C), bf16)
    G[12:14] = jnp.zeros((2, 6, W16, 3 * C), bf16)
    GO[0:1] = gains[...]
    GO[1:2] = shifts[...]
    pl.semaphore_wait(barrier, 3 * NB + 3)

    @pl.when(s <= 1)
    def _():
        for k in range(SPANS):
            remote(video.at[0, fr(k), pl.ds(0, 1)], XP.at[fr(k), pl.ds(5, 1)], s_xr.at[k], xph.at[k], (dp, s, up))
            remote(video.at[0, fr(k), pl.ds(3, 1)], XP.at[fr(k), pl.ds(0, 1)], s_xr.at[k], xph.at[k], (dp, s, dn))

    @pl.when(s == LAYERS - 1)
    def _():
        for k in reversed(range(SPANS)):
            remote(ograd.at[0, fr(k), pl.ds(0, 1)], UR.at[fr(k), pl.ds(5, 1)], s_og.at[k], ur.at[k], (dp, s, up))
            remote(ograd.at[0, fr(k), pl.ds(3, 1)], UR.at[fr(k), pl.ds(0, 1)], s_og.at[k], ur.at[k], (dp, s, dn))

    @pl.when(s < LAYERS - 1)
    def _():
        remote(GO, GP, s_gp, gps, (dp, nxt, h))

    @pl.when(s > 0)
    def _():
        await_bytes(GP, gps)

    row = lax.broadcasted_iota(jnp.int32, (1, 6, 1, 1), 1)
    valid = jnp.where(row == 0, (h > 0).astype(f32), jnp.where(row == 5, (h < NB - 1).astype(f32), 1.0))

    def normalized(conv, table_ref, k):
        mu, inv = combine(table_ref[k])
        own = (table_ref[k, h][0:1] - mu).reshape(1, 1, 1, C)
        above = (table_ref[k, up][0:1] - mu).reshape(1, 1, 1, C)
        below = (table_ref[k, dn][0:1] - mu).reshape(1, 1, 1, C)
        off = jnp.concatenate([above, own, own, own, own, below], axis=1)
        return (conv + off) * inv.reshape(1, 1, 1, C)

    gain4 = GO[0:1].reshape(1, 1, 1, C)
    shift4 = GO[1:2].reshape(1, 1, 1, C)
    own = [None] * SPANS

    def layer(k):
        await_bytes(XP.at[fr(k), pl.ds(1, R)], xpc.at[k])

        await_bytes(XP.at[fr(k), pl.ds(0, 2)], xph.at[k])

        @pl.when(s == 0)
        def _():
            x = XP[F * k : F * k + F].astype(f32) * valid
            XR[F * k : F * k + F] = x.astype(bf16)
            put_shifted(S, 2 + F * k, x)

        @pl.when(s > 0)
        def _():
            await_bytes(STP.at[k], stp.at[k])
            await_bytes(CP.at[fr(k)], cp.at[k])
            normed = normalized(CP[F * k : F * k + F].astype(f32), STP, k)
            pre = normed * GP[0:1].reshape(1, 1, 1, C) + GP[1:2].reshape(1, 1, 1, C)
            sig = sigmoid(pre)
            x = XP[F * k : F * k + F].astype(f32) + pre * sig
            x16 = (x * valid).astype(bf16)
            XR[F * k : F * k + F] = x16
            put_shifted(S, 2 + F * k, x16.astype(f32))
            NP[k] = normed[:, 1:5].reshape(POS, C)
            LP[k] = (sig * (1.0 + pre * (1.0 - sig)))[:, 1:5].reshape(POS, C)

        if k == 0:
            wcopy.wait()
        acc = None
        for ab in range(9):
            a, b = divmod(ab, 3)
            lhs = S[F * k + a : F * k + a + F, b : b + R].reshape(POS, 3 * C)
            d = jnp.dot(lhs, W[ab * 768 : ab * 768 + 768, :], preferred_element_type=f32)
            acc = d if acc is None else acc + d
        mean = jnp.sum(acc, axis=0, keepdims=True) * (1.0 / POS)
        cen = acc - mean
        STO[k, h] = jnp.concatenate([mean, jnp.sum(cen * cen, axis=0, keepdims=True)], axis=0)
        CF[F * k : F * k + F, 1:5] = cen.reshape(F, R, W16, C)
        CO[F * k : F * k + F] = cen.astype(bf16).reshape(F, R, W16, C)

        @pl.when(s < LAYERS - 1)
        def _():
            for b in bands:
                remote(STO.at[k, h], STP.at[k, h], s_stn.at[k], stp.at[k], (dp, nxt, b))

        for b in bands[:-1]:
            remote(STO.at[k, h], STO.at[k, h], s_sto.at[k], sto.at[k], (dp, s, b))

        @pl.when(s < LAYERS - 1)
        def _():
            remote(CO.at[fr(k), pl.ds(0, 1)], CP.at[fr(k), pl.ds(5, 1)], s_c.at[k], cp.at[k], (dp, nxt, up))
            remote(CO.at[fr(k), pl.ds(3, 1)], CP.at[fr(k), pl.ds(0, 1)], s_c.at[k], cp.at[k], (dp, nxt, dn))
            remote(CO.at[fr(k)], CP.at[fr(k), pl.ds(1, R)], s_c.at[k], cp.at[k], (dp, nxt, h))

        remote(CF.at[fr(k), pl.ds(1, 1)], CF.at[fr(k), pl.ds(5, 1)], s_ch.at[k], cfh.at[k], (dp, s, up))
        remote(CF.at[fr(k), pl.ds(4, 1)], CF.at[fr(k), pl.ds(0, 1)], s_ch.at[k], cfh.at[k], (dp, s, dn))
        remote(XR.at[fr(k)], PX.at[fr(k)], s_px.at[k], px.at[k], (other, s, h))

    def own_rows(k):
        await_bytes(STO.at[k, pl.ds(0, NB - 1)], sto.at[k])
        mu, inv = combine(STO[k])
        own[k] = (mu, inv)
        off = (STO[k, h][0:1] - mu).reshape(1, 1, 1, C)
        normed = (CF[F * k : F * k + F, 1:5] + off) * inv.reshape(1, 1, 1, C)
        pre = normed * gain4 + shift4
        sig = sigmoid(pre)
        slope = sig * (1.0 + pre * (1.0 - sig))
        NO[F * k : F * k + F, 1:5] = normed
        LO[F * k : F * k + F, 1:5] = slope

        @pl.when(s <= 1)
        def _():
            XN[F * k : F * k + F] = (XR[F * k : F * k + F, 1:5].astype(f32) + pre * sig).astype(bf16)

        @pl.when(s == 0)
        def _():
            remote(XN.at[fr(k)], RL.at[fr(k)], s_x.at[k], rl.at[k], (dp, prv, h))

        @pl.when(s == 1)
        def _():
            far = lax.rem(s + 2, LAYERS)
            remote(XN.at[fr(k), pl.ds(0, 1)], XP.at[fr(k), pl.ds(5, 1)], s_xn.at[k], xph.at[k], (dp, far, up))
            remote(XN.at[fr(k), pl.ds(3, 1)], XP.at[fr(k), pl.ds(0, 1)], s_xn.at[k], xph.at[k], (dp, far, dn))
            remote(XN.at[fr(k)], XP.at[fr(k), pl.ds(1, R)], s_x.at[k], xpc.at[k], (dp, far, h))

        @pl.when(s == LAYERS - 1)
        def _():
            await_bytes(UR.at[fr(k)], ur.at[k])
            gpre = (UR[F * k : F * k + F, 1:5].astype(f32) * slope).reshape(POS, C)
            nn = normed.reshape(POS, C)
            SB[k, h] = jnp.concatenate(
                [jnp.sum(gpre * nn, axis=0, keepdims=True), jnp.sum(gpre, axis=0, keepdims=True)], axis=0
            )
            for b in bands[:-1]:
                remote(SB.at[k, h], SB.at[k, h], s_sbo.at[k], sb.at[k], (dp, s, b))

    def own_halo(k):
        await_bytes(CF.at[fr(k), pl.ds(0, 2)], cfh.at[k])
        mu, inv = own[k]
        for r, b in ((0, up), (5, dn)):
            off = (STO[k, b][0:1] - mu).reshape(1, 1, 1, C)
            normed = (CF[F * k : F * k + F, r : r + 1] + off) * inv.reshape(1, 1, 1, C)
            pre = normed * gain4 + shift4
            sig = sigmoid(pre)
            NO[F * k : F * k + F, r : r + 1] = normed
            LO[F * k : F * k + F, r : r + 1] = sig * (1.0 + pre * (1.0 - sig))

    @pl.when(s == LAYERS - 1)
    def _():
        for k in range(SPANS):
            await_bytes(RL.at[fr(k)], rl.at[k])
            remote(RL.at[fr(k), pl.ds(0, 1)], XP.at[fr(k), pl.ds(5, 1)], s_rl.at[k], xph.at[k], (dp, prv, up))
            remote(RL.at[fr(k), pl.ds(3, 1)], XP.at[fr(k), pl.ds(0, 1)], s_rl.at[k], xph.at[k], (dp, prv, dn))
            remote(RL.at[fr(k)], XP.at[fr(k), pl.ds(1, R)], s_rl.at[k], xpc.at[k], (dp, prv, h))

    layer(0)
    layer(1)
    own_rows(0)
    layer(2)
    own_rows(1)
    own_rows(2)
    for k in reversed(range(SPANS)):
        own_halo(k)

    for k in range(SPANS):
        await_bytes(PX.at[fr(k)], px.at[k])
        put_shifted(PS, 2 + F * k, PX[F * k : F * k + F].astype(f32))

    sides = ((S, 0), (PS, 1))

    def add_rows(off, rows, lhs, side, k, first):
        d = lax.dot_general(lhs, GG[side, k], (((0,), (0,)), ((), ())), preferred_element_type=f32)
        if first:
            WG[pl.ds(off, rows), :] = d
        else:
            WG[pl.ds(off, rows), :] += d

    def part(q, side, k, first):
        ab = q + dp * (8 - 2 * q)
        a, b = lax.div(ab, 3), lax.rem(ab, 3)
        off = pl.multiple_of(ab * 768 - HALF * dp, 128)
        lhs = sides[side][0][pl.ds(F * k + a, F), pl.ds(b, R)].reshape(POS, 3 * C)
        add_rows(off, 768, lhs, side, k, first)

    def middle(side, k, first):
        off = pl.multiple_of((HALF - 384) * (1 - dp), 128)
        full = sides[side][0][F * k + 1 : F * k + 1 + F, 1 : 1 + R].reshape(POS, 3 * C)
        lhs = jnp.where(dp == 0, full[:, 0:384], full[:, 384:768])
        add_rows(off, 384, lhs, side, k, first)

    def weight_grad_now(side, k, first=False):
        for q in range(4):
            part(q, side, k, first)
        middle(side, k, first)

    def weight_grad(side, k, first=False):
        def body(q, carry):
            part(q, side, k, first)
            return carry

        lax.fori_loop(0, 4, body, 0)
        middle(side, k, first)

    TA, TB = 14, 13

    def tiles(row, n):
        v = WG[pl.ds(pl.multiple_of(row, 8), 8 * n), :].reshape(n, 8, C)
        return jnp.concatenate([v[:, :, 0:128], v[:, :, 128:256]], axis=1)

    def rows(t):
        return jnp.concatenate([t[:, 0:8], t[:, 8:16]], axis=2).reshape(8 * t.shape[0], C)

    def first_phase(m):
        z = m + dp * (3 - 2 * m)
        for y in range(4):
            row = (4 * z + y) * SHARE
            A1S[z, y] = tiles(row, TA).astype(bf16)
            B1S[y, z] = tiles(row + 8 * TA, TB).astype(bf16)
        dz = lax.rem(z - zz + 4, 4)

        @pl.when(dz != 0)
        def _():
            remote(A1S.at[z], A1R.at[dz - 1], s_a1, a1, (dp, s, 4 * z + yy))

        for dy in range(1, 4):
            y = lax.rem(yy + dy, 4)
            remote(B1S.at[y, z], B1R.at[dy - 1, z], s_b1, b1, (dp, s, 4 * zz + y))

    norm_sum = jnp.zeros((2, C), f32)
    for k in reversed(range(SPANS)):

        @pl.when(s < LAYERS - 1)
        def _():
            await_bytes(SB.at[k], sb.at[k])
            await_bytes(UR.at[fr(k)], ur.at[k])

        @pl.when(s == LAYERS - 1)
        def _():
            await_bytes(SB.at[k, pl.ds(0, NB - 1)], sb.at[k])

        sums = jnp.sum(SB[k], axis=0)
        norm_sum = norm_sum + sums
        gain = GO[0:1]
        m2 = group_sum(sums[0:1] * gain) * (1.0 / GSIZE)
        m1 = group_sum(sums[1:2] * gain) * (1.0 / GSIZE)
        upstream = UR[F * k : F * k + F].astype(f32)
        gn = upstream * LO[F * k : F * k + F] * gain.reshape(1, 1, 1, C)
        nn = NO[F * k : F * k + F]
        inv = own[k][1]
        gc = (gn - m1.reshape(1, 1, 1, C) - nn * m2.reshape(1, 1, 1, C)) * inv.reshape(1, 1, 1, C)
        gc16 = jnp.where(valid > 0, gc, 0.0).astype(bf16)
        GG[0, k] = gc16[:, 1:5].reshape(POS, C)
        remote(GG.at[0, k], GG.at[1, k], s_pg.at[k], pg.at[k], (other, s, h))

        @pl.when(s > 0)
        def _():
            put_shifted(G, F * k, gc16.astype(f32))
            acc = None
            for ab in range(9):
                a, b = divmod(ab, 3)
                for c in range(3):
                    lhs = G[F * k + a : F * k + a + F, b : b + R, :, C * c : C * c + C].reshape(POS, C)
                    t = 9 * (2 - a) + 3 * (2 - b) + 2 - c
                    d = lax.dot_general(
                        lhs, W[t * C : t * C + C, :], (((1,), (1,)), ((), ())), preferred_element_type=f32
                    )
                    acc = d if acc is None else acc + d
            u16 = (UR[F * k : F * k + F, 1:5].astype(f32).reshape(POS, C) + acc).astype(bf16)
            UO[F * k : F * k + F] = u16.reshape(F, R, W16, C)
            gpre = u16.astype(f32) * LP[k]
            SBO[k] = jnp.concatenate(
                [jnp.sum(gpre * NP[k], axis=0, keepdims=True), jnp.sum(gpre, axis=0, keepdims=True)], axis=0
            )
            for b in bands:
                remote(SBO.at[k], SB.at[k, h], s_sb.at[k], sb.at[k], (dp, prv, b))
            remote(UO.at[fr(k), pl.ds(0, 1)], UR.at[fr(k), pl.ds(5, 1)], s_ur.at[k], ur.at[k], (dp, prv, up))
            remote(UO.at[fr(k), pl.ds(3, 1)], UR.at[fr(k), pl.ds(0, 1)], s_ur.at[k], ur.at[k], (dp, prv, dn))
            remote(UO.at[fr(k)], UR.at[fr(k), pl.ds(1, R)], s_ur.at[k], ur.at[k], (dp, prv, h))

        @pl.when(s == 0)
        def _():
            weight_grad_now(0, k, k == SPANS - 1)
            if k < SPANS - 1:
                await_bytes(GG.at[1, k + 1], pg.at[k + 1])
                weight_grad_now(1, k + 1)

    NG[0] = norm_sum
    remote(NG.at[0], NG.at[1], s_ng, ngs, (other, s, h))

    @pl.when(s > 0)
    def _():
        for k in reversed(range(SPANS)):
            weight_grad(0, k, k == SPANS - 1)
        for k in (2, 1):
            await_bytes(GG.at[1, k], pg.at[k])
            weight_grad(1, k)

    await_bytes(GG.at[1, 0], pg.at[0])
    for q in range(4):
        part(q, 1, 0, False)
        if q > 0:
            first_phase(q - 1)
    middle(1, 0, False)
    first_phase(3)

    await_bytes(NG.at[1], ngs)
    out_n[0] = NG[0] + NG[1]

    def total(r, *at):
        return sum(r[(j, *at)].astype(f32) for j in range(3))

    await_bytes(A1R, a1)
    for dy in range(1, 4):
        y = lax.rem(yy + dy, 4)
        A2S[dy - 1] = (tiles((4 * zz + y) * SHARE, TA) + total(A1R, y)).astype(bf16)
        remote(A2S.at[dy - 1], A2R.at[dy - 1], s_a2, a2, (dp, s, 4 * zz + y))
    await_bytes(B1R, b1)
    for dz in range(1, 4):
        z = lax.rem(zz + dz, 4)
        B2S[dz - 1] = (tiles((4 * z + yy) * SHARE + 8 * TA, TB) + total(B1R, z)).astype(bf16)
        remote(B2S.at[dz - 1], B2R.at[dz - 1], s_b2, b2, (dp, s, 4 * z + yy))
    mine_a = tiles(h * SHARE, TA) + total(A1R, yy)
    mine_b = tiles(h * SHARE + 8 * TA, TB) + total(B1R, zz)
    await_bytes(A2R, a2)
    out_k[0, 0 : 8 * TA] = rows(mine_a + total(A2R))
    await_bytes(B2R, b2)
    out_k[0, 8 * TA : SHARE] = rows(mine_b + total(B2R))

    for k in range(SPANS):
        await_bytes(STO.at[k, pl.ds(0, NB - 1)], s_sto.at[k])
        await_bytes(CF.at[fr(k), pl.ds(0, 2)], s_ch.at[k])
        await_bytes(PX.at[fr(k)], s_px.at[k])
        await_bytes(GG.at[0, k], s_pg.at[k])

        @pl.when(s < LAYERS - 1)
        def _():
            await_bytes(STP.at[k], s_stn.at[k])
            await_bytes(CP.at[fr(k)], s_c.at[k])

        @pl.when(s <= 1)
        def _():
            await_bytes(XN.at[fr(k)], s_x.at[k])

            await_bytes(XP.at[fr(k), pl.ds(0, 2)], s_xr.at[k])

        @pl.when(s == 1)
        def _():
            await_bytes(XP.at[fr(k), pl.ds(0, 2)], s_xn.at[k])

        @pl.when(s > 0)
        def _():
            await_bytes(UR.at[fr(k)], s_ur.at[k])
            await_bytes(SB.at[k], s_sb.at[k])

        @pl.when(s == LAYERS - 1)
        def _():
            await_bytes(XP.at[fr(k)], s_rl.at[k])
            await_bytes(UR.at[fr(k), pl.ds(0, 2)], s_og.at[k])
            await_bytes(SB.at[k, pl.ds(0, NB - 1)], s_sbo.at[k])

    @pl.when(s < LAYERS - 1)
    def _():
        await_bytes(GO, s_gp)

    await_bytes(NG.at[0], s_ng)
    await_bytes(A1R, s_a1)
    await_bytes(B1R, s_b1)
    await_bytes(A2R, s_a2)
    await_bytes(B2R, s_b2)


def per_device(video, kernels, gains, shifts, out_grad):
    dma = pltpu.SemaphoreType.DMA
    six = (F * SPANS, 6, W16, C)
    four = (F * SPANS, R, W16, C)
    wide = (F * SPANS + 2, 6, W16, 3 * C)
    table = (SPANS, NB, 2, C)
    scratch = [
        pltpu.VMEM((27 * C, C), bf16),
        pltpu.VMEM(six, bf16),
        pltpu.VMEM(six, bf16),
        pltpu.VMEM(four, bf16),
        pltpu.VMEM(four, bf16),
        pltpu.VMEM(six, bf16),
        pltpu.VMEM(four, bf16),
        pltpu.VMEM(six, f32),
        pltpu.VMEM(wide, bf16),
        pltpu.VMEM(six, bf16),
        pltpu.VMEM(wide, bf16),
        pltpu.VMEM(wide, bf16),
        pltpu.VMEM((2, SPANS, POS, C), bf16),
        pltpu.VMEM(six, bf16),
        pltpu.VMEM(four, bf16),
        pltpu.VMEM(table, f32),
        pltpu.VMEM(table, f32),
        pltpu.VMEM(table, f32),
        pltpu.VMEM((SPANS, 2, C), f32),
        pltpu.VMEM((2, C), f32),
        pltpu.VMEM((2, C), f32),
        pltpu.VMEM((SPANS, POS, C), f32),
        pltpu.VMEM((SPANS, POS, C), f32),
        pltpu.VMEM(six, f32),
        pltpu.VMEM(six, f32),
        pltpu.VMEM((HALF, C), f32),
        pltpu.VMEM((4, 4, 14, 16, 128), bf16),
        pltpu.VMEM((3, 4, 14, 16, 128), bf16),
        pltpu.VMEM((4, 4, 13, 16, 128), bf16),
        pltpu.VMEM((3, 4, 13, 16, 128), bf16),
        pltpu.VMEM((3, 14, 16, 128), bf16),
        pltpu.VMEM((3, 14, 16, 128), bf16),
        pltpu.VMEM((3, 13, 16, 128), bf16),
        pltpu.VMEM((3, 13, 16, 128), bf16),
        pltpu.VMEM((2, 2, C), f32),
    ]
    k3 = dma((SPANS,))
    sems = [dma] + [k3] * 11 + [dma] * 6
    sems += [k3] * 14 + [dma] * 6
    anyspec = pl.BlockSpec(memory_space=pl.ANY)
    vm = pl.BlockSpec(memory_space=pltpu.VMEM)
    return pl.pallas_call(
        kernel,
        out_shape=(
            jax.ShapeDtypeStruct((1, SHARE, C), f32),
            jax.ShapeDtypeStruct((1, 2, C), f32),
        ),
        in_specs=[anyspec, anyspec, vm, vm, anyspec],
        out_specs=(vm, vm),
        scratch_shapes=scratch + sems,
        compiler_params=pltpu.CompilerParams(
            collective_id=0, has_side_effects=True, vmem_limit_bytes=60 * 2**20
        ),
    )(video, kernels, gains, shifts, out_grad)


def solution(mesh):
    return jax.shard_map(
        per_device,
        mesh=mesh,
        in_specs=(
            P("dp", None, "height", None, None),
            P("pipe", None, None),
            P("pipe", None),
            P("pipe", None),
            P("dp", None, "height", None, None),
        ),
        out_specs=(P("pipe", ("dp", "height"), None), P("pipe", None, None)),
        check_vma=False,
    )
```

```python
import functools

import jax
import jax.numpy as jnp
from jax import lax
from jax.experimental import pallas as pl
from jax.experimental.pallas import tpu as pltpu
from jax.sharding import PartitionSpec as P

GROUPS = 32
F = 4
SPANS = 3
NB = 16
LAYERS = 4
R = 4
W16 = 16
C = 256
POS = F * R * W16
GSIZE = float(POS * NB * (C // GROUPS))
HALF = 3456
SHARE = 216
EPS = 1e-05
f32 = jnp.float32
bf16 = jnp.bfloat16
MESH = pl.DeviceIdType.MESH


def group_sum(x):
    lane = lax.broadcasted_iota(jnp.int32, x.shape, 1)
    for d in (1, 2, 4):
        x = x + jnp.where((lane & d) != 0, pltpu.roll(x, d, 1), pltpu.roll(x, C - d, 1))
    return x


def combine(table):
    sums = jnp.sum(table, axis=0)
    mean_c = sums[0:1] * (1.0 / NB)
    between = jnp.sum((table - mean_c[None]) ** 2, axis=0)[0:1]
    dev_c = sums[1:2] + POS * between
    per = C // GROUPS
    mu = group_sum(mean_c) * (1.0 / per)
    var = group_sum(dev_c + (POS * NB) * (mean_c - mu) ** 2) * (1.0 / GSIZE)
    return mu, lax.rsqrt(var + EPS)


def sigmoid(v):
    return 1.0 / (1.0 + jnp.exp(-v))


def put_shifted(dst, frame, x):
    v = x.reshape(F * 6, W16, C)
    col = lax.broadcasted_iota(jnp.int32, v.shape, 1)
    left = jnp.where(col == 0, 0.0, pltpu.roll(v, 1, 1))
    right = jnp.where(col == W16 - 1, 0.0, pltpu.roll(v, W16 - 1, 1))
    dst[pl.ds(frame, F), :, :, 0:C] = left.astype(bf16).reshape(F, 6, W16, C)
    dst[pl.ds(frame, F), :, :, C : 2 * C] = v.astype(bf16).reshape(F, 6, W16, C)
    dst[pl.ds(frame, F), :, :, 2 * C : 3 * C] = right.astype(bf16).reshape(F, 6, W16, C)


def kernel(
    video, kern, gains, shifts, ograd, out_k, out_n,
    W, XP, XR, XN, RL, CP, CO, CF, SS, PX, G, GG, UR, UO, STP, STO, SB, SBO, GO, GP, NP, LP, NO, LO, MI,
    WG, A1S, A1R, B1S, B1R, A2S, A2R, B2S, B2R, NG,
    ready, w_sem, xpc, xph, rl, cp, stp, sto, cfh, ur, sb, px, pg, a1, b1, a2, b2, ngs, gps,
    s_x, s_xn, s_xr, s_rl, s_c, s_ch, s_sto, s_stn, s_px, s_pg, s_ur, s_og, s_sb, s_sbo, s_a1, s_b1, s_a2, s_b2, s_ng, s_gp,
):
    dp, s, h = lax.axis_index("dp"), lax.axis_index("pipe"), lax.axis_index("height")
    nxt, prv = lax.rem(s + 1, LAYERS), lax.rem(s + LAYERS - 1, LAYERS)
    up, dn = lax.rem(h + NB - 1, NB), lax.rem(h + 1, NB)
    other = 1 - dp
    zz, yy = lax.div(h, 4), lax.rem(h, 4)
    steps = [(i, j) for i in range(4) for j in range(4)]
    steps.sort(key=lambda o: -(min(o[0], 4 - o[0]) + min(o[1], 4 - o[1])))
    bands = [lax.rem(zz + i, 4) * 4 + lax.rem(yy + j, 4) for i, j in steps]

    def remote(src, dst, ssem, rsem, dev):
        pltpu.make_async_remote_copy(
            src_ref=src, dst_ref=dst, send_sem=ssem, recv_sem=rsem, device_id=dev, device_id_type=MESH
        ).start()

    def await_bytes(ref, sem):
        pltpu.make_async_copy(ref, ref, sem).wait()

    inside = (h > 0) & (h < NB - 1)

    def await_edges(ref, k, sem, rows=0):
        @pl.when(inside)
        def _():
            await_bytes(ref.at[fr(k), pl.ds(0, rows + 2)], sem)

        @pl.when(jnp.logical_not(inside))
        def _():
            await_bytes(ref.at[fr(k), pl.ds(0, rows + 1)], sem)

    def send_edges(src, first, last, dst, k, ssem, rsem, layer):
        @pl.when(h > 0)
        def _():
            remote(src.at[fr(k), pl.ds(first, 1)], dst.at[fr(k), pl.ds(5, 1)], ssem, rsem, (dp, layer, up))

        @pl.when(h < NB - 1)
        def _():
            remote(src.at[fr(k), pl.ds(last, 1)], dst.at[fr(k), pl.ds(0, 1)], ssem, rsem, (dp, layer, dn))

    def fr(k, first=0):
        return pl.ds(F * k + first, F)

    wcopy = pltpu.make_async_copy(kern.at[0], W, w_sem)
    wcopy.start()
    barrier = pltpu.get_barrier_semaphore()
    for j, b in enumerate(bands):
        if j < NB - 1:
            pl.semaphore_signal(barrier, inc=1, device_id=(dp, s, b), device_id_type=MESH)
    far = lax.rem(s + 2, LAYERS)
    for b in (h, up, dn):
        pl.semaphore_signal(barrier, inc=1, device_id=(dp, far, b), device_id_type=MESH)
    for p in (nxt, prv):
        pl.semaphore_signal(barrier, inc=1, device_id=(dp, p, h), device_id_type=MESH)
    pl.semaphore_signal(barrier, inc=1, device_id=(other, s, h), device_id_type=MESH)

    @pl.when(s <= 1)
    def _():
        for k in range(SPANS):
            pltpu.make_async_copy(video.at[0, fr(k)], XP.at[fr(k), pl.ds(1, R)], xpc.at[k]).start()

    @pl.when(s == LAYERS - 1)
    def _():
        for k in range(SPANS):
            pltpu.make_async_copy(ograd.at[0, fr(k)], UR.at[fr(k), pl.ds(1, R)], ur.at[k]).start()

    SS[:, 0:2] = jnp.zeros((2, 2, 6, W16, 3 * C), bf16)
    G[12:14] = jnp.zeros((2, 6, W16, 3 * C), bf16)
    GO[0:1] = gains[...]
    GO[1:2] = shifts[...]
    pl.semaphore_wait(barrier, NB - 1 + 3 + 2 + 1)
    for p in (nxt, prv):
        pl.semaphore_signal(ready, inc=1, device_id=(dp, p, h), device_id_type=MESH)

    @pl.when(s <= 1)
    def _():
        for k in range(SPANS):
            send_edges(video.at[0], 0, 3, XP, k, s_xr.at[k], xph.at[k], s)

    @pl.when(s == LAYERS - 1)
    def _():
        for k in reversed(range(SPANS)):
            send_edges(ograd.at[0], 0, 3, UR, k, s_og.at[k], ur.at[k], s)

    pl.semaphore_wait(ready, 2)

    @pl.when(s < LAYERS - 1)
    def _():
        remote(GO, GP, s_gp, gps, (dp, nxt, h))

    @pl.when(s > 0)
    def _():
        await_bytes(GP, gps)

    row = lax.broadcasted_iota(jnp.int32, (1, 6, 1, 1), 1)
    valid = jnp.where(row == 0, (h > 0).astype(f32), jnp.where(row == 5, (h < NB - 1).astype(f32), 1.0))

    def normalized(conv, table_ref, k):
        mu, inv = combine(table_ref[k])
        own = (table_ref[k, h][0:1] - mu).reshape(1, 1, 1, C)
        above = (table_ref[k, up][0:1] - mu).reshape(1, 1, 1, C)
        below = (table_ref[k, dn][0:1] - mu).reshape(1, 1, 1, C)
        off = jnp.concatenate([above, own, own, own, own, below], axis=1)
        return (conv + off) * inv.reshape(1, 1, 1, C)

    gain4 = GO[0:1].reshape(1, 1, 1, C)
    shift4 = GO[1:2].reshape(1, 1, 1, C)

    def layer(k):
        await_bytes(XP.at[fr(k), pl.ds(1, R)], xpc.at[k])

        await_edges(XP, k, xph.at[k])

        @pl.when(s == 0)
        def _():
            x = jnp.where(valid > 0, XP[fr(k)].astype(f32), 0.0)
            XR[fr(k)] = x.astype(bf16)
            put_shifted(SS.at[0], 2 + F * k, x)

        @pl.when(s > 0)
        def _():
            await_bytes(STP.at[k], stp.at[k])
            await_edges(CP, k, cp.at[k], R)
            normed = normalized(CP[fr(k)].astype(f32), STP, k)
            pre = normed * GP[0:1].reshape(1, 1, 1, C) + GP[1:2].reshape(1, 1, 1, C)
            sig = sigmoid(pre)
            x = XP[fr(k)].astype(f32) + pre * sig
            x16 = jnp.where(valid > 0, x, 0.0).astype(bf16)
            XR[fr(k)] = x16
            put_shifted(SS.at[0], 2 + F * k, x16.astype(f32))
            NP[k] = normed[:, 1:5].reshape(POS, C)
            LP[k] = (sig * (1.0 + pre * (1.0 - sig)))[:, 1:5].reshape(POS, C)

        @pl.when(k == 0)
        def _():
            wcopy.wait()

        acc = None
        for ab in range(9):
            a, b = divmod(ab, 3)
            lhs = SS[0, fr(k, a), b : b + R].reshape(POS, 3 * C)
            d = jnp.dot(lhs, W[ab * 768 : ab * 768 + 768, :], preferred_element_type=f32)
            acc = d if acc is None else acc + d
        mean = jnp.sum(acc, axis=0, keepdims=True) * (1.0 / POS)
        cen = acc - mean
        STO[k, h] = jnp.concatenate([mean, jnp.sum(cen * cen, axis=0, keepdims=True)], axis=0)
        CF[fr(k), 1:5] = cen.reshape(F, R, W16, C)
        CO[fr(k)] = cen.astype(bf16).reshape(F, R, W16, C)

        @pl.when(s < LAYERS - 1)
        def _():
            for b in bands:
                remote(STO.at[k, h], STP.at[k, h], s_stn.at[k], stp.at[k], (dp, nxt, b))

        for b in bands[:-1]:
            remote(STO.at[k, h], STO.at[k, h], s_sto.at[k], sto.at[k], (dp, s, b))

        @pl.when(s < LAYERS - 1)
        def _():
            send_edges(CO, 0, 3, CP, k, s_c.at[k], cp.at[k], nxt)
            remote(CO.at[fr(k)], CP.at[fr(k), pl.ds(1, R)], s_c.at[k], cp.at[k], (dp, nxt, h))

        send_edges(CF, 1, 4, CF, k, s_ch.at[k], cfh.at[k], s)
        remote(XR.at[fr(k)], PX.at[fr(k)], s_px.at[k], px.at[k], (other, s, h))

    def own_rows(k):
        await_bytes(STO.at[k, pl.ds(0, NB - 1)], sto.at[k])
        mu, inv = combine(STO[k])
        MI[k] = jnp.concatenate([mu, inv], axis=0)
        off = (STO[k, h][0:1] - mu).reshape(1, 1, 1, C)
        normed = (CF[fr(k), 1:5] + off) * inv.reshape(1, 1, 1, C)
        pre = normed * gain4 + shift4
        sig = sigmoid(pre)
        slope = sig * (1.0 + pre * (1.0 - sig))
        NO[fr(k), 1:5] = normed
        LO[fr(k), 1:5] = slope

        @pl.when(s <= 1)
        def _():
            XN[fr(k)] = (XR[fr(k), 1:5].astype(f32) + pre * sig).astype(bf16)

        @pl.when(s == 0)
        def _():
            remote(XN.at[fr(k)], RL.at[fr(k)], s_x.at[k], rl.at[k], (dp, prv, h))

        @pl.when(s == 1)
        def _():
            far = lax.rem(s + 2, LAYERS)
            send_edges(XN, 0, 3, XP, k, s_xn.at[k], xph.at[k], far)
            remote(XN.at[fr(k)], XP.at[fr(k), pl.ds(1, R)], s_x.at[k], xpc.at[k], (dp, far, h))

        @pl.when(s == LAYERS - 1)
        def _():
            await_edges(UR, k, ur.at[k], R)
            gpre = (UR[fr(k), 1:5].astype(f32) * slope).reshape(POS, C)
            nn = normed.reshape(POS, C)
            SB[k, h] = jnp.concatenate(
                [jnp.sum(gpre * nn, axis=0, keepdims=True), jnp.sum(gpre, axis=0, keepdims=True)], axis=0
            )
            for b in bands[:-1]:
                remote(SB.at[k, h], SB.at[k, h], s_sbo.at[k], sb.at[k], (dp, s, b))

    def own_halo(k):
        await_edges(CF, k, cfh.at[k])
        mu, inv = MI[k, 0:1], MI[k, 1:2]
        for r, b in ((0, up), (5, dn)):
            off = (STO[k, b][0:1] - mu).reshape(1, 1, 1, C)
            normed = (CF[fr(k), r : r + 1] + off) * inv.reshape(1, 1, 1, C)
            pre = normed * gain4 + shift4
            sig = sigmoid(pre)
            NO[fr(k), r : r + 1] = normed
            LO[fr(k), r : r + 1] = sig * (1.0 + pre * (1.0 - sig))

    @pl.when(s == LAYERS - 1)
    def _():
        for k in range(SPANS):
            await_bytes(RL.at[fr(k)], rl.at[k])
            send_edges(RL, 0, 3, XP, k, s_rl.at[k], xph.at[k], prv)
            remote(RL.at[fr(k)], XP.at[fr(k), pl.ds(1, R)], s_rl.at[k], xpc.at[k], (dp, prv, h))

    lag = jnp.where(s == 0, SPANS, 1)

    def forward(i, carry):
        @pl.when(i < SPANS)
        def _():
            layer(i)

        @pl.when((i >= lag) & (i < SPANS + lag))
        def _():
            own_rows(i - lag)

        return carry

    lax.fori_loop(0, SPANS + lag, forward, 0)

    def halo(i, carry):
        own_halo(SPANS - 1 - i)
        return carry

    lax.fori_loop(0, SPANS, halo, 0)

    def partner(k, carry):
        await_bytes(PX.at[fr(k)], px.at[k])
        put_shifted(SS.at[1], 2 + F * k, PX[fr(k)].astype(f32))
        return carry

    lax.fori_loop(0, SPANS, partner, 0)
    WG[...] = jnp.zeros((HALF, C), f32)

    def add_rows(off, rows, lhs, side, k):
        WG[pl.ds(off, rows), :] += lax.dot_general(
            lhs, GG[side, k], (((0,), (0,)), ((), ())), preferred_element_type=f32
        )

    def part(q, side, k):
        ab = q + dp * (8 - 2 * q)
        a, b = lax.div(ab, 3), lax.rem(ab, 3)
        off = pl.multiple_of(ab * 768 - HALF * dp, 128)
        add_rows(off, 768, SS[side, fr(k, a), pl.ds(b, R)].reshape(POS, 3 * C), side, k)

    def middle(side, k):
        off = pl.multiple_of((HALF - 384) * (1 - dp), 128)
        full = SS[side, fr(k, 1), 1 : 1 + R].reshape(POS, 3 * C)
        add_rows(off, 384, jnp.where(dp == 0, full[:, 0:384], full[:, 384:768]), side, k)

    def weight_grad(side, k):
        for q in range(4):
            part(q, side, k)
        middle(side, k)

    TA, TB = 14, 13

    def tiles(row, n):
        v = WG[pl.ds(pl.multiple_of(row, 8), 8 * n), :].reshape(n, 8, C)
        return jnp.concatenate([v[:, :, 0:128], v[:, :, 128:256]], axis=1)

    def rows(t):
        return jnp.concatenate([t[:, 0:8], t[:, 8:16]], axis=2).reshape(8 * t.shape[0], C)

    def first_phase(m):
        z = m + dp * (3 - 2 * m)
        for y in range(4):
            row = (4 * z + y) * SHARE
            A1S[z, y] = tiles(row, TA).astype(bf16)
            B1S[y, z] = tiles(row + 8 * TA, TB).astype(bf16)
        dz = lax.rem(z - zz + 4, 4)

        @pl.when(dz != 0)
        def _():
            remote(A1S.at[z], A1R.at[dz - 1], s_a1, a1, (dp, s, 4 * z + yy))

        for dy in range(1, 4):
            y = lax.rem(yy + dy, 4)
            remote(B1S.at[y, z], B1R.at[dy - 1, z], s_b1, b1, (dp, s, 4 * zz + y))

    def backward(i, norm_sum):
        k = SPANS - 1 - i

        @pl.when(s < LAYERS - 1)
        def _():
            await_bytes(SB.at[k], sb.at[k])
            await_edges(UR, k, ur.at[k], R)

        @pl.when(s == LAYERS - 1)
        def _():
            await_bytes(SB.at[k, pl.ds(0, NB - 1)], sb.at[k])

        sums = jnp.sum(SB[k], axis=0)
        norm_sum = norm_sum + sums
        gain = GO[0:1]
        m2 = group_sum(sums[0:1] * gain) * (1.0 / GSIZE)
        m1 = group_sum(sums[1:2] * gain) * (1.0 / GSIZE)
        upstream = UR[fr(k)].astype(f32)
        gn = upstream * LO[fr(k)] * gain.reshape(1, 1, 1, C)
        nn = NO[fr(k)]
        inv = MI[k, 1:2]
        gc = (gn - m1.reshape(1, 1, 1, C) - nn * m2.reshape(1, 1, 1, C)) * inv.reshape(1, 1, 1, C)
        gc16 = jnp.where(valid > 0, gc, 0.0).astype(bf16)
        GG[0, k] = gc16[:, 1:5].reshape(POS, C)
        remote(GG.at[0, k], GG.at[1, k], s_pg.at[k], pg.at[k], (other, s, h))

        @pl.when(s > 0)
        def _():
            put_shifted(G, F * k, gc16.astype(f32))
            acc = None
            for ab in range(9):
                a, b = divmod(ab, 3)
                for c in range(3):
                    lhs = G[fr(k, a), b : b + R, :, C * c : C * c + C].reshape(POS, C)
                    t = 9 * (2 - a) + 3 * (2 - b) + 2 - c
                    d = lax.dot_general(
                        lhs, W[t * C : t * C + C, :], (((1,), (1,)), ((), ())), preferred_element_type=f32
                    )
                    acc = d if acc is None else acc + d
            u16 = (UR[fr(k), 1:5].astype(f32).reshape(POS, C) + acc).astype(bf16)
            UO[fr(k)] = u16.reshape(F, R, W16, C)
            gpre = u16.astype(f32) * LP[k]
            SBO[k] = jnp.concatenate(
                [jnp.sum(gpre * NP[k], axis=0, keepdims=True), jnp.sum(gpre, axis=0, keepdims=True)], axis=0
            )
            for b in bands:
                remote(SBO.at[k], SB.at[k, h], s_sb.at[k], sb.at[k], (dp, prv, b))
            send_edges(UO, 0, 3, UR, k, s_ur.at[k], ur.at[k], prv)
            remote(UO.at[fr(k)], UR.at[fr(k), pl.ds(1, R)], s_ur.at[k], ur.at[k], (dp, prv, h))

        @pl.when((s == 0) & ((dp == 1) | (k > 0)))
        def _():
            weight_grad(0, k)

        return norm_sum

    @pl.when((s == 0) & (dp == 0))
    def _():
        def term(i, carry):
            k = SPANS - 1 - i
            await_bytes(GG.at[1, k], pg.at[k])
            weight_grad(1, k)
            return carry

        lax.fori_loop(0, SPANS, term, 0)

    norm_sum = jnp.zeros((2, C), f32)
    for i in range(SPANS):
        norm_sum = backward(i, norm_sum)
    NG[0] = norm_sum
    remote(NG.at[0], NG.at[1], s_ng, ngs, (other, s, h))

    @pl.when((s > 0) | (dp == 1))
    def _():
        await_bytes(GG.at[1, 2], pg.at[2])
        await_bytes(GG.at[1, 1], pg.at[1])

    @pl.when((s > 0) & (dp == 0))
    def _():
        await_bytes(GG.at[1, 0], pg.at[0])

    def term(t, carry):
        late = (t >= 2 + dp).astype(jnp.int32)
        weight_grad(late, SPANS - 1 - (t - late * (2 + dp)))
        return carry

    lax.fori_loop(jnp.where(s > 0, 0, jnp.where(dp == 1, 3, 5)), 5, term, 0)

    @pl.when(dp == 1)
    def _():
        await_bytes(GG.at[1, 0], pg.at[0])

    for q in range(4):
        part(q, dp, 0)
        if q > 0:
            first_phase(q - 1)
    middle(dp, 0)
    first_phase(3)

    await_bytes(NG.at[1], ngs)
    out_n[0] = NG[0] + NG[1]

    def total(r, *at):
        return sum(r[(j, *at)].astype(f32) for j in range(3))

    await_bytes(A1R, a1)
    for dy in range(1, 4):
        y = lax.rem(yy + dy, 4)
        A2S[dy - 1] = (tiles((4 * zz + y) * SHARE, TA) + total(A1R, y)).astype(bf16)
        remote(A2S.at[dy - 1], A2R.at[dy - 1], s_a2, a2, (dp, s, 4 * zz + y))
    await_bytes(B1R, b1)
    for dz in range(1, 4):
        z = lax.rem(zz + dz, 4)
        B2S[dz - 1] = (tiles((4 * z + yy) * SHARE + 8 * TA, TB) + total(B1R, z)).astype(bf16)
        remote(B2S.at[dz - 1], B2R.at[dz - 1], s_b2, b2, (dp, s, 4 * z + yy))
    mine_a = tiles(h * SHARE, TA) + total(A1R, yy)
    mine_b = tiles(h * SHARE + 8 * TA, TB) + total(B1R, zz)
    await_bytes(A2R, a2)
    out_k[0, 0 : 8 * TA] = rows(mine_a + total(A2R))
    await_bytes(B2R, b2)
    out_k[0, 8 * TA : SHARE] = rows(mine_b + total(B2R))

    for k in range(SPANS):
        await_bytes(STO.at[k, pl.ds(0, NB - 1)], s_sto.at[k])
        await_edges(CF, k, s_ch.at[k])
        await_bytes(PX.at[fr(k)], s_px.at[k])
        await_bytes(GG.at[0, k], s_pg.at[k])

        @pl.when(s < LAYERS - 1)
        def _():
            await_bytes(STP.at[k], s_stn.at[k])
            await_edges(CP, k, s_c.at[k], R)

        @pl.when(s <= 1)
        def _():
            await_bytes(XN.at[fr(k)], s_x.at[k])

            await_edges(XP, k, s_xr.at[k])

        @pl.when(s == 1)
        def _():
            await_edges(XP, k, s_xn.at[k])

        @pl.when(s > 0)
        def _():
            await_edges(UR, k, s_ur.at[k], R)
            await_bytes(SB.at[k], s_sb.at[k])

        @pl.when(s == LAYERS - 1)
        def _():
            await_edges(XP, k, s_rl.at[k], R)
            await_edges(UR, k, s_og.at[k])
            await_bytes(SB.at[k, pl.ds(0, NB - 1)], s_sbo.at[k])

    @pl.when(s < LAYERS - 1)
    def _():
        await_bytes(GO, s_gp)

    await_bytes(NG.at[0], s_ng)
    await_bytes(A1R, s_a1)
    await_bytes(B1R, s_b1)
    await_bytes(A2R, s_a2)
    await_bytes(B2R, s_b2)


def per_device(video, kernels, gains, shifts, out_grad):
    dma = pltpu.SemaphoreType.DMA
    six = (F * SPANS, 6, W16, C)
    four = (F * SPANS, R, W16, C)
    wide = (F * SPANS + 2, 6, W16, 3 * C)
    table = (SPANS, NB, 2, C)
    scratch = [
        pltpu.VMEM((27 * C, C), bf16),
        pltpu.VMEM(six, bf16),
        pltpu.VMEM(six, bf16),
        pltpu.VMEM(four, bf16),
        pltpu.VMEM(four, bf16),
        pltpu.VMEM(six, bf16),
        pltpu.VMEM(four, bf16),
        pltpu.VMEM(six, f32),
        pltpu.VMEM((2,) + wide, bf16),
        pltpu.VMEM(six, bf16),
        pltpu.VMEM(wide, bf16),
        pltpu.VMEM((2, SPANS, POS, C), bf16),
        pltpu.VMEM(six, bf16),
        pltpu.VMEM(four, bf16),
        pltpu.VMEM(table, f32),
        pltpu.VMEM(table, f32),
        pltpu.VMEM(table, f32),
        pltpu.VMEM((SPANS, 2, C), f32),
        pltpu.VMEM((2, C), f32),
        pltpu.VMEM((2, C), f32),
        pltpu.VMEM((SPANS, POS, C), f32),
        pltpu.VMEM((SPANS, POS, C), f32),
        pltpu.VMEM(six, f32),
        pltpu.VMEM(six, f32),
        pltpu.VMEM((SPANS, 2, C), f32),
        pltpu.VMEM((HALF, C), f32),
        pltpu.VMEM((4, 4, 14, 16, 128), bf16),
        pltpu.VMEM((3, 4, 14, 16, 128), bf16),
        pltpu.VMEM((4, 4, 13, 16, 128), bf16),
        pltpu.VMEM((3, 4, 13, 16, 128), bf16),
        pltpu.VMEM((3, 14, 16, 128), bf16),
        pltpu.VMEM((3, 14, 16, 128), bf16),
        pltpu.VMEM((3, 13, 16, 128), bf16),
        pltpu.VMEM((3, 13, 16, 128), bf16),
        pltpu.VMEM((2, 2, C), f32),
    ]
    k3 = dma((SPANS,))
    sems = [pltpu.SemaphoreType.REGULAR, dma] + [k3] * 11 + [dma] * 6
    sems += [k3] * 14 + [dma] * 6
    anyspec = pl.BlockSpec(memory_space=pl.ANY)
    vm = pl.BlockSpec(memory_space=pltpu.VMEM)
    return pl.pallas_call(
        kernel,
        out_shape=(
            jax.ShapeDtypeStruct((1, SHARE, C), f32),
            jax.ShapeDtypeStruct((1, 2, C), f32),
        ),
        in_specs=[anyspec, anyspec, vm, vm, anyspec],
        out_specs=(vm, vm),
        scratch_shapes=scratch + sems,
        compiler_params=pltpu.CompilerParams(
            collective_id=0, has_side_effects=True, vmem_limit_bytes=60 * 2**20
        ),
    )(video, kernels, gains, shifts, out_grad)


def solution(mesh):
    return jax.shard_map(
        per_device,
        mesh=mesh,
        in_specs=(
            P("dp", None, "height", None, None),
            P("pipe", None, None),
            P("pipe", None),
            P("pipe", None),
            P("dp", None, "height", None, None),
        ),
        out_specs=(P("pipe", ("dp", "height"), None), P("pipe", None, None)),
        check_vma=False,
    )
```

```python
import functools

import jax
import jax.numpy as jnp
from jax import lax
from jax.experimental import pallas as pl
from jax.experimental.pallas import tpu as pltpu
from jax.sharding import PartitionSpec as P

GROUPS = 32
F = 4
SPANS = 3
NB = 16
LAYERS = 4
R = 4
W16 = 16
C = 256
POS = F * R * W16
GSIZE = float(POS * NB * (C // GROUPS))
HALF = 3456
SHARE = 216
EPS = 1e-05
f32 = jnp.float32
bf16 = jnp.bfloat16
MESH = pl.DeviceIdType.MESH


def group_mate(x, d):
    lane = lax.broadcasted_iota(jnp.int32, x.shape, 1)
    return jnp.where((lane & d) != 0, pltpu.roll(x, d, 1), pltpu.roll(x, C - d, 1))


def group_sum(x):
    for d in (1, 2, 4):
        x = x + group_mate(x, d)
    return x


def combine(table):
    sums = jnp.sum(table, axis=0)
    mean_c = sums[0:1] * (1.0 / NB)
    between = jnp.sum((table - mean_c[None]) ** 2, axis=0)[0:1]
    both = jnp.concatenate([mean_c, sums[1:2] + POS * between], axis=0)
    count = float(POS * NB)
    for d in (1, 2, 4):
        mate = group_mate(both, d)
        gap = both[0:1] - mate[0:1]
        both = jnp.concatenate(
            [0.5 * (both[0:1] + mate[0:1]), both[1:2] + mate[1:2] + (0.5 * count) * gap * gap], axis=0
        )
        count = 2.0 * count
    return both[0:1], lax.rsqrt(both[1:2] * (1.0 / GSIZE) + EPS)


def sigmoid(v):
    return 1.0 / (1.0 + jnp.exp(-v))


def put_shifted(dst, frame, x):
    v = x.reshape(F * 6, W16, C)
    col = lax.broadcasted_iota(jnp.int32, v.shape, 1)
    left = jnp.where(col == 0, 0.0, pltpu.roll(v, 1, 1))
    right = jnp.where(col == W16 - 1, 0.0, pltpu.roll(v, W16 - 1, 1))
    dst[pl.ds(frame, F), :, :, 0:C] = left.astype(bf16).reshape(F, 6, W16, C)
    dst[pl.ds(frame, F), :, :, C : 2 * C] = v.astype(bf16).reshape(F, 6, W16, C)
    dst[pl.ds(frame, F), :, :, 2 * C : 3 * C] = right.astype(bf16).reshape(F, 6, W16, C)


def kernel(
    video, kern, gains, shifts, ograd, out_k, out_n,
    W, XP, XR, XN, RL, CP, CO, CF, SS, PX, G, GG, UR, UO, STP, STO, SB, SBO, GO, GP, NP, LP, NO, LO, MI,
    WG, A1S, A1R, B1S, B1R, A2S, A2R, B2S, B2R, NG,
    ready, w_sem, xpc, xph, rl, cp, stp, sto, cfh, ur, sb, px, pg, a1, b1, a2, b2, ngs, gps,
    s_x, s_xn, s_xr, s_rl, s_c, s_ch, s_sto, s_stn, s_px, s_pg, s_ur, s_og, s_sb, s_sbo, s_a1, s_b1, s_a2, s_b2, s_ng, s_gp,
):
    dp, s, h = lax.axis_index("dp"), lax.axis_index("pipe"), lax.axis_index("height")
    nxt, prv = lax.rem(s + 1, LAYERS), lax.rem(s + LAYERS - 1, LAYERS)
    up, dn = lax.rem(h + NB - 1, NB), lax.rem(h + 1, NB)
    other = 1 - dp
    zz, yy = lax.div(h, 4), lax.rem(h, 4)
    steps = [(i, j) for i in range(4) for j in range(4)]
    steps.sort(key=lambda o: -(min(o[0], 4 - o[0]) + min(o[1], 4 - o[1])))
    bands = [lax.rem(zz + i, 4) * 4 + lax.rem(yy + j, 4) for i, j in steps]

    def remote(src, dst, ssem, rsem, dev):
        pltpu.make_async_remote_copy(
            src_ref=src, dst_ref=dst, send_sem=ssem, recv_sem=rsem, device_id=dev, device_id_type=MESH
        ).start()

    def await_bytes(ref, sem):
        pltpu.make_async_copy(ref, ref, sem).wait()

    inside = (h > 0) & (h < NB - 1)

    def await_edges(ref, k, sem, rows=0):
        @pl.when(inside)
        def _():
            await_bytes(ref.at[fr(k), pl.ds(0, rows + 2)], sem)

        @pl.when(jnp.logical_not(inside))
        def _():
            await_bytes(ref.at[fr(k), pl.ds(0, rows + 1)], sem)

    def send_edges(src, first, last, dst, k, ssem, rsem, layer):
        @pl.when(h > 0)
        def _():
            remote(src.at[fr(k), pl.ds(first, 1)], dst.at[fr(k), pl.ds(5, 1)], ssem, rsem, (dp, layer, up))

        @pl.when(h < NB - 1)
        def _():
            remote(src.at[fr(k), pl.ds(last, 1)], dst.at[fr(k), pl.ds(0, 1)], ssem, rsem, (dp, layer, dn))

    def fr(k, first=0):
        return pl.ds(F * k + first, F)

    wcopy = pltpu.make_async_copy(kern.at[0], W, w_sem)
    wcopy.start()
    barrier = pltpu.get_barrier_semaphore()
    far = lax.rem(s + 2, LAYERS)

    @pl.when(s == LAYERS - 1)
    def _():
        @pl.when(h > 0)
        def _():
            pl.semaphore_signal(barrier, inc=1, device_id=(dp, far, up), device_id_type=MESH)

        @pl.when(h < NB - 1)
        def _():
            pl.semaphore_signal(barrier, inc=1, device_id=(dp, far, dn), device_id_type=MESH)

        pl.semaphore_signal(barrier, inc=1, device_id=(dp, far, h), device_id_type=MESH)

    for b in bands[:-1]:
        pl.semaphore_signal(barrier, inc=1, device_id=(dp, s, b), device_id_type=MESH)
    for p in (nxt, prv):
        pl.semaphore_signal(barrier, inc=1, device_id=(dp, p, h), device_id_type=MESH)
    pl.semaphore_signal(barrier, inc=1, device_id=(other, s, h), device_id_type=MESH)

    @pl.when(s <= 1)
    def _():
        for k in range(SPANS):
            pltpu.make_async_copy(video.at[0, fr(k)], XP.at[fr(k), pl.ds(1, R)], xpc.at[k]).start()

    @pl.when(s == LAYERS - 1)
    def _():
        for k in range(SPANS):
            pltpu.make_async_copy(ograd.at[0, fr(k)], UR.at[fr(k), pl.ds(1, R)], ur.at[k]).start()

    SS[:, 0:2] = jnp.zeros((2, 2, 6, W16, 3 * C), bf16)
    G[12:14] = jnp.zeros((2, 6, W16, 3 * C), bf16)
    GO[0:1] = gains[...]
    GO[1:2] = shifts[...]
    from_far = (h > 0).astype(jnp.int32) + (h < NB - 1).astype(jnp.int32) + 1
    pl.semaphore_wait(barrier, NB - 1 + 2 + 1 + jnp.where(s == 1, from_far, 0))
    for p in (nxt, prv):
        pl.semaphore_signal(ready, inc=1, device_id=(dp, p, h), device_id_type=MESH)

    @pl.when(s <= 1)
    def _():
        for k in range(SPANS):
            send_edges(video.at[0], 0, 3, XP, k, s_xr.at[k], xph.at[k], s)

    @pl.when(s == LAYERS - 1)
    def _():
        for k in reversed(range(SPANS)):
            send_edges(ograd.at[0], 0, 3, UR, k, s_og.at[k], ur.at[k], s)

    @pl.when(s < LAYERS - 1)
    def _():
        remote(GO, GP, s_gp, gps, (dp, nxt, h))

    @pl.when(s > 0)
    def _():
        await_bytes(GP, gps)

    row = lax.broadcasted_iota(jnp.int32, (1, 6, 1, 1), 1)
    valid = jnp.where(row == 0, (h > 0).astype(f32), jnp.where(row == 5, (h < NB - 1).astype(f32), 1.0))

    def normalized(conv, table_ref, k):
        mu, inv = combine(table_ref[k])
        own = (table_ref[k, h][0:1] - mu).reshape(1, 1, 1, C)
        above = (table_ref[k, up][0:1] - mu).reshape(1, 1, 1, C)
        below = (table_ref[k, dn][0:1] - mu).reshape(1, 1, 1, C)
        off = jnp.concatenate([above, own, own, own, own, below], axis=1)
        return (conv + off) * inv.reshape(1, 1, 1, C)

    gain4 = GO[0:1].reshape(1, 1, 1, C)
    shift4 = GO[1:2].reshape(1, 1, 1, C)

    def layer(k):
        await_bytes(XP.at[fr(k), pl.ds(1, R)], xpc.at[k])

        await_edges(XP, k, xph.at[k])

        @pl.when(s == 0)
        def _():
            x = jnp.where(valid > 0, XP[fr(k)].astype(f32), 0.0)
            XR[fr(k)] = x.astype(bf16)
            put_shifted(SS.at[0], 2 + F * k, x)

        @pl.when(s > 0)
        def _():
            await_bytes(STP.at[k], stp.at[k])
            await_edges(CP, k, cp.at[k], R)
            normed = normalized(CP[fr(k)].astype(f32), STP, k)
            pre = normed * GP[0:1].reshape(1, 1, 1, C) + GP[1:2].reshape(1, 1, 1, C)
            sig = sigmoid(pre)
            x = XP[fr(k)].astype(f32) + pre * sig
            x16 = jnp.where(valid > 0, x, 0.0).astype(bf16)
            XR[fr(k)] = x16
            put_shifted(SS.at[0], 2 + F * k, x16.astype(f32))
            NP[k] = normed[:, 1:5].reshape(POS, C)
            LP[k] = (sig * (1.0 + pre * (1.0 - sig)))[:, 1:5].reshape(POS, C)

        @pl.when(k == 0)
        def _():
            wcopy.wait()

        acc = None
        for ab in range(9):
            a, b = divmod(ab, 3)
            lhs = SS[0, fr(k, a), b : b + R].reshape(POS, 3 * C)
            d = jnp.dot(lhs, W[ab * 768 : ab * 768 + 768, :], preferred_element_type=f32)
            acc = d if acc is None else acc + d
        mean = jnp.sum(acc, axis=0, keepdims=True) * (1.0 / POS)
        cen = acc - mean
        STO[k, h] = jnp.concatenate([mean, jnp.sum(cen * cen, axis=0, keepdims=True)], axis=0)
        CF[fr(k), 1:5] = cen.reshape(F, R, W16, C)
        CO[fr(k)] = cen.astype(bf16).reshape(F, R, W16, C)

        @pl.when((s < LAYERS - 1) & (k == 0))
        def _():
            pl.semaphore_wait(ready, 2)

        @pl.when(s < LAYERS - 1)
        def _():
            for b in bands:
                remote(STO.at[k, h], STP.at[k, h], s_stn.at[k], stp.at[k], (dp, nxt, b))

        for b in bands[:-1]:
            remote(STO.at[k, h], STO.at[k, h], s_sto.at[k], sto.at[k], (dp, s, b))

        @pl.when(s < LAYERS - 1)
        def _():
            send_edges(CO, 0, 3, CP, k, s_c.at[k], cp.at[k], nxt)
            remote(CO.at[fr(k)], CP.at[fr(k), pl.ds(1, R)], s_c.at[k], cp.at[k], (dp, nxt, h))

        send_edges(CF, 1, 4, CF, k, s_ch.at[k], cfh.at[k], s)
        remote(XR.at[fr(k)], PX.at[fr(k)], s_px.at[k], px.at[k], (other, s, h))

    def own_rows(k):
        await_bytes(STO.at[k, pl.ds(0, NB - 1)], sto.at[k])
        mu, inv = combine(STO[k])
        MI[k] = jnp.concatenate([mu, inv], axis=0)
        off = (STO[k, h][0:1] - mu).reshape(1, 1, 1, C)
        normed = (CF[fr(k), 1:5] + off) * inv.reshape(1, 1, 1, C)
        pre = normed * gain4 + shift4
        sig = sigmoid(pre)
        slope = sig * (1.0 + pre * (1.0 - sig))
        NO[fr(k), 1:5] = normed
        LO[fr(k), 1:5] = slope

        @pl.when(s <= 1)
        def _():
            XN[fr(k)] = (XR[fr(k), 1:5].astype(f32) + pre * sig).astype(bf16)

        @pl.when(s == 0)
        def _():
            remote(XN.at[fr(k)], RL.at[fr(k)], s_x.at[k], rl.at[k], (dp, prv, h))

        @pl.when(s == 1)
        def _():
            far = lax.rem(s + 2, LAYERS)
            send_edges(XN, 0, 3, XP, k, s_xn.at[k], xph.at[k], far)
            remote(XN.at[fr(k)], XP.at[fr(k), pl.ds(1, R)], s_x.at[k], xpc.at[k], (dp, far, h))

        @pl.when(s == LAYERS - 1)
        def _():
            await_edges(UR, k, ur.at[k], R)
            gpre = (UR[fr(k), 1:5].astype(f32) * slope).reshape(POS, C)
            nn = normed.reshape(POS, C)
            SB[k, h] = jnp.concatenate(
                [jnp.sum(gpre * nn, axis=0, keepdims=True), jnp.sum(gpre, axis=0, keepdims=True)], axis=0
            )
            for b in bands[:-1]:
                remote(SB.at[k, h], SB.at[k, h], s_sbo.at[k], sb.at[k], (dp, s, b))

    def own_halo(k):
        await_edges(CF, k, cfh.at[k])
        mu, inv = MI[k, 0:1], MI[k, 1:2]
        for r, b in ((0, up), (5, dn)):
            off = (STO[k, b][0:1] - mu).reshape(1, 1, 1, C)
            normed = (CF[fr(k), r : r + 1] + off) * inv.reshape(1, 1, 1, C)
            pre = normed * gain4 + shift4
            sig = sigmoid(pre)
            NO[fr(k), r : r + 1] = normed
            LO[fr(k), r : r + 1] = sig * (1.0 + pre * (1.0 - sig))

    @pl.when(s == LAYERS - 1)
    def _():
        pl.semaphore_wait(ready, 2)
        for k in range(SPANS):
            await_bytes(RL.at[fr(k)], rl.at[k])
            send_edges(RL, 0, 3, XP, k, s_rl.at[k], xph.at[k], prv)
            remote(RL.at[fr(k)], XP.at[fr(k), pl.ds(1, R)], s_rl.at[k], xpc.at[k], (dp, prv, h))

    def forward(k, carry):
        layer(k)
        return carry

    lax.fori_loop(0, SPANS, forward, 0)

    def own(k, carry):
        own_rows(k)
        return carry

    lax.fori_loop(0, SPANS, own, 0)

    def halo(i, carry):
        own_halo(SPANS - 1 - i)
        return carry

    lax.fori_loop(0, SPANS, halo, 0)

    def partner(k, carry):
        await_bytes(PX.at[fr(k)], px.at[k])
        put_shifted(SS.at[1], 2 + F * k, PX[fr(k)].astype(f32))
        return carry

    lax.fori_loop(0, SPANS, partner, 0)
    WG[...] = jnp.zeros((HALF, C), f32)

    def add_rows(off, rows, lhs, side, k):
        WG[pl.ds(off, rows), :] += lax.dot_general(
            lhs, GG[side, k], (((0,), (0,)), ((), ())), preferred_element_type=f32
        )

    def part(q, side, k):
        ab = q + dp * (8 - 2 * q)
        a, b = lax.div(ab, 3), lax.rem(ab, 3)
        off = pl.multiple_of(ab * 768 - HALF * dp, 128)
        add_rows(off, 768, SS[side, fr(k, a), pl.ds(b, R)].reshape(POS, 3 * C), side, k)

    def middle(side, k):
        off = pl.multiple_of((HALF - 384) * (1 - dp), 128)
        full = SS[side, fr(k, 1), 1 : 1 + R].reshape(POS, 3 * C)
        add_rows(off, 384, jnp.where(dp == 0, full[:, 0:384], full[:, 384:768]), side, k)

    def weight_grad(side, k):
        for q in range(4):
            part(q, side, k)
        middle(side, k)

    TA, TB = 14, 13
    cuts = ((10, 0), (4, 10))

    def tiles(row, n):
        v = WG[pl.ds(pl.multiple_of(row, 8), 8 * n), :].reshape(n, 8, C)
        return jnp.concatenate([v[:, :, 0:128], v[:, :, 128:256]], axis=1)

    def rows(t):
        return jnp.concatenate([t[:, 0:8], t[:, 8:16]], axis=2).reshape(8 * t.shape[0], C)

    def first_phase(m):
        z = m + dp * (3 - 2 * m)
        for y in range(4):
            row = (4 * z + y) * SHARE
            A1S[z, y] = tiles(row, TA).astype(bf16)
            B1S[y, z] = tiles(row + 8 * TA, TB).astype(bf16)
        dz = lax.rem(z - zz + 4, 4)
        n, _ = cuts[0]

        @pl.when(dz != 0)
        def _():
            remote(
                A1S.at[z, :, pl.ds(0, n)], A1R.at[dz - 1, :, pl.ds(0, n)], s_a1.at[0], a1.at[0], (dp, s, 4 * z + yy)
            )

        for dy in range(1, 4):
            y = lax.rem(yy + dy, 4)
            remote(
                B1S.at[y, z, pl.ds(0, n)], B1R.at[dy - 1, z, pl.ds(0, n)], s_b1.at[0], b1.at[0], (dp, s, 4 * zz + y)
            )

    def first_phase_rest():
        n = cuts[0][0]
        for d in range(1, 4):
            z, y = lax.rem(zz + d, 4), lax.rem(yy + d, 4)
            rest = pl.ds(n, TA - n)
            remote(A1S.at[z, :, rest], A1R.at[d - 1, :, rest], s_a1.at[1], a1.at[1], (dp, s, 4 * z + yy))
            rest = pl.ds(n, TB - n)
            remote(B1S.at[y, :, rest], B1R.at[d - 1, :, rest], s_b1.at[1], b1.at[1], (dp, s, 4 * zz + y))

    def backward(i, norm_sum):
        k = SPANS - 1 - i

        @pl.when(s < LAYERS - 1)
        def _():
            await_bytes(SB.at[k], sb.at[k])
            await_edges(UR, k, ur.at[k], R)

        @pl.when(s == LAYERS - 1)
        def _():
            await_bytes(SB.at[k, pl.ds(0, NB - 1)], sb.at[k])

        sums = jnp.sum(SB[k], axis=0)
        norm_sum = norm_sum + sums
        gain = GO[0:1]
        means = group_sum(sums * gain) * (1.0 / GSIZE)
        m2, m1 = means[0:1], means[1:2]
        upstream = UR[fr(k)].astype(f32)
        gn = upstream * LO[fr(k)] * gain.reshape(1, 1, 1, C)
        nn = NO[fr(k)]
        inv = MI[k, 1:2]
        gc = (gn - m1.reshape(1, 1, 1, C) - nn * m2.reshape(1, 1, 1, C)) * inv.reshape(1, 1, 1, C)
        gc16 = jnp.where(valid > 0, gc, 0.0).astype(bf16)
        GG[0, k] = gc16[:, 1:5].reshape(POS, C)
        remote(GG.at[0, k], GG.at[1, k], s_pg.at[k], pg.at[k], (other, s, h))

        @pl.when(s > 0)
        def _():
            put_shifted(G, F * k, gc16.astype(f32))
            acc = None
            for ab in range(9):
                a, b = divmod(ab, 3)
                for c in range(3):
                    lhs = G[fr(k, a), b : b + R, :, C * c : C * c + C].reshape(POS, C)
                    t = 9 * (2 - a) + 3 * (2 - b) + 2 - c
                    d = lax.dot_general(
                        lhs, W[t * C : t * C + C, :], (((1,), (1,)), ((), ())), preferred_element_type=f32
                    )
                    acc = d if acc is None else acc + d
            u16 = (UR[fr(k), 1:5].astype(f32).reshape(POS, C) + acc).astype(bf16)
            UO[fr(k)] = u16.reshape(F, R, W16, C)
            gpre = u16.astype(f32) * LP[k]
            SBO[k] = jnp.concatenate(
                [jnp.sum(gpre * NP[k], axis=0, keepdims=True), jnp.sum(gpre, axis=0, keepdims=True)], axis=0
            )
            for b in bands:
                remote(SBO.at[k], SB.at[k, h], s_sb.at[k], sb.at[k], (dp, prv, b))
            send_edges(UO, 0, 3, UR, k, s_ur.at[k], ur.at[k], prv)
            remote(UO.at[fr(k)], UR.at[fr(k), pl.ds(1, R)], s_ur.at[k], ur.at[k], (dp, prv, h))

        @pl.when((s == 0) & ((dp == 1) | (k > 0)))
        def _():
            weight_grad(0, k)

        if i == 0:

            @pl.when((s == 0) & (dp == 0))
            def _():
                await_bytes(GG.at[1, 0], pg.at[0])
                weight_grad(1, 0)

        return norm_sum

    @pl.when((s == 0) & (dp == 0))
    def _():
        def term(i, carry):
            k = SPANS - 1 - i
            await_bytes(GG.at[1, k], pg.at[k])
            weight_grad(1, k)
            return carry

        lax.fori_loop(0, SPANS - 1, term, 0)

    norm_sum = jnp.zeros((2, C), f32)
    for i in range(SPANS):
        norm_sum = backward(i, norm_sum)
    NG[0] = norm_sum
    remote(NG.at[0], NG.at[1], s_ng, ngs, (other, s, h))

    @pl.when((s > 0) | (dp == 1))
    def _():
        await_bytes(GG.at[1, 2], pg.at[2])
        await_bytes(GG.at[1, 1], pg.at[1])

    @pl.when((s > 0) & (dp == 0))
    def _():
        await_bytes(GG.at[1, 0], pg.at[0])

    def term(t, carry):
        late = (t >= 2 + dp).astype(jnp.int32)
        weight_grad(late, SPANS - 1 - (t - late * (2 + dp)))
        return carry

    lax.fori_loop(jnp.where(s > 0, 0, jnp.where(dp == 1, 3, 5)), 5, term, 0)

    @pl.when(dp == 1)
    def _():
        await_bytes(GG.at[1, 0], pg.at[0])

    for q in range(4):
        part(q, dp, 0)
        if q > 0:
            first_phase(q - 1)
    middle(dp, 0)
    first_phase(3)
    first_phase_rest()

    await_bytes(NG.at[1], ngs)
    out_n[0] = NG[0] + NG[1]

    def total(r, *at):
        return sum(r[(j, *at)].astype(f32) for j in range(3))

    for i, (n, t0) in enumerate(cuts):
        span = pl.ds(t0, n)
        await_bytes(A1R.at[:, :, span], a1.at[i])
        for dy in range(1, 4):
            y = lax.rem(yy + dy, 4)
            A2S[dy - 1, span] = (tiles((4 * zz + y) * SHARE + 8 * t0, n) + total(A1R, y, span)).astype(bf16)
            remote(A2S.at[dy - 1, span], A2R.at[dy - 1, span], s_a2, a2, (dp, s, 4 * zz + y))
        n = min(n, TB - t0)
        span = pl.ds(t0, n)
        await_bytes(B1R.at[:, :, span], b1.at[i])
        for dz in range(1, 4):
            z = lax.rem(zz + dz, 4)
            row = (4 * z + yy) * SHARE + 8 * (TA + t0)
            B2S[dz - 1, span] = (tiles(row, n) + total(B1R, z, span)).astype(bf16)
            remote(B2S.at[dz - 1, span], B2R.at[dz - 1, span], s_b2, b2, (dp, s, 4 * z + yy))
    mine_a = tiles(h * SHARE, TA) + total(A1R, yy)
    mine_b = tiles(h * SHARE + 8 * TA, TB) + total(B1R, zz)
    await_bytes(A2R, a2)
    out_k[0, 0 : 8 * TA] = rows(mine_a + total(A2R))
    await_bytes(B2R, b2)
    out_k[0, 8 * TA : SHARE] = rows(mine_b + total(B2R))

    for k in range(SPANS):
        await_bytes(STO.at[k, pl.ds(0, NB - 1)], s_sto.at[k])
        await_edges(CF, k, s_ch.at[k])
        await_bytes(PX.at[fr(k)], s_px.at[k])
        await_bytes(GG.at[0, k], s_pg.at[k])

        @pl.when(s < LAYERS - 1)
        def _():
            await_bytes(STP.at[k], s_stn.at[k])
            await_edges(CP, k, s_c.at[k], R)

        @pl.when(s <= 1)
        def _():
            await_bytes(XN.at[fr(k)], s_x.at[k])

            await_edges(XP, k, s_xr.at[k])

        @pl.when(s == 1)
        def _():
            await_edges(XP, k, s_xn.at[k])

        @pl.when(s > 0)
        def _():
            await_edges(UR, k, s_ur.at[k], R)
            await_bytes(SB.at[k], s_sb.at[k])

        @pl.when(s == LAYERS - 1)
        def _():
            await_edges(XP, k, s_rl.at[k], R)
            await_edges(UR, k, s_og.at[k])
            await_bytes(SB.at[k, pl.ds(0, NB - 1)], s_sbo.at[k])

    @pl.when(s < LAYERS - 1)
    def _():
        await_bytes(GO, s_gp)

    await_bytes(NG.at[0], s_ng)
    for i, (n, t0) in enumerate(cuts):
        await_bytes(A1R.at[:, :, pl.ds(t0, n)], s_a1.at[i])
        await_bytes(B1R.at[:, :, pl.ds(t0, min(n, TB - t0))], s_b1.at[i])
    await_bytes(A2R, s_a2)
    await_bytes(B2R, s_b2)


def per_device(video, kernels, gains, shifts, out_grad):
    dma = pltpu.SemaphoreType.DMA
    six = (F * SPANS, 6, W16, C)
    four = (F * SPANS, R, W16, C)
    wide = (F * SPANS + 2, 6, W16, 3 * C)
    table = (SPANS, NB, 2, C)
    scratch = [
        pltpu.VMEM((27 * C, C), bf16),
        pltpu.VMEM(six, bf16),
        pltpu.VMEM(six, bf16),
        pltpu.VMEM(four, bf16),
        pltpu.VMEM(four, bf16),
        pltpu.VMEM(six, bf16),
        pltpu.VMEM(four, bf16),
        pltpu.VMEM(six, f32),
        pltpu.VMEM((2,) + wide, bf16),
        pltpu.VMEM(six, bf16),
        pltpu.VMEM(wide, bf16),
        pltpu.VMEM((2, SPANS, POS, C), bf16),
        pltpu.VMEM(six, bf16),
        pltpu.VMEM(four, bf16),
        pltpu.VMEM(table, f32),
        pltpu.VMEM(table, f32),
        pltpu.VMEM(table, f32),
        pltpu.VMEM((SPANS, 2, C), f32),
        pltpu.VMEM((2, C), f32),
        pltpu.VMEM((2, C), f32),
        pltpu.VMEM((SPANS, POS, C), f32),
        pltpu.VMEM((SPANS, POS, C), f32),
        pltpu.VMEM(six, f32),
        pltpu.VMEM(six, f32),
        pltpu.VMEM((SPANS, 2, C), f32),
        pltpu.VMEM((HALF, C), f32),
        pltpu.VMEM((4, 4, 14, 16, 128), bf16),
        pltpu.VMEM((3, 4, 14, 16, 128), bf16),
        pltpu.VMEM((4, 4, 13, 16, 128), bf16),
        pltpu.VMEM((3, 4, 13, 16, 128), bf16),
        pltpu.VMEM((3, 14, 16, 128), bf16),
        pltpu.VMEM((3, 14, 16, 128), bf16),
        pltpu.VMEM((3, 13, 16, 128), bf16),
        pltpu.VMEM((3, 13, 16, 128), bf16),
        pltpu.VMEM((2, 2, C), f32),
    ]
    k3 = dma((SPANS,))
    two = dma((2,))
    sems = [pltpu.SemaphoreType.REGULAR, dma] + [k3] * 11 + [two, two] + [dma] * 4
    sems += [k3] * 14 + [two, two] + [dma] * 4
    anyspec = pl.BlockSpec(memory_space=pl.ANY)
    vm = pl.BlockSpec(memory_space=pltpu.VMEM)
    return pl.pallas_call(
        kernel,
        out_shape=(
            pltpu.VMEM((1, SHARE, C), f32),
            pltpu.VMEM((1, 2, C), f32),
        ),
        in_specs=[anyspec, anyspec, vm, vm, anyspec],
        out_specs=(vm, vm),
        scratch_shapes=scratch + sems,
        compiler_params=pltpu.CompilerParams(
            collective_id=0, has_side_effects=True, vmem_limit_bytes=60 * 2**20
        ),
    )(video, kernels, gains, shifts, out_grad)


def solution(mesh):
    return jax.shard_map(
        per_device,
        mesh=mesh,
        in_specs=(
            P("dp", None, "height", None, None),
            P("pipe", None, None),
            P("pipe", None),
            P("pipe", None),
            P("dp", None, "height", None, None),
        ),
        out_specs=(P("pipe", ("dp", "height"), None), P("pipe", None, None)),
        check_vma=False,
    )
```

```python
import functools

import jax
import jax.numpy as jnp
from jax import lax
from jax.experimental import pallas as pl
from jax.experimental.pallas import tpu as pltpu
from jax.sharding import PartitionSpec as P

GROUPS = 32
F = 4
SPANS = 3
NB = 16
LAYERS = 4
R = 4
W16 = 16
C = 256
POS = F * R * W16
GSIZE = float(POS * NB * (C // GROUPS))
HALF = 3456
SHARE = 216
EPS = 1e-05
f32 = jnp.float32
bf16 = jnp.bfloat16
MESH = pl.DeviceIdType.MESH


def group_mate(x, d):
    lane = lax.broadcasted_iota(jnp.int32, x.shape, 1)
    return jnp.where((lane & d) != 0, pltpu.roll(x, d, 1), pltpu.roll(x, C - d, 1))


def group_sum(x):
    for d in (1, 2, 4):
        x = x + group_mate(x, d)
    return x


def even(x):
    return (lax.broadcasted_iota(jnp.int32, x.shape, 1) & 1) == 0


def spread(x):
    return jnp.where(even(x), x, pltpu.roll(x, 1, 1))


def summary(mean_c, dev_c):
    both = jnp.concatenate([mean_c, dev_c], axis=0)
    count = float(POS)
    for d in (1, 2, 4):
        mate = group_mate(both, d)
        gap = both[0:1] - mate[0:1]
        both = jnp.concatenate(
            [0.5 * (both[0:1] + mate[0:1]), both[1:2] + mate[1:2] + (0.5 * count) * gap * gap], axis=0
        )
        count = 2.0 * count
    return both[0:1], jnp.where(even(mean_c), both[0:1], both[1:2])


def combine(table):
    sums = jnp.sum(table, axis=0)
    mean = sums * (1.0 / NB)
    between = jnp.sum((table - mean[None]) ** 2, axis=0)
    dev = pltpu.roll(sums, C - 1, 1) + (GSIZE / NB) * between
    both = spread(jnp.concatenate([mean, lax.rsqrt(dev * (1.0 / GSIZE) + EPS)], axis=0))
    return both[0:1], both[1:2]


def sigmoid(v):
    return 0.5 * jnp.tanh(0.5 * v) + 0.5


def put_shifted(dst, frame, x):
    n = x.shape[1]
    v = x.reshape(F * n, W16, C)
    col = lax.broadcasted_iota(jnp.int32, v.shape, 1)
    left = jnp.where(col == 0, 0.0, pltpu.roll(v, 1, 1))
    right = jnp.where(col == W16 - 1, 0.0, pltpu.roll(v, W16 - 1, 1))
    for c, part in enumerate((left, v, right)):
        dst[pl.ds(frame, F), :, :, C * c : C * c + C] = part.astype(bf16).reshape(F, n, W16, C)


def kernel(
    video, kern, gains, shifts, ograd, out_k, out_n,
    W, XP, XR, XN, RL, CP, CO, CF, SS, PX, G, GG, UR, UO, STP, STO, SB, SBO, GO, GP, NP, LP, NO, LO, MI,
    WG, A1S, A1R, B1S, B1R, A2S, A2R, B2S, B2R, NG,
    ready, w_sem, xpc, xph, rl, cp, stp, sto, cfh, ur, sb, px, pg, a1, b1, a2, b2, ngs, gps,
    s_x, s_xn, s_xr, s_rl, s_c, s_ch, s_sto, s_stn, s_px, s_pg, s_ur, s_og, s_sb, s_sbo, s_a1, s_b1, s_a2, s_b2, s_ng, s_gp,
):
    dp, s, h = lax.axis_index("dp"), lax.axis_index("pipe"), lax.axis_index("height")
    nxt, prv = lax.rem(s + 1, LAYERS), lax.rem(s + LAYERS - 1, LAYERS)
    up, dn = lax.rem(h + NB - 1, NB), lax.rem(h + 1, NB)
    other = 1 - dp
    zz, yy = lax.div(h, 4), lax.rem(h, 4)
    steps = [(i, j) for i in range(4) for j in range(4)]
    steps.sort(key=lambda o: -(min(o[0], 4 - o[0]) + min(o[1], 4 - o[1])))
    bands = [lax.rem(zz + i, 4) * 4 + lax.rem(yy + j, 4) for i, j in steps]

    def remote(src, dst, ssem, rsem, dev):
        pltpu.make_async_remote_copy(
            src_ref=src, dst_ref=dst, send_sem=ssem, recv_sem=rsem, device_id=dev, device_id_type=MESH
        ).start()

    def await_bytes(ref, sem):
        pltpu.make_async_copy(ref, ref, sem).wait()

    inside = (h > 0) & (h < NB - 1)

    def await_edges(ref, k, sem, rows=0):
        @pl.when(inside)
        def _():
            await_bytes(ref.at[fr(k), pl.ds(0, rows + 2)], sem)

        @pl.when(jnp.logical_not(inside))
        def _():
            await_bytes(ref.at[fr(k), pl.ds(0, rows + 1)], sem)

    def send_edges(src, first, last, dst, k, ssem, rsem, layer):
        @pl.when(h > 0)
        def _():
            remote(src.at[fr(k), pl.ds(first, 1)], dst.at[fr(k), pl.ds(5, 1)], ssem, rsem, (dp, layer, up))

        @pl.when(h < NB - 1)
        def _():
            remote(src.at[fr(k), pl.ds(last, 1)], dst.at[fr(k), pl.ds(0, 1)], ssem, rsem, (dp, layer, dn))

    def fr(k, first=0):
        return pl.ds(F * k + first, F)

    wcopy = pltpu.make_async_copy(kern.at[0], W, w_sem)
    wcopy.start()
    barrier = pltpu.get_barrier_semaphore()
    far = lax.rem(s + 2, LAYERS)

    @pl.when(s == LAYERS - 1)
    def _():
        @pl.when(h > 0)
        def _():
            pl.semaphore_signal(barrier, inc=1, device_id=(dp, far, up), device_id_type=MESH)

        @pl.when(h < NB - 1)
        def _():
            pl.semaphore_signal(barrier, inc=1, device_id=(dp, far, dn), device_id_type=MESH)

        pl.semaphore_signal(barrier, inc=1, device_id=(dp, far, h), device_id_type=MESH)

    for b in bands[:-1]:
        pl.semaphore_signal(barrier, inc=1, device_id=(dp, s, b), device_id_type=MESH)
    for p in (nxt, prv):
        pl.semaphore_signal(barrier, inc=1, device_id=(dp, p, h), device_id_type=MESH)
    pl.semaphore_signal(barrier, inc=1, device_id=(other, s, h), device_id_type=MESH)

    @pl.when(s <= 1)
    def _():
        for k in range(SPANS):
            pltpu.make_async_copy(video.at[0, fr(k)], XP.at[fr(k), pl.ds(1, R)], xpc.at[k]).start()

    @pl.when(s == LAYERS - 1)
    def _():
        for k in range(SPANS):
            pltpu.make_async_copy(ograd.at[0, fr(k)], UR.at[fr(k), pl.ds(1, R)], ur.at[k]).start()

    SS[:, 0:2] = jnp.zeros((2, 2, 6, W16, 3 * C), bf16)
    G[12:14] = jnp.zeros((2, 6, W16, 3 * C), bf16)
    GO[0:1] = gains[...]
    GO[1:2] = shifts[...]
    from_far = (h > 0).astype(jnp.int32) + (h < NB - 1).astype(jnp.int32) + 1
    pl.semaphore_wait(barrier, NB - 1 + 2 + 1 + jnp.where(s == 1, from_far, 0))
    for p in (nxt, prv):
        pl.semaphore_signal(ready, inc=1, device_id=(dp, p, h), device_id_type=MESH)

    @pl.when(s <= 1)
    def _():
        for k in range(SPANS):
            send_edges(video.at[0], 0, 3, XP, k, s_xr.at[k], xph.at[k], s)

    @pl.when(s == LAYERS - 1)
    def _():
        for k in reversed(range(SPANS)):
            send_edges(ograd.at[0], 0, 3, UR, k, s_og.at[k], ur.at[k], s)

    @pl.when(s < LAYERS - 1)
    def _():
        remote(GO, GP, s_gp, gps, (dp, nxt, h))

    @pl.when(s > 0)
    def _():
        await_bytes(GP, gps)

    row = lax.broadcasted_iota(jnp.int32, (1, 6, 1, 1), 1)
    valid = jnp.where(row == 0, (h > 0).astype(f32), jnp.where(row == 5, (h < NB - 1).astype(f32), 1.0))

    def normalized(conv, table_ref, k):
        mu, inv = combine(table_ref[k])
        own = (spread(table_ref[k, h]) - mu).reshape(1, 1, 1, C)
        above = (spread(table_ref[k, up]) - mu).reshape(1, 1, 1, C)
        below = (spread(table_ref[k, dn]) - mu).reshape(1, 1, 1, C)
        off = jnp.concatenate([above, own, own, own, own, below], axis=1)
        return (conv + off) * inv.reshape(1, 1, 1, C)

    gain4 = GO[0:1].reshape(1, 1, 1, C)
    shift4 = GO[1:2].reshape(1, 1, 1, C)

    def layer(k):
        await_bytes(XP.at[fr(k), pl.ds(1, R)], xpc.at[k])

        await_edges(XP, k, xph.at[k])

        @pl.when(s == 0)
        def _():
            x = jnp.where(valid > 0, XP[fr(k)].astype(f32), 0.0)
            XR[fr(k)] = x.astype(bf16)
            put_shifted(SS.at[0], 2 + F * k, x)

        @pl.when(s > 0)
        def _():
            await_bytes(STP.at[k], stp.at[k])
            await_edges(CP, k, cp.at[k], R)
            normed = normalized(CP[fr(k)].astype(f32), STP, k)
            pre = normed * GP[0:1].reshape(1, 1, 1, C) + GP[1:2].reshape(1, 1, 1, C)
            x = XP[fr(k)].astype(f32) + pre * sigmoid(pre)
            x16 = jnp.where(valid > 0, x, 0.0).astype(bf16)
            XR[fr(k)] = x16
            put_shifted(SS.at[0], 2 + F * k, x16.astype(f32))
            NP[k] = normed[:, 1:5].reshape(POS, C)

        @pl.when(k == 0)
        def _():
            wcopy.wait()

        acc = None
        for ab in range(9):
            a, b = divmod(ab, 3)
            lhs = SS[0, fr(k, a), b : b + R].reshape(POS, 3 * C)
            d = jnp.dot(lhs, W[ab * 768 : ab * 768 + 768, :], preferred_element_type=f32)
            acc = d if acc is None else acc + d
        mean = jnp.sum(acc, axis=0, keepdims=True) * (1.0 / POS)
        mean, STO[k, h] = summary(mean, jnp.sum((acc - mean) ** 2, axis=0, keepdims=True))
        cen = acc - mean

        @pl.when((s < LAYERS - 1) & (k == 0))
        def _():
            pl.semaphore_wait(ready, 2)

        @pl.when(s < LAYERS - 1)
        def _():
            for b in bands:
                remote(STO.at[k, h], STP.at[k, h], s_stn.at[k], stp.at[k], (dp, nxt, b))

        for b in bands[:-1]:
            remote(STO.at[k, h], STO.at[k, h], s_sto.at[k], sto.at[k], (dp, s, b))

        CF[fr(k), 1:5] = cen.reshape(F, R, W16, C)
        CO[fr(k)] = cen.astype(bf16).reshape(F, R, W16, C)

        @pl.when(s < LAYERS - 1)
        def _():
            send_edges(CO, 0, 3, CP, k, s_c.at[k], cp.at[k], nxt)
            remote(CO.at[fr(k)], CP.at[fr(k), pl.ds(1, R)], s_c.at[k], cp.at[k], (dp, nxt, h))

        send_edges(CF, 1, 4, CF, k, s_ch.at[k], cfh.at[k], s)
        remote(XR.at[fr(k)], PX.at[fr(k)], s_px.at[k], px.at[k], (other, s, h))

    def own_rows(k):
        await_bytes(STO.at[k, pl.ds(0, NB - 1)], sto.at[k])
        mu, inv = combine(STO[k])
        MI[k] = jnp.concatenate([mu, inv], axis=0)
        off = (spread(STO[k, h]) - mu).reshape(1, 1, 1, C)
        normed = (CF[fr(k), 1:5] + off) * inv.reshape(1, 1, 1, C)
        pre = normed * gain4 + shift4
        sig = sigmoid(pre)
        slope = sig * (1.0 + pre * (1.0 - sig))
        NO[fr(k), 1:5] = normed
        LO[fr(k), 1:5] = slope

        @pl.when(s <= 1)
        def _():
            XN[fr(k)] = (XR[fr(k), 1:5].astype(f32) + pre * sig).astype(bf16)

        @pl.when(s == 0)
        def _():
            remote(XN.at[fr(k)], RL.at[fr(k)], s_x.at[k], rl.at[k], (dp, prv, h))

        @pl.when(s == 1)
        def _():
            far = lax.rem(s + 2, LAYERS)
            send_edges(XN, 0, 3, XP, k, s_xn.at[k], xph.at[k], far)
            remote(XN.at[fr(k)], XP.at[fr(k), pl.ds(1, R)], s_x.at[k], xpc.at[k], (dp, far, h))

        @pl.when(s == LAYERS - 1)
        def _():
            await_edges(UR, k, ur.at[k], R)
            gpre = (UR[fr(k), 1:5].astype(f32) * slope).reshape(POS, C)
            nn = normed.reshape(POS, C)
            SB[k, h] = jnp.concatenate(
                [jnp.sum(gpre * nn, axis=0, keepdims=True), jnp.sum(gpre, axis=0, keepdims=True)], axis=0
            )
            for b in bands[:-1]:
                remote(SB.at[k, h], SB.at[k, h], s_sbo.at[k], sb.at[k], (dp, s, b))

    def own_halo(k):
        await_edges(CF, k, cfh.at[k])
        mu, inv = MI[k, 0:1], MI[k, 1:2]
        for r, b in ((0, up), (5, dn)):
            off = (spread(STO[k, b]) - mu).reshape(1, 1, 1, C)
            normed = (CF[fr(k), r : r + 1] + off) * inv.reshape(1, 1, 1, C)
            pre = normed * gain4 + shift4
            sig = sigmoid(pre)
            NO[fr(k), r : r + 1] = normed
            LO[fr(k), r : r + 1] = sig * (1.0 + pre * (1.0 - sig))

    @pl.when(s == LAYERS - 1)
    def _():
        pl.semaphore_wait(ready, 2)
        for k in range(SPANS):
            await_bytes(RL.at[fr(k)], rl.at[k])
            send_edges(RL, 0, 3, XP, k, s_rl.at[k], xph.at[k], prv)
            remote(RL.at[fr(k)], XP.at[fr(k), pl.ds(1, R)], s_rl.at[k], xpc.at[k], (dp, prv, h))

    def forward(k, carry):
        layer(k)
        return carry

    lax.fori_loop(0, SPANS, forward, 0)

    def own(k, carry):
        own_rows(k)
        return carry

    lax.fori_loop(0, SPANS, own, 0)

    def halo(i, carry):
        own_halo(SPANS - 1 - i)

        @pl.when(s > 0)
        def _():
            pre = NP[i] * GP[0:1] + GP[1:2]
            sig = sigmoid(pre)
            LP[i] = sig * (1.0 + pre * (1.0 - sig))

        return carry

    lax.fori_loop(0, SPANS, halo, 0)

    def partner(k, carry):
        await_bytes(PX.at[fr(k)], px.at[k])
        put_shifted(SS.at[1], 2 + F * k, PX[fr(k)].astype(f32))
        return carry

    lax.fori_loop(0, SPANS, partner, 0)
    WG[...] = jnp.zeros((HALF, C), f32)

    def add_rows(off, rows, lhs, side, k):
        WG[pl.ds(off, rows), :] += lax.dot_general(
            lhs, GG[side, k], (((0,), (0,)), ((), ())), preferred_element_type=f32
        )

    def part(q, side, k):
        ab = q + dp * (8 - 2 * q)
        a, b = lax.div(ab, 3), lax.rem(ab, 3)
        off = pl.multiple_of(ab * 768 - HALF * dp, 128)
        add_rows(off, 768, SS[side, fr(k, a), pl.ds(b, R)].reshape(POS, 3 * C), side, k)

    def middle(side, k):
        off = pl.multiple_of((HALF - 384) * (1 - dp), 128)
        full = SS[side, fr(k, 1), 1 : 1 + R].reshape(POS, 3 * C)
        add_rows(off, 384, jnp.where(dp == 0, full[:, 0:384], full[:, 384:768]), side, k)

    def weight_grad(side, k):
        for q in range(4):
            part(q, side, k)
        middle(side, k)

    TA, TB = 14, 13
    cuts = ((10, 0), (4, 10))

    def tiles(row, n):
        v = WG[pl.ds(pl.multiple_of(row, 8), 8 * n), :].reshape(n, 8, C)
        return jnp.concatenate([v[:, :, 0:128], v[:, :, 128:256]], axis=1)

    def rows(t):
        return jnp.concatenate([t[:, 0:8], t[:, 8:16]], axis=2).reshape(8 * t.shape[0], C)

    def first_phase(m):
        z = m + dp * (3 - 2 * m)
        for y in range(4):
            row = (4 * z + y) * SHARE
            A1S[z, y] = tiles(row, TA).astype(bf16)
            B1S[y, z] = tiles(row + 8 * TA, TB).astype(bf16)
        dz = lax.rem(z - zz + 4, 4)
        n, _ = cuts[0]

        @pl.when(dz != 0)
        def _():
            remote(
                A1S.at[z, :, pl.ds(0, n)], A1R.at[dz - 1, :, pl.ds(0, n)], s_a1.at[0], a1.at[0], (dp, s, 4 * z + yy)
            )

        for dy in range(1, 4):
            y = lax.rem(yy + dy, 4)
            remote(
                B1S.at[y, z, pl.ds(0, n)], B1R.at[dy - 1, z, pl.ds(0, n)], s_b1.at[0], b1.at[0], (dp, s, 4 * zz + y)
            )

    def first_phase_rest():
        n = cuts[0][0]
        for d in range(1, 4):
            z, y = lax.rem(zz + d, 4), lax.rem(yy + d, 4)
            rest = pl.ds(n, TA - n)
            remote(A1S.at[z, :, rest], A1R.at[d - 1, :, rest], s_a1.at[1], a1.at[1], (dp, s, 4 * z + yy))
            rest = pl.ds(n, TB - n)
            remote(B1S.at[y, :, rest], B1R.at[d - 1, :, rest], s_b1.at[1], b1.at[1], (dp, s, 4 * zz + y))

    def backward(i, norm_sum):
        k = SPANS - 1 - i

        @pl.when(s < LAYERS - 1)
        def _():
            await_bytes(SB.at[k], sb.at[k])
            await_edges(UR, k, ur.at[k], R)

        @pl.when(s == LAYERS - 1)
        def _():
            await_bytes(SB.at[k, pl.ds(0, NB - 1)], sb.at[k])

        sums = jnp.sum(SB[k], axis=0)
        norm_sum = norm_sum + sums
        gain = GO[0:1]
        means = group_sum(sums * gain) * (1.0 / GSIZE)
        m2, m1 = means[0:1], means[1:2]
        upstream = UR[fr(k)].astype(f32)
        gn = upstream * LO[fr(k)] * gain.reshape(1, 1, 1, C)
        nn = NO[fr(k)]
        inv = MI[k, 1:2]
        gc = (gn - m1.reshape(1, 1, 1, C) - nn * m2.reshape(1, 1, 1, C)) * inv.reshape(1, 1, 1, C)
        gc16 = jnp.where(valid > 0, gc, 0.0).astype(bf16)
        GG[0, k] = gc16[:, 1:5].reshape(POS, C)
        remote(GG.at[0, k], GG.at[1, k], s_pg.at[k], pg.at[k], (other, s, h))

        @pl.when(s > 0)
        def _():
            put_shifted(G, F * k, gc16.astype(f32))
            acc = None
            for ab in range(9):
                a, b = divmod(ab, 3)
                for c in range(3):
                    lhs = G[fr(k, a), b : b + R, :, C * c : C * c + C].reshape(POS, C)
                    t = 9 * (2 - a) + 3 * (2 - b) + 2 - c
                    d = lax.dot_general(
                        lhs, W[t * C : t * C + C, :], (((1,), (1,)), ((), ())), preferred_element_type=f32
                    )
                    acc = d if acc is None else acc + d
            u16 = (UR[fr(k), 1:5].astype(f32).reshape(POS, C) + acc).astype(bf16)
            gpre = u16.astype(f32) * LP[k]
            SBO[k] = jnp.concatenate(
                [jnp.sum(gpre * NP[k], axis=0, keepdims=True), jnp.sum(gpre, axis=0, keepdims=True)], axis=0
            )
            for b in bands:
                remote(SBO.at[k], SB.at[k, h], s_sb.at[k], sb.at[k], (dp, prv, b))
            UO[fr(k)] = u16.reshape(F, R, W16, C)
            send_edges(UO, 0, 3, UR, k, s_ur.at[k], ur.at[k], prv)
            remote(UO.at[fr(k)], UR.at[fr(k), pl.ds(1, R)], s_ur.at[k], ur.at[k], (dp, prv, h))

        @pl.when((s == 0) & ((dp == 1) | (k > 0)))
        def _():
            weight_grad(0, k)

        if i == 0:

            @pl.when((s == 0) & (dp == 0))
            def _():
                await_bytes(GG.at[1, 0], pg.at[0])
                weight_grad(1, 0)

        return norm_sum

    @pl.when((s == 0) & (dp == 0))
    def _():
        def term(i, carry):
            k = SPANS - 1 - i
            await_bytes(GG.at[1, k], pg.at[k])
            weight_grad(1, k)
            return carry

        lax.fori_loop(0, SPANS - 1, term, 0)

    norm_sum = jnp.zeros((2, C), f32)
    for i in range(SPANS):
        norm_sum = backward(i, norm_sum)
    NG[0] = norm_sum
    remote(NG.at[0], NG.at[1], s_ng, ngs, (other, s, h))

    @pl.when((s > 0) | (dp == 1))
    def _():
        await_bytes(GG.at[1, 2], pg.at[2])
        await_bytes(GG.at[1, 1], pg.at[1])

    @pl.when((s > 0) & (dp == 0))
    def _():
        await_bytes(GG.at[1, 0], pg.at[0])

    def term(t, carry):
        late = (t >= 2 + dp).astype(jnp.int32)
        weight_grad(late, SPANS - 1 - (t - late * (2 + dp)))
        return carry

    lax.fori_loop(jnp.where(s > 0, 0, jnp.where(dp == 1, 3, 5)), 5, term, 0)

    @pl.when(dp == 1)
    def _():
        await_bytes(GG.at[1, 0], pg.at[0])

    for q in range(4):
        part(q, dp, 0)
        if q > 0:
            first_phase(q - 1)
    middle(dp, 0)
    first_phase(3)
    first_phase_rest()

    await_bytes(NG.at[1], ngs)
    out_n[0] = NG[0] + NG[1]

    def total(r, *at):
        return sum(r[(j, *at)].astype(f32) for j in range(3))

    for i, (n, t0) in enumerate(cuts):
        span = pl.ds(t0, n)
        await_bytes(A1R.at[:, :, span], a1.at[i])
        for dy in range(1, 4):
            y = lax.rem(yy + dy, 4)
            A2S[dy - 1, span] = (tiles((4 * zz + y) * SHARE + 8 * t0, n) + total(A1R, y, span)).astype(bf16)
            remote(A2S.at[dy - 1, span], A2R.at[dy - 1, span], s_a2, a2, (dp, s, 4 * zz + y))
        n = min(n, TB - t0)
        span = pl.ds(t0, n)
        await_bytes(B1R.at[:, :, span], b1.at[i])
        for dz in range(1, 4):
            z = lax.rem(zz + dz, 4)
            row = (4 * z + yy) * SHARE + 8 * (TA + t0)
            B2S[dz - 1, span] = (tiles(row, n) + total(B1R, z, span)).astype(bf16)
            remote(B2S.at[dz - 1, span], B2R.at[dz - 1, span], s_b2, b2, (dp, s, 4 * z + yy))
    mine_a = tiles(h * SHARE, TA) + total(A1R, yy)
    mine_b = tiles(h * SHARE + 8 * TA, TB) + total(B1R, zz)
    await_bytes(A2R, a2)
    out_k[0, 0 : 8 * TA] = rows(mine_a + total(A2R))
    await_bytes(B2R, b2)
    out_k[0, 8 * TA : SHARE] = rows(mine_b + total(B2R))

    for k in range(SPANS):
        await_bytes(STO.at[k, pl.ds(0, NB - 1)], s_sto.at[k])
        await_edges(CF, k, s_ch.at[k])
        await_bytes(PX.at[fr(k)], s_px.at[k])
        await_bytes(GG.at[0, k], s_pg.at[k])

        @pl.when(s < LAYERS - 1)
        def _():
            await_bytes(STP.at[k], s_stn.at[k])
            await_edges(CP, k, s_c.at[k], R)

        @pl.when(s <= 1)
        def _():
            await_bytes(XN.at[fr(k)], s_x.at[k])

            await_edges(XP, k, s_xr.at[k])

        @pl.when(s == 1)
        def _():
            await_edges(XP, k, s_xn.at[k])

        @pl.when(s > 0)
        def _():
            await_edges(UR, k, s_ur.at[k], R)
            await_bytes(SB.at[k], s_sb.at[k])

        @pl.when(s == LAYERS - 1)
        def _():
            await_edges(XP, k, s_rl.at[k], R)
            await_edges(UR, k, s_og.at[k])
            await_bytes(SB.at[k, pl.ds(0, NB - 1)], s_sbo.at[k])

    @pl.when(s < LAYERS - 1)
    def _():
        await_bytes(GO, s_gp)

    await_bytes(NG.at[0], s_ng)
    for i, (n, t0) in enumerate(cuts):
        await_bytes(A1R.at[:, :, pl.ds(t0, n)], s_a1.at[i])
        await_bytes(B1R.at[:, :, pl.ds(t0, min(n, TB - t0))], s_b1.at[i])
    await_bytes(A2R, s_a2)
    await_bytes(B2R, s_b2)


def per_device(video, kernels, gains, shifts, out_grad):
    dma = pltpu.SemaphoreType.DMA
    six = (F * SPANS, 6, W16, C)
    four = (F * SPANS, R, W16, C)
    wide = (F * SPANS + 2, 6, W16, 3 * C)
    table = (SPANS, NB, 2, C)
    scratch = [
        pltpu.VMEM((27 * C, C), bf16),
        pltpu.VMEM(six, bf16),
        pltpu.VMEM(six, bf16),
        pltpu.VMEM(four, bf16),
        pltpu.VMEM(four, bf16),
        pltpu.VMEM(six, bf16),
        pltpu.VMEM(four, bf16),
        pltpu.VMEM(six, f32),
        pltpu.VMEM((2,) + wide, bf16),
        pltpu.VMEM(six, bf16),
        pltpu.VMEM(wide, bf16),
        pltpu.VMEM((2, SPANS, POS, C), bf16),
        pltpu.VMEM(six, bf16),
        pltpu.VMEM(four, bf16),
        pltpu.VMEM((SPANS, NB, 1, C), f32),
        pltpu.VMEM((SPANS, NB, 1, C), f32),
        pltpu.VMEM(table, f32),
        pltpu.VMEM((SPANS, 2, C), f32),
        pltpu.VMEM((2, C), f32),
        pltpu.VMEM((2, C), f32),
        pltpu.VMEM((SPANS, POS, C), f32),
        pltpu.VMEM((SPANS, POS, C), f32),
        pltpu.VMEM(six, f32),
        pltpu.VMEM(six, f32),
        pltpu.VMEM((SPANS, 2, C), f32),
        pltpu.VMEM((HALF, C), f32),
        pltpu.VMEM((4, 4, 14, 16, 128), bf16),
        pltpu.VMEM((3, 4, 14, 16, 128), bf16),
        pltpu.VMEM((4, 4, 13, 16, 128), bf16),
        pltpu.VMEM((3, 4, 13, 16, 128), bf16),
        pltpu.VMEM((3, 14, 16, 128), bf16),
        pltpu.VMEM((3, 14, 16, 128), bf16),
        pltpu.VMEM((3, 13, 16, 128), bf16),
        pltpu.VMEM((3, 13, 16, 128), bf16),
        pltpu.VMEM((2, 2, C), f32),
    ]
    k3 = dma((SPANS,))
    two = dma((2,))
    sems = [pltpu.SemaphoreType.REGULAR, dma] + [k3] * 11 + [two, two] + [dma] * 4
    sems += [k3] * 14 + [two, two] + [dma] * 4
    anyspec = pl.BlockSpec(memory_space=pl.ANY)
    vm = pl.BlockSpec(memory_space=pltpu.VMEM)
    return pl.pallas_call(
        kernel,
        out_shape=(
            pltpu.VMEM((1, SHARE, C), f32),
            pltpu.VMEM((1, 2, C), f32),
        ),
        in_specs=[anyspec, anyspec, vm, vm, anyspec],
        out_specs=(vm, vm),
        scratch_shapes=scratch + sems,
        compiler_params=pltpu.CompilerParams(
            collective_id=0, has_side_effects=True, vmem_limit_bytes=60 * 2**20
        ),
    )(video, kernels, gains, shifts, out_grad)


def solution(mesh):
    return jax.shard_map(
        per_device,
        mesh=mesh,
        in_specs=(
            P("dp", None, "height", None, None),
            P("pipe", None, None),
            P("pipe", None),
            P("pipe", None),
            P("dp", None, "height", None, None),
        ),
        out_specs=(P("pipe", ("dp", "height"), None), P("pipe", None, None)),
        check_vma=False,
    )
```

```python
import functools

import jax
import jax.numpy as jnp
from jax import lax
from jax.experimental import pallas as pl
from jax.experimental.pallas import tpu as pltpu
from jax.sharding import PartitionSpec as P

GROUPS = 32
F = 4
SPANS = 3
NB = 16
LAYERS = 4
R = 4
W16 = 16
C = 256
POS = F * R * W16
GSIZE = float(POS * NB * (C // GROUPS))
HALF = 3456
SHARE = 216
EPS = 1e-05
f32 = jnp.float32
bf16 = jnp.bfloat16
MESH = pl.DeviceIdType.MESH


def group_mate(x, d):
    lane = lax.broadcasted_iota(jnp.int32, x.shape, 1)
    return jnp.where((lane & d) != 0, pltpu.roll(x, d, 1), pltpu.roll(x, C - d, 1))


def group_sum(x):
    for d in (1, 2, 4):
        x = x + group_mate(x, d)
    return x


def even(x):
    return (lax.broadcasted_iota(jnp.int32, x.shape, 1) & 1) == 0


def spread(x):
    return jnp.where(even(x), x, pltpu.roll(x, 1, 1))


def summary(mean_c, dev_c):
    both = jnp.concatenate([mean_c, dev_c], axis=0)
    count = float(POS)
    for d in (1, 2, 4):
        mate = group_mate(both, d)
        gap = both[0:1] - mate[0:1]
        both = jnp.concatenate(
            [0.5 * (both[0:1] + mate[0:1]), both[1:2] + mate[1:2] + (0.5 * count) * gap * gap], axis=0
        )
        count = 2.0 * count
    return both[0:1], jnp.where(even(mean_c), both[0:1], both[1:2])


def gradient_summary(gpre, normed, gain):
    sums = jnp.concatenate(
        [jnp.sum(gpre * normed, axis=0, keepdims=True), jnp.sum(gpre, axis=0, keepdims=True)], axis=0
    )
    sums = group_sum(sums * gain)
    return jnp.where(even(gain), sums[0:1], sums[1:2])


def combine(table):
    sums = jnp.sum(table, axis=0)
    mean = sums * (1.0 / NB)
    between = jnp.sum((table - mean[None]) ** 2, axis=0)
    dev = pltpu.roll(sums, C - 1, 1) + (GSIZE / NB) * between
    both = spread(jnp.concatenate([mean, lax.rsqrt(dev * (1.0 / GSIZE) + EPS)], axis=0))
    return both[0:1], both[1:2]


def sigmoid(v):
    return 0.5 * jnp.tanh(0.5 * v) + 0.5


def put_shifted(dst, frame, x):
    n = x.shape[1]
    v = x.reshape(F * n, W16, C)
    col = lax.broadcasted_iota(jnp.int32, v.shape, 1)
    left = jnp.where(col == 0, 0.0, pltpu.roll(v, 1, 1))
    right = jnp.where(col == W16 - 1, 0.0, pltpu.roll(v, W16 - 1, 1))
    for c, part in enumerate((left, v, right)):
        dst[pl.ds(frame, F), :, :, C * c : C * c + C] = part.astype(bf16).reshape(F, n, W16, C)


def kernel(
    video, kern, gains, shifts, ograd, out_k, out_n,
    W, XP, XR, XN, RL, CP, CO, CF, SS, PX, G, GG, UR, UO, STP, STO, SB, SBO, GO, GP, NP, LP, NO, LO, MI,
    WG, A1S, A1R, B1S, B1R, A2S, A2R, B2S, B2R, NG, NT,
    ready, w_sem, xpc, xph, rl, cp, stp, sto, cfh, ur, sb, px, pg, a1, b1, a2, b2, ngs, gps, nt,
    s_x, s_xn, s_xr, s_rl, s_c, s_ch, s_sto, s_stn, s_px, s_pg, s_ur, s_og, s_sb, s_sbo, s_a1, s_b1, s_a2, s_b2, s_ng, s_gp, s_nt,
):
    dp, s, h = lax.axis_index("dp"), lax.axis_index("pipe"), lax.axis_index("height")
    nxt, prv = lax.rem(s + 1, LAYERS), lax.rem(s + LAYERS - 1, LAYERS)
    up, dn = lax.rem(h + NB - 1, NB), lax.rem(h + 1, NB)
    other = 1 - dp
    zz, yy = lax.div(h, 4), lax.rem(h, 4)
    steps = [(i, j) for i in range(4) for j in range(4)]
    steps.sort(key=lambda o: -(min(o[0], 4 - o[0]) + min(o[1], 4 - o[1])))
    bands = [lax.rem(zz + i, 4) * 4 + lax.rem(yy + j, 4) for i, j in steps]

    def remote(src, dst, ssem, rsem, dev):
        pltpu.make_async_remote_copy(
            src_ref=src, dst_ref=dst, send_sem=ssem, recv_sem=rsem, device_id=dev, device_id_type=MESH
        ).start()

    def await_bytes(ref, sem):
        pltpu.make_async_copy(ref, ref, sem).wait()

    inside = (h > 0) & (h < NB - 1)

    def await_edges(ref, k, sem, rows=0):
        @pl.when(inside)
        def _():
            await_bytes(ref.at[fr(k), pl.ds(0, rows + 2)], sem)

        @pl.when(jnp.logical_not(inside))
        def _():
            await_bytes(ref.at[fr(k), pl.ds(0, rows + 1)], sem)

    def send_edges(src, first, last, dst, k, ssem, rsem, layer):
        @pl.when(h > 0)
        def _():
            remote(src.at[fr(k), pl.ds(first, 1)], dst.at[fr(k), pl.ds(5, 1)], ssem, rsem, (dp, layer, up))

        @pl.when(h < NB - 1)
        def _():
            remote(src.at[fr(k), pl.ds(last, 1)], dst.at[fr(k), pl.ds(0, 1)], ssem, rsem, (dp, layer, dn))

    def fr(k, first=0):
        return pl.ds(F * k + first, F)

    wcopy = pltpu.make_async_copy(kern.at[0], W, w_sem)
    wcopy.start()
    barrier = pltpu.get_barrier_semaphore()
    far = lax.rem(s + 2, LAYERS)

    @pl.when(s == LAYERS - 1)
    def _():
        @pl.when(h > 0)
        def _():
            pl.semaphore_signal(barrier, inc=1, device_id=(dp, far, up), device_id_type=MESH)

        @pl.when(h < NB - 1)
        def _():
            pl.semaphore_signal(barrier, inc=1, device_id=(dp, far, dn), device_id_type=MESH)

        pl.semaphore_signal(barrier, inc=1, device_id=(dp, far, h), device_id_type=MESH)

    for b in bands[:-1]:
        pl.semaphore_signal(barrier, inc=1, device_id=(dp, s, b), device_id_type=MESH)
    for p in (nxt, prv):
        pl.semaphore_signal(barrier, inc=1, device_id=(dp, p, h), device_id_type=MESH)
    pl.semaphore_signal(barrier, inc=1, device_id=(other, s, h), device_id_type=MESH)

    @pl.when(s <= 1)
    def _():
        for k in range(SPANS):
            pltpu.make_async_copy(video.at[0, fr(k)], XP.at[fr(k), pl.ds(1, R)], xpc.at[k]).start()

    @pl.when(s == LAYERS - 1)
    def _():
        for k in range(SPANS):
            pltpu.make_async_copy(ograd.at[0, fr(k)], UR.at[fr(k), pl.ds(1, R)], ur.at[k]).start()

    SS[:, 0:2] = jnp.zeros((2, 2, 6, W16, 3 * C), bf16)
    G[12:14] = jnp.zeros((2, 6, W16, 3 * C), bf16)
    GO[0:1] = gains[...]
    GO[1:2] = shifts[...]
    from_far = (h > 0).astype(jnp.int32) + (h < NB - 1).astype(jnp.int32) + 1
    pl.semaphore_wait(barrier, NB - 1 + 2 + 1 + jnp.where(s == 1, from_far, 0))
    for p in (nxt, prv):
        pl.semaphore_signal(ready, inc=1, device_id=(dp, p, h), device_id_type=MESH)

    @pl.when(s <= 1)
    def _():
        for k in range(SPANS):
            send_edges(video.at[0], 0, 3, XP, k, s_xr.at[k], xph.at[k], s)

    @pl.when(s == LAYERS - 1)
    def _():
        for k in reversed(range(SPANS)):
            send_edges(ograd.at[0], 0, 3, UR, k, s_og.at[k], ur.at[k], s)

    @pl.when(s < LAYERS - 1)
    def _():
        remote(GO, GP, s_gp, gps, (dp, nxt, h))

    @pl.when(s > 0)
    def _():
        await_bytes(GP, gps)

    row = lax.broadcasted_iota(jnp.int32, (1, 6, 1, 1), 1)
    valid = jnp.where(row == 0, (h > 0).astype(f32), jnp.where(row == 5, (h < NB - 1).astype(f32), 1.0))

    def normalized(conv, table_ref, k):
        mu, inv = combine(table_ref[k])
        own = (spread(table_ref[k, h]) - mu).reshape(1, 1, 1, C)
        above = (spread(table_ref[k, up]) - mu).reshape(1, 1, 1, C)
        below = (spread(table_ref[k, dn]) - mu).reshape(1, 1, 1, C)
        off = jnp.concatenate([above, own, own, own, own, below], axis=1)
        return (conv + off) * inv.reshape(1, 1, 1, C)

    gain4 = GO[0:1].reshape(1, 1, 1, C)
    shift4 = GO[1:2].reshape(1, 1, 1, C)

    def layer(k):
        await_bytes(XP.at[fr(k), pl.ds(1, R)], xpc.at[k])

        await_edges(XP, k, xph.at[k])

        @pl.when(s == 0)
        def _():
            x = jnp.where(valid > 0, XP[fr(k)].astype(f32), 0.0)
            XR[fr(k)] = x.astype(bf16)
            put_shifted(SS.at[0], 2 + F * k, x)

        @pl.when(s > 0)
        def _():
            await_bytes(STP.at[k], stp.at[k])
            await_edges(CP, k, cp.at[k], R)
            normed = normalized(CP[fr(k)].astype(f32), STP, k)
            pre = normed * GP[0:1].reshape(1, 1, 1, C) + GP[1:2].reshape(1, 1, 1, C)
            x = XP[fr(k)].astype(f32) + pre * sigmoid(pre)
            x16 = jnp.where(valid > 0, x, 0.0).astype(bf16)
            XR[fr(k)] = x16
            put_shifted(SS.at[0], 2 + F * k, x16.astype(f32))
            NP[k] = normed[:, 1:5].reshape(POS, C)

        @pl.when(k == 0)
        def _():
            wcopy.wait()

        acc = None
        for ab in range(9):
            a, b = divmod(ab, 3)
            lhs = SS[0, fr(k, a), b : b + R].reshape(POS, 3 * C)
            d = jnp.dot(lhs, W[ab * 768 : ab * 768 + 768, :], preferred_element_type=f32)
            acc = d if acc is None else acc + d
        mean = jnp.sum(acc, axis=0, keepdims=True) * (1.0 / POS)
        mean, STO[k, h] = summary(mean, jnp.sum((acc - mean) ** 2, axis=0, keepdims=True))
        cen = acc - mean

        @pl.when((s < LAYERS - 1) & (k == 0))
        def _():
            pl.semaphore_wait(ready, 2)

        @pl.when(s < LAYERS - 1)
        def _():
            for b in bands:
                remote(STO.at[k, h], STP.at[k, h], s_stn.at[k], stp.at[k], (dp, nxt, b))

        for b in bands[:-1]:
            remote(STO.at[k, h], STO.at[k, h], s_sto.at[k], sto.at[k], (dp, s, b))

        CF[fr(k), 1:5] = cen.reshape(F, R, W16, C)
        CO[fr(k)] = cen.astype(bf16).reshape(F, R, W16, C)

        @pl.when(s < LAYERS - 1)
        def _():
            send_edges(CO, 0, 3, CP, k, s_c.at[k], cp.at[k], nxt)
            remote(CO.at[fr(k)], CP.at[fr(k), pl.ds(1, R)], s_c.at[k], cp.at[k], (dp, nxt, h))

        send_edges(CF, 1, 4, CF, k, s_ch.at[k], cfh.at[k], s)
        remote(XR.at[fr(k)], PX.at[fr(k)], s_px.at[k], px.at[k], (other, s, h))

    def own_rows(k):
        await_bytes(STO.at[k, pl.ds(0, NB - 1)], sto.at[k])
        mu, inv = combine(STO[k])
        MI[k] = jnp.concatenate([mu, inv], axis=0)
        off = (spread(STO[k, h]) - mu).reshape(1, 1, 1, C)
        normed = (CF[fr(k), 1:5] + off) * inv.reshape(1, 1, 1, C)
        pre = normed * gain4 + shift4
        sig = sigmoid(pre)
        slope = sig * (1.0 + pre * (1.0 - sig))
        NO[fr(k), 1:5] = normed
        LO[fr(k), 1:5] = slope

        @pl.when(s <= 1)
        def _():
            XN[fr(k)] = (XR[fr(k), 1:5].astype(f32) + pre * sig).astype(bf16)

        @pl.when(s == 0)
        def _():
            remote(XN.at[fr(k)], RL.at[fr(k)], s_x.at[k], rl.at[k], (dp, prv, h))

        @pl.when(s == 1)
        def _():
            far = lax.rem(s + 2, LAYERS)
            send_edges(XN, 0, 3, XP, k, s_xn.at[k], xph.at[k], far)
            remote(XN.at[fr(k)], XP.at[fr(k), pl.ds(1, R)], s_x.at[k], xpc.at[k], (dp, far, h))

        @pl.when(s == LAYERS - 1)
        def _():
            await_edges(UR, k, ur.at[k], R)
            gpre = (UR[fr(k), 1:5].astype(f32) * slope).reshape(POS, C)
            nn = normed.reshape(POS, C)
            SB[k, h] = gradient_summary(gpre, nn, GO[0:1])
            for b in bands[:-1]:
                remote(SB.at[k, h], SB.at[k, h], s_sbo.at[k], sb.at[k], (dp, s, b))

    def own_halo(k):
        await_edges(CF, k, cfh.at[k])
        mu, inv = MI[k, 0:1], MI[k, 1:2]
        for r, b in ((0, up), (5, dn)):
            off = (spread(STO[k, b]) - mu).reshape(1, 1, 1, C)
            normed = (CF[fr(k), r : r + 1] + off) * inv.reshape(1, 1, 1, C)
            pre = normed * gain4 + shift4
            sig = sigmoid(pre)
            NO[fr(k), r : r + 1] = normed
            LO[fr(k), r : r + 1] = sig * (1.0 + pre * (1.0 - sig))

    @pl.when(s == LAYERS - 1)
    def _():
        pl.semaphore_wait(ready, 2)
        for k in range(SPANS):
            await_bytes(RL.at[fr(k)], rl.at[k])
            send_edges(RL, 0, 3, XP, k, s_rl.at[k], xph.at[k], prv)
            remote(RL.at[fr(k)], XP.at[fr(k), pl.ds(1, R)], s_rl.at[k], xpc.at[k], (dp, prv, h))

    def forward(k, carry):
        layer(k)
        return carry

    lax.fori_loop(0, SPANS, forward, 0)

    def own(k, carry):
        own_rows(k)
        return carry

    lax.fori_loop(0, SPANS, own, 0)

    def halo(i, carry):
        own_halo(SPANS - 1 - i)

        @pl.when(s > 0)
        def _():
            pre = NP[i] * GP[0:1] + GP[1:2]
            sig = sigmoid(pre)
            LP[i] = sig * (1.0 + pre * (1.0 - sig))

        return carry

    lax.fori_loop(0, SPANS, halo, 0)

    def partner(k, carry):
        await_bytes(PX.at[fr(k)], px.at[k])
        put_shifted(SS.at[1], 2 + F * k, PX[fr(k)].astype(f32))
        return carry

    lax.fori_loop(0, SPANS, partner, 0)
    WG[...] = jnp.zeros((HALF, C), f32)

    def add_rows(off, rows, lhs, side, k):
        WG[pl.ds(off, rows), :] += lax.dot_general(
            lhs, GG[side, k], (((0,), (0,)), ((), ())), preferred_element_type=f32
        )

    def part(q, side, k):
        ab = q + dp * (8 - 2 * q)
        a, b = lax.div(ab, 3), lax.rem(ab, 3)
        off = pl.multiple_of(ab * 768 - HALF * dp, 128)
        add_rows(off, 768, SS[side, fr(k, a), pl.ds(b, R)].reshape(POS, 3 * C), side, k)

    def middle(side, k):
        off = pl.multiple_of((HALF - 384) * (1 - dp), 128)
        full = SS[side, fr(k, 1), 1 : 1 + R].reshape(POS, 3 * C)
        add_rows(off, 384, jnp.where(dp == 0, full[:, 0:384], full[:, 384:768]), side, k)

    def weight_grad(side, k):
        for q in range(4):
            part(q, side, k)
        middle(side, k)

    TA, TB = 14, 13
    cuts = ((10, 0), (4, 10))

    def tiles(row, n):
        v = WG[pl.ds(pl.multiple_of(row, 8), 8 * n), :].reshape(n, 8, C)
        return jnp.concatenate([v[:, :, 0:128], v[:, :, 128:256]], axis=1)

    def rows(t):
        return jnp.concatenate([t[:, 0:8], t[:, 8:16]], axis=2).reshape(8 * t.shape[0], C)

    def first_phase(m):
        z = m + dp * (3 - 2 * m)
        for y in range(4):
            row = (4 * z + y) * SHARE
            A1S[z, y] = tiles(row, TA).astype(bf16)
            B1S[y, z] = tiles(row + 8 * TA, TB).astype(bf16)
        dz = lax.rem(z - zz + 4, 4)
        n, _ = cuts[0]

        @pl.when(dz != 0)
        def _():
            remote(
                A1S.at[z, :, pl.ds(0, n)], A1R.at[dz - 1, :, pl.ds(0, n)], s_a1.at[0], a1.at[0], (dp, s, 4 * z + yy)
            )

        for dy in range(1, 4):
            y = lax.rem(yy + dy, 4)
            remote(
                B1S.at[y, z, pl.ds(0, n)], B1R.at[dy - 1, z, pl.ds(0, n)], s_b1.at[0], b1.at[0], (dp, s, 4 * zz + y)
            )

    def first_phase_rest():
        n = cuts[0][0]
        for d in range(1, 4):
            z, y = lax.rem(zz + d, 4), lax.rem(yy + d, 4)
            rest = pl.ds(n, TA - n)
            remote(A1S.at[z, :, rest], A1R.at[d - 1, :, rest], s_a1.at[1], a1.at[1], (dp, s, 4 * z + yy))
            rest = pl.ds(n, TB - n)
            remote(B1S.at[y, :, rest], B1R.at[d - 1, :, rest], s_b1.at[1], b1.at[1], (dp, s, 4 * zz + y))

    def backward(i):
        k = SPANS - 1 - i

        @pl.when(s < LAYERS - 1)
        def _():
            await_bytes(SB.at[k], sb.at[k])
            await_edges(UR, k, ur.at[k], R)

        @pl.when(s == LAYERS - 1)
        def _():
            await_bytes(SB.at[k, pl.ds(0, NB - 1)], sb.at[k])

        sums = jnp.sum(SB[k], axis=0)
        gain = GO[0:1]
        means = sums * (1.0 / GSIZE)
        m2, m1 = spread(means), jnp.where(even(means), pltpu.roll(means, C - 1, 1), means)
        upstream = UR[fr(k)].astype(f32)
        gn = upstream * LO[fr(k)] * gain.reshape(1, 1, 1, C)
        nn = NO[fr(k)]
        inv = MI[k, 1:2]
        gc = (gn - m1.reshape(1, 1, 1, C) - nn * m2.reshape(1, 1, 1, C)) * inv.reshape(1, 1, 1, C)
        gc16 = jnp.where(valid > 0, gc, 0.0).astype(bf16)
        GG[0, k] = gc16[:, 1:5].reshape(POS, C)
        remote(GG.at[0, k], GG.at[1, k], s_pg.at[k], pg.at[k], (other, s, h))

        @pl.when(s > 0)
        def _():
            put_shifted(G, F * k, gc16.astype(f32))
            acc = None
            for ab in range(9):
                a, b = divmod(ab, 3)
                for c in range(3):
                    lhs = G[fr(k, a), b : b + R, :, C * c : C * c + C].reshape(POS, C)
                    t = 9 * (2 - a) + 3 * (2 - b) + 2 - c
                    d = lax.dot_general(
                        lhs, W[t * C : t * C + C, :], (((1,), (1,)), ((), ())), preferred_element_type=f32
                    )
                    acc = d if acc is None else acc + d
            u16 = (UR[fr(k), 1:5].astype(f32).reshape(POS, C) + acc).astype(bf16)
            gpre = u16.astype(f32) * LP[k]
            SBO[k] = gradient_summary(gpre, NP[k], GP[0:1])
            for b in bands:
                remote(SBO.at[k], SB.at[k, h], s_sb.at[k], sb.at[k], (dp, prv, b))
            UO[fr(k)] = u16.reshape(F, R, W16, C)
            send_edges(UO, 0, 3, UR, k, s_ur.at[k], ur.at[k], prv)
            remote(UO.at[fr(k)], UR.at[fr(k), pl.ds(1, R)], s_ur.at[k], ur.at[k], (dp, prv, h))

        @pl.when((s == 0) & ((dp == 1) | (k > 0)))
        def _():
            weight_grad(0, k)

        if i == 0:

            @pl.when((s == 0) & (dp == 0))
            def _():
                await_bytes(GG.at[1, 0], pg.at[0])
                weight_grad(1, 0)

    @pl.when((s == 0) & (dp == 0))
    def _():
        def term(i, carry):
            k = SPANS - 1 - i
            await_bytes(GG.at[1, k], pg.at[k])
            weight_grad(1, k)
            return carry

        lax.fori_loop(0, SPANS - 1, term, 0)

    for i in range(SPANS):
        backward(i)

    @pl.when((s > 0) | (dp == 1))
    def _():
        await_bytes(GG.at[1, 2], pg.at[2])
        await_bytes(GG.at[1, 1], pg.at[1])

    @pl.when((s > 0) & (dp == 0))
    def _():
        await_bytes(GG.at[1, 0], pg.at[0])

    def term(t, carry):
        late = (t >= 2 + dp).astype(jnp.int32)
        weight_grad(late, SPANS - 1 - (t - late * (2 + dp)))
        return carry

    lax.fori_loop(jnp.where(s > 0, 0, jnp.where(dp == 1, 3, 5)), 5, term, 0)

    @pl.when(dp == 1)
    def _():
        await_bytes(GG.at[1, 0], pg.at[0])

    for q in range(4):
        part(q, dp, 0)
        if q > 0:
            first_phase(q - 1)
    middle(dp, 0)
    first_phase(3)
    first_phase_rest()

    def norm_terms(k, total):
        gpre = (UR[fr(k), 1:5].astype(f32) * LO[fr(k), 1:5]).reshape(POS, C)
        both = jnp.concatenate(
            [
                jnp.sum(gpre * NO[fr(k), 1:5].reshape(POS, C), axis=0, keepdims=True),
                jnp.sum(gpre, axis=0, keepdims=True),
            ],
            axis=0,
        )
        return total + both

    NT[h] = lax.fori_loop(0, SPANS, norm_terms, jnp.zeros((2, C), f32))
    for b in bands[:-1]:
        remote(NT.at[h], NT.at[h], s_nt, nt, (dp, s, b))

    def total(r, *at):
        return sum(r[(j, *at)].astype(f32) for j in range(3))

    for i, (n, t0) in enumerate(cuts):
        span = pl.ds(t0, n)
        await_bytes(A1R.at[:, :, span], a1.at[i])
        for dy in range(1, 4):
            y = lax.rem(yy + dy, 4)
            A2S[dy - 1, span] = (tiles((4 * zz + y) * SHARE + 8 * t0, n) + total(A1R, y, span)).astype(bf16)
            remote(A2S.at[dy - 1, span], A2R.at[dy - 1, span], s_a2, a2, (dp, s, 4 * zz + y))
        n = min(n, TB - t0)
        span = pl.ds(t0, n)
        await_bytes(B1R.at[:, :, span], b1.at[i])
        for dz in range(1, 4):
            z = lax.rem(zz + dz, 4)
            row = (4 * z + yy) * SHARE + 8 * (TA + t0)
            B2S[dz - 1, span] = (tiles(row, n) + total(B1R, z, span)).astype(bf16)
            remote(B2S.at[dz - 1, span], B2R.at[dz - 1, span], s_b2, b2, (dp, s, 4 * z + yy))
    await_bytes(NT.at[pl.ds(0, NB - 1)], nt)
    NG[0] = jnp.sum(NT[...], axis=0)
    remote(NG.at[0], NG.at[1], s_ng, ngs, (other, s, h))
    mine_a = tiles(h * SHARE, TA) + total(A1R, yy)
    mine_b = tiles(h * SHARE + 8 * TA, TB) + total(B1R, zz)
    await_bytes(A2R, a2)
    out_k[0, 0 : 8 * TA] = rows(mine_a + total(A2R))
    await_bytes(B2R, b2)
    out_k[0, 8 * TA : SHARE] = rows(mine_b + total(B2R))
    await_bytes(NG.at[1], ngs)
    out_n[0] = NG[0] + NG[1]

    for k in range(SPANS):
        await_bytes(STO.at[k, pl.ds(0, NB - 1)], s_sto.at[k])
        await_edges(CF, k, s_ch.at[k])
        await_bytes(PX.at[fr(k)], s_px.at[k])
        await_bytes(GG.at[0, k], s_pg.at[k])

        @pl.when(s < LAYERS - 1)
        def _():
            await_bytes(STP.at[k], s_stn.at[k])
            await_edges(CP, k, s_c.at[k], R)

        @pl.when(s <= 1)
        def _():
            await_bytes(XN.at[fr(k)], s_x.at[k])

            await_edges(XP, k, s_xr.at[k])

        @pl.when(s == 1)
        def _():
            await_edges(XP, k, s_xn.at[k])

        @pl.when(s > 0)
        def _():
            await_edges(UR, k, s_ur.at[k], R)
            await_bytes(SB.at[k], s_sb.at[k])

        @pl.when(s == LAYERS - 1)
        def _():
            await_edges(XP, k, s_rl.at[k], R)
            await_edges(UR, k, s_og.at[k])
            await_bytes(SB.at[k, pl.ds(0, NB - 1)], s_sbo.at[k])

    @pl.when(s < LAYERS - 1)
    def _():
        await_bytes(GO, s_gp)

    await_bytes(NG.at[0], s_ng)
    await_bytes(NT.at[pl.ds(0, NB - 1)], s_nt)
    for i, (n, t0) in enumerate(cuts):
        await_bytes(A1R.at[:, :, pl.ds(t0, n)], s_a1.at[i])
        await_bytes(B1R.at[:, :, pl.ds(t0, min(n, TB - t0))], s_b1.at[i])
    await_bytes(A2R, s_a2)
    await_bytes(B2R, s_b2)


def per_device(video, kernels, gains, shifts, out_grad):
    dma = pltpu.SemaphoreType.DMA
    six = (F * SPANS, 6, W16, C)
    four = (F * SPANS, R, W16, C)
    wide = (F * SPANS + 2, 6, W16, 3 * C)
    scratch = [
        pltpu.VMEM((27 * C, C), bf16),
        pltpu.VMEM(six, bf16),
        pltpu.VMEM(six, bf16),
        pltpu.VMEM(four, bf16),
        pltpu.VMEM(four, bf16),
        pltpu.VMEM(six, bf16),
        pltpu.VMEM(four, bf16),
        pltpu.VMEM(six, f32),
        pltpu.VMEM((2,) + wide, bf16),
        pltpu.VMEM(six, bf16),
        pltpu.VMEM(wide, bf16),
        pltpu.VMEM((2, SPANS, POS, C), bf16),
        pltpu.VMEM(six, bf16),
        pltpu.VMEM(four, bf16),
        pltpu.VMEM((SPANS, NB, 1, C), f32),
        pltpu.VMEM((SPANS, NB, 1, C), f32),
        pltpu.VMEM((SPANS, NB, 1, C), f32),
        pltpu.VMEM((SPANS, 1, C), f32),
        pltpu.VMEM((2, C), f32),
        pltpu.VMEM((2, C), f32),
        pltpu.VMEM((SPANS, POS, C), f32),
        pltpu.VMEM((SPANS, POS, C), f32),
        pltpu.VMEM(six, f32),
        pltpu.VMEM(six, f32),
        pltpu.VMEM((SPANS, 2, C), f32),
        pltpu.VMEM((HALF, C), f32),
        pltpu.VMEM((4, 4, 14, 16, 128), bf16),
        pltpu.VMEM((3, 4, 14, 16, 128), bf16),
        pltpu.VMEM((4, 4, 13, 16, 128), bf16),
        pltpu.VMEM((3, 4, 13, 16, 128), bf16),
        pltpu.VMEM((3, 14, 16, 128), bf16),
        pltpu.VMEM((3, 14, 16, 128), bf16),
        pltpu.VMEM((3, 13, 16, 128), bf16),
        pltpu.VMEM((3, 13, 16, 128), bf16),
        pltpu.VMEM((2, 2, C), f32),
        pltpu.VMEM((NB, 2, C), f32),
    ]
    k3 = dma((SPANS,))
    two = dma((2,))
    sems = [pltpu.SemaphoreType.REGULAR, dma] + [k3] * 11 + [two, two] + [dma] * 5
    sems += [k3] * 14 + [two, two] + [dma] * 5
    anyspec = pl.BlockSpec(memory_space=pl.ANY)
    vm = pl.BlockSpec(memory_space=pltpu.VMEM)
    return pl.pallas_call(
        kernel,
        out_shape=(
            pltpu.VMEM((1, SHARE, C), f32),
            pltpu.VMEM((1, 2, C), f32),
        ),
        in_specs=[anyspec, anyspec, vm, vm, anyspec],
        out_specs=(vm, vm),
        scratch_shapes=scratch + sems,
        compiler_params=pltpu.CompilerParams(
            collective_id=0, has_side_effects=True, vmem_limit_bytes=60 * 2**20
        ),
    )(video, kernels, gains, shifts, out_grad)


def solution(mesh):
    return jax.shard_map(
        per_device,
        mesh=mesh,
        in_specs=(
            P("dp", None, "height", None, None),
            P("pipe", None, None),
            P("pipe", None),
            P("pipe", None),
            P("dp", None, "height", None, None),
        ),
        out_specs=(P("pipe", ("dp", "height"), None), P("pipe", None, None)),
        check_vma=False,
    )
```

```python
import functools

import jax
import jax.numpy as jnp
from jax import lax
from jax.experimental import pallas as pl
from jax.experimental.pallas import tpu as pltpu
from jax.sharding import PartitionSpec as P

GROUPS = 32
F = 4
SPANS = 3
NB = 16
LAYERS = 4
R = 4
W16 = 16
C = 256
POS = F * R * W16
GSIZE = float(POS * NB * (C // GROUPS))
HALF = 3456
SHARE = 216
EPS = 1e-05
f32 = jnp.float32
bf16 = jnp.bfloat16
MESH = pl.DeviceIdType.MESH


def group_mate(x, d):
    lane = lax.broadcasted_iota(jnp.int32, x.shape, 1)
    return jnp.where((lane & d) != 0, pltpu.roll(x, d, 1), pltpu.roll(x, C - d, 1))


def group_sum(x):
    for d in (1, 2, 4):
        x = x + group_mate(x, d)
    return x


def even(x):
    return (lax.broadcasted_iota(jnp.int32, x.shape, 1) & 1) == 0


def spread(x):
    return jnp.where(even(x), x, pltpu.roll(x, 1, 1))


def summary(mean_c, dev_c):
    both = jnp.concatenate([mean_c, dev_c], axis=0)
    count = float(POS)
    for d in (1, 2, 4):
        mate = group_mate(both, d)
        gap = both[0:1] - mate[0:1]
        both = jnp.concatenate(
            [0.5 * (both[0:1] + mate[0:1]), both[1:2] + mate[1:2] + (0.5 * count) * gap * gap], axis=0
        )
        count = 2.0 * count
    return both[0:1], jnp.where(even(mean_c), both[0:1], both[1:2])


def gradient_summary(gpre, normed, gain):
    sums = jnp.concatenate(
        [jnp.sum(gpre * normed, axis=0, keepdims=True), jnp.sum(gpre, axis=0, keepdims=True)], axis=0
    )
    sums = group_sum(sums * gain)
    return jnp.where(even(gain), sums[0:1], sums[1:2])


def combine(table):
    sums = jnp.sum(table, axis=0)
    mean = sums * (1.0 / NB)
    between = jnp.sum((table - mean[None]) ** 2, axis=0)
    dev = pltpu.roll(sums, C - 1, 1) + (GSIZE / NB) * between
    both = spread(jnp.concatenate([mean, lax.rsqrt(dev * (1.0 / GSIZE) + EPS)], axis=0))
    return both[0:1], both[1:2]


def sigmoid(v):
    return 0.5 * jnp.tanh(0.5 * v) + 0.5


def put_shifted(dst, frame, x):
    n = x.shape[1]
    v = x.reshape(F * n, W16, C)
    col = lax.broadcasted_iota(jnp.int32, v.shape, 1)
    left = jnp.where(col == 0, 0.0, pltpu.roll(v, 1, 1))
    right = jnp.where(col == W16 - 1, 0.0, pltpu.roll(v, W16 - 1, 1))
    for c, part in enumerate((left, v, right)):
        dst[pl.ds(frame, F), :, :, C * c : C * c + C] = part.astype(bf16).reshape(F, n, W16, C)


def kernel(
    video, kern, gains, shifts, ograd, out_k, out_n,
    W, XP, XR, XN, RL, CP, CO, CF, SS, PX, G, GG, UR, UO, STP, STO, SB, SBO, GO, GP, NP, LP, NO, LO, MI,
    WG, A1S, A1R, B1S, B1R, A2S, A2R, B2S, B2R, NG, NT,
    ready, w_sem, xpc, xph, rl, cp, stp, sto, cfh, ur, sb, px, pg, a1, b1, a2, b2, ngs, gps, nt,
    s_x, s_xn, s_xr, s_rl, s_c, s_ch, s_sto, s_stn, s_px, s_pg, s_ur, s_og, s_sb, s_sbo, s_a1, s_b1, s_a2, s_b2, s_ng, s_gp, s_nt,
):
    dp, s, h = lax.axis_index("dp"), lax.axis_index("pipe"), lax.axis_index("height")
    nxt, prv = lax.rem(s + 1, LAYERS), lax.rem(s + LAYERS - 1, LAYERS)
    up, dn = lax.rem(h + NB - 1, NB), lax.rem(h + 1, NB)
    other = 1 - dp
    zz, yy = lax.div(h, 4), lax.rem(h, 4)
    steps = [(i, j) for i in range(4) for j in range(4)]
    steps.sort(key=lambda o: -(min(o[0], 4 - o[0]) + min(o[1], 4 - o[1])))
    bands = [lax.rem(zz + i, 4) * 4 + lax.rem(yy + j, 4) for i, j in steps]

    def remote(src, dst, ssem, rsem, dev):
        pltpu.make_async_remote_copy(
            src_ref=src, dst_ref=dst, send_sem=ssem, recv_sem=rsem, device_id=dev, device_id_type=MESH
        ).start()

    def await_bytes(ref, sem):
        pltpu.make_async_copy(ref, ref, sem).wait()

    inside = (h > 0) & (h < NB - 1)

    def await_edges(ref, k, sem, rows=0):
        @pl.when(inside)
        def _():
            await_bytes(ref.at[fr(k), pl.ds(0, rows + 2)], sem)

        @pl.when(jnp.logical_not(inside))
        def _():
            await_bytes(ref.at[fr(k), pl.ds(0, rows + 1)], sem)

    def send_edges(src, first, last, dst, k, ssem, rsem, layer):
        @pl.when(h > 0)
        def _():
            remote(src.at[fr(k), pl.ds(first, 1)], dst.at[fr(k), pl.ds(5, 1)], ssem, rsem, (dp, layer, up))

        @pl.when(h < NB - 1)
        def _():
            remote(src.at[fr(k), pl.ds(last, 1)], dst.at[fr(k), pl.ds(0, 1)], ssem, rsem, (dp, layer, dn))

    def fr(k, first=0):
        return pl.ds(F * k + first, F)

    wcopy = pltpu.make_async_copy(kern.at[0], W, w_sem)
    wcopy.start()
    barrier = pltpu.get_barrier_semaphore()
    far = lax.rem(s + 2, LAYERS)

    @pl.when(s == LAYERS - 1)
    def _():
        @pl.when(h > 0)
        def _():
            pl.semaphore_signal(barrier, inc=1, device_id=(dp, far, up), device_id_type=MESH)

        @pl.when(h < NB - 1)
        def _():
            pl.semaphore_signal(barrier, inc=1, device_id=(dp, far, dn), device_id_type=MESH)

        pl.semaphore_signal(barrier, inc=1, device_id=(dp, far, h), device_id_type=MESH)

    for b in bands[:-1]:
        pl.semaphore_signal(barrier, inc=1, device_id=(dp, s, b), device_id_type=MESH)
    for p in (nxt, prv):
        pl.semaphore_signal(barrier, inc=1, device_id=(dp, p, h), device_id_type=MESH)
    pl.semaphore_signal(barrier, inc=1, device_id=(other, s, h), device_id_type=MESH)

    @pl.when(s <= 1)
    def _():
        for k in range(SPANS):
            pltpu.make_async_copy(video.at[0, fr(k)], XP.at[fr(k), pl.ds(1, R)], xpc.at[k]).start()

    @pl.when(s == LAYERS - 1)
    def _():
        for k in range(SPANS):
            pltpu.make_async_copy(ograd.at[0, fr(k)], UR.at[fr(k), pl.ds(1, R)], ur.at[k]).start()

    SS[:, 0:2] = jnp.zeros((2, 2, 6, W16, 3 * C), bf16)
    G[12:14] = jnp.zeros((2, 6, W16, 3 * C), bf16)
    GO[0:1] = gains[...]
    GO[1:2] = shifts[...]
    from_far = (h > 0).astype(jnp.int32) + (h < NB - 1).astype(jnp.int32) + 1
    pl.semaphore_wait(barrier, NB - 1 + 2 + 1 + jnp.where(s == 1, from_far, 0))
    for p in (nxt, prv):
        pl.semaphore_signal(ready, inc=1, device_id=(dp, p, h), device_id_type=MESH)

    @pl.when(s <= 1)
    def _():
        for k in range(SPANS):
            send_edges(video.at[0], 0, 3, XP, k, s_xr.at[k], xph.at[k], s)

    @pl.when(s == LAYERS - 1)
    def _():
        for k in reversed(range(SPANS)):
            send_edges(ograd.at[0], 0, 3, UR, k, s_og.at[k], ur.at[k], s)

    @pl.when(s < LAYERS - 1)
    def _():
        remote(GO, GP, s_gp, gps, (dp, nxt, h))

    @pl.when(s > 0)
    def _():
        await_bytes(GP, gps)

    row = lax.broadcasted_iota(jnp.int32, (1, 6, 1, 1), 1)
    valid = jnp.where(row == 0, (h > 0).astype(f32), jnp.where(row == 5, (h < NB - 1).astype(f32), 1.0))

    def normalized(conv, table_ref, k):
        mu, inv = combine(table_ref[k])
        own = (spread(table_ref[k, h]) - mu).reshape(1, 1, 1, C)
        above = (spread(table_ref[k, up]) - mu).reshape(1, 1, 1, C)
        below = (spread(table_ref[k, dn]) - mu).reshape(1, 1, 1, C)
        off = jnp.concatenate([above, own, own, own, own, below], axis=1)
        return (conv + off) * inv.reshape(1, 1, 1, C)

    gain4 = GO[0:1].reshape(1, 1, 1, C)
    shift4 = GO[1:2].reshape(1, 1, 1, C)

    def layer(k):
        await_bytes(XP.at[fr(k), pl.ds(1, R)], xpc.at[k])

        await_edges(XP, k, xph.at[k])

        @pl.when(s == 0)
        def _():
            x = jnp.where(valid > 0, XP[fr(k)].astype(f32), 0.0)
            XR[fr(k)] = x.astype(bf16)
            put_shifted(SS.at[0], 2 + F * k, x)

        @pl.when(s > 0)
        def _():
            await_bytes(STP.at[k], stp.at[k])
            await_edges(CP, k, cp.at[k], R)
            normed = normalized(CP[fr(k)].astype(f32), STP, k)
            pre = normed * GP[0:1].reshape(1, 1, 1, C) + GP[1:2].reshape(1, 1, 1, C)
            x = XP[fr(k)].astype(f32) + pre * sigmoid(pre)
            x16 = jnp.where(valid > 0, x, 0.0).astype(bf16)
            XR[fr(k)] = x16
            put_shifted(SS.at[0], 2 + F * k, x16.astype(f32))
            NP[k] = normed[:, 1:5].reshape(POS, C)

        @pl.when(k == 0)
        def _():
            wcopy.wait()

        acc = None
        for ab in range(9):
            a, b = divmod(ab, 3)
            lhs = SS[0, fr(k, a), b : b + R].reshape(POS, 3 * C)
            d = jnp.dot(lhs, W[ab * 768 : ab * 768 + 768, :], preferred_element_type=f32)
            acc = d if acc is None else acc + d
        mean = jnp.sum(acc, axis=0, keepdims=True) * (1.0 / POS)
        mean, STO[k, h] = summary(mean, jnp.sum((acc - mean) ** 2, axis=0, keepdims=True))
        cen = acc - mean

        @pl.when((s < LAYERS - 1) & (k == 0))
        def _():
            pl.semaphore_wait(ready, 2)

        @pl.when(s < LAYERS - 1)
        def _():
            for b in bands:
                remote(STO.at[k, h], STP.at[k, h], s_stn.at[k], stp.at[k], (dp, nxt, b))

        for b in bands[:-1]:
            remote(STO.at[k, h], STO.at[k, h], s_sto.at[k], sto.at[k], (dp, s, b))

        CF[fr(k), 1:5] = cen.reshape(F, R, W16, C)
        CO[fr(k)] = cen.astype(bf16).reshape(F, R, W16, C)

        @pl.when(s < LAYERS - 1)
        def _():
            send_edges(CO, 0, 3, CP, k, s_c.at[k], cp.at[k], nxt)
            remote(CO.at[fr(k)], CP.at[fr(k), pl.ds(1, R)], s_c.at[k], cp.at[k], (dp, nxt, h))

        send_edges(CF, 1, 4, CF, k, s_ch.at[k], cfh.at[k], s)
        remote(XR.at[fr(k)], PX.at[fr(k)], s_px.at[k], px.at[k], (other, s, h))

    def own_rows(k):
        await_bytes(STO.at[k, pl.ds(0, NB - 1)], sto.at[k])
        mu, inv = combine(STO[k])
        MI[k] = jnp.concatenate([mu, inv], axis=0)
        off = (spread(STO[k, h]) - mu).reshape(1, 1, 1, C)
        normed = (CF[fr(k), 1:5] + off) * inv.reshape(1, 1, 1, C)
        pre = normed * gain4 + shift4
        sig = sigmoid(pre)
        slope = sig * (1.0 + pre * (1.0 - sig))
        NO[fr(k), 1:5] = normed
        LO[fr(k), 1:5] = slope

        @pl.when(s <= 1)
        def _():
            XN[fr(k)] = (XR[fr(k), 1:5].astype(f32) + pre * sig).astype(bf16)

        @pl.when(s == 0)
        def _():
            remote(XN.at[fr(k)], RL.at[fr(k)], s_x.at[k], rl.at[k], (dp, prv, h))

        @pl.when(s == 1)
        def _():
            far = lax.rem(s + 2, LAYERS)
            send_edges(XN, 0, 3, XP, k, s_xn.at[k], xph.at[k], far)
            remote(XN.at[fr(k)], XP.at[fr(k), pl.ds(1, R)], s_x.at[k], xpc.at[k], (dp, far, h))

        @pl.when(s == LAYERS - 1)
        def _():
            await_edges(UR, k, ur.at[k], R)
            gpre = (UR[fr(k), 1:5].astype(f32) * slope).reshape(POS, C)
            nn = normed.reshape(POS, C)
            SB[k, h] = gradient_summary(gpre, nn, GO[0:1])
            for b in bands[:-1]:
                remote(SB.at[k, h], SB.at[k, h], s_sbo.at[k], sb.at[k], (dp, s, b))

    def own_halo(k):
        await_edges(CF, k, cfh.at[k])
        mu, inv = MI[k, 0:1], MI[k, 1:2]
        for r, b in ((0, up), (5, dn)):
            off = (spread(STO[k, b]) - mu).reshape(1, 1, 1, C)
            normed = (CF[fr(k), r : r + 1] + off) * inv.reshape(1, 1, 1, C)
            pre = normed * gain4 + shift4
            sig = sigmoid(pre)
            NO[fr(k), r : r + 1] = normed
            LO[fr(k), r : r + 1] = sig * (1.0 + pre * (1.0 - sig))

    @pl.when(s == LAYERS - 1)
    def _():
        pl.semaphore_wait(ready, 2)
        for k in range(SPANS):
            await_bytes(RL.at[fr(k)], rl.at[k])
            send_edges(RL, 0, 3, XP, k, s_rl.at[k], xph.at[k], prv)
            remote(RL.at[fr(k)], XP.at[fr(k), pl.ds(1, R)], s_rl.at[k], xpc.at[k], (dp, prv, h))

    def forward(k, carry):
        layer(k)
        return carry

    lax.fori_loop(0, SPANS, forward, 0)

    def own(k, carry):
        own_rows(k)
        return carry

    lax.fori_loop(0, SPANS, own, 0)

    def halo(i, carry):
        own_halo(SPANS - 1 - i)

        @pl.when(s > 0)
        def _():
            pre = NP[i] * GP[0:1] + GP[1:2]
            sig = sigmoid(pre)
            LP[i] = sig * (1.0 + pre * (1.0 - sig))

        return carry

    lax.fori_loop(0, SPANS, halo, 0)

    def partner(k, carry):
        await_bytes(PX.at[fr(k)], px.at[k])
        put_shifted(SS.at[1], 2 + F * k, PX[fr(k)].astype(f32))
        return carry

    lax.fori_loop(0, SPANS, partner, 0)
    WG[...] = jnp.zeros((HALF, C), f32)

    def add_rows(off, rows, lhs, side, k):
        WG[pl.ds(off, rows), :] += lax.dot_general(
            lhs, GG[side, k], (((0,), (0,)), ((), ())), preferred_element_type=f32
        )

    def part(q, side, k):
        ab = q + dp * (8 - 2 * q)
        a, b = lax.div(ab, 3), lax.rem(ab, 3)
        off = pl.multiple_of(ab * 768 - HALF * dp, 128)
        add_rows(off, 768, SS[side, fr(k, a), pl.ds(b, R)].reshape(POS, 3 * C), side, k)

    def middle(side, k):
        off = pl.multiple_of((HALF - 384) * (1 - dp), 128)
        full = SS[side, fr(k, 1), 1 : 1 + R].reshape(POS, 3 * C)
        add_rows(off, 384, jnp.where(dp == 0, full[:, 0:384], full[:, 384:768]), side, k)

    def weight_grad(side, k):
        for q in range(4):
            part(q, side, k)
        middle(side, k)

    TA, TB = 14, 13
    cuts = ((12, 0), (2, 12))

    def tiles(row, n):
        v = WG[pl.ds(pl.multiple_of(row, 8), 8 * n), :].reshape(n, 8, C)
        return jnp.concatenate([v[:, :, 0:128], v[:, :, 128:256]], axis=1)

    def rows(t):
        return jnp.concatenate([t[:, 0:8], t[:, 8:16]], axis=2).reshape(8 * t.shape[0], C)

    def first_phase(m):
        z = m + dp * (3 - 2 * m)
        for y in range(4):
            row = (4 * z + y) * SHARE
            A1S[z, y] = tiles(row, TA).astype(bf16)
            B1S[y, z] = tiles(row + 8 * TA, TB).astype(bf16)
        dz = lax.rem(z - zz + 4, 4)
        n, _ = cuts[0]

        @pl.when(dz != 0)
        def _():
            remote(
                A1S.at[z, :, pl.ds(0, n)], A1R.at[dz - 1, :, pl.ds(0, n)], s_a1.at[0], a1.at[0], (dp, s, 4 * z + yy)
            )

        for dy in range(1, 4):
            y = lax.rem(yy + dy, 4)
            remote(
                B1S.at[y, z, pl.ds(0, n)], B1R.at[dy - 1, z, pl.ds(0, n)], s_b1.at[0], b1.at[0], (dp, s, 4 * zz + y)
            )

    def first_phase_rest():
        n = cuts[0][0]
        for d in range(1, 4):
            z, y = lax.rem(zz + d, 4), lax.rem(yy + d, 4)
            rest = pl.ds(n, TA - n)
            remote(A1S.at[z, :, rest], A1R.at[d - 1, :, rest], s_a1.at[1], a1.at[1], (dp, s, 4 * z + yy))
            rest = pl.ds(n, TB - n)
            remote(B1S.at[y, :, rest], B1R.at[d - 1, :, rest], s_b1.at[1], b1.at[1], (dp, s, 4 * zz + y))

    def backward(i):
        k = SPANS - 1 - i

        @pl.when(s < LAYERS - 1)
        def _():
            await_bytes(SB.at[k], sb.at[k])
            await_edges(UR, k, ur.at[k], R)

        @pl.when(s == LAYERS - 1)
        def _():
            await_bytes(SB.at[k, pl.ds(0, NB - 1)], sb.at[k])

        sums = jnp.sum(SB[k], axis=0)
        gain = GO[0:1]
        means = sums * (1.0 / GSIZE)
        m2, m1 = spread(means), jnp.where(even(means), pltpu.roll(means, C - 1, 1), means)
        upstream = UR[fr(k)].astype(f32)
        gn = upstream * LO[fr(k)] * gain.reshape(1, 1, 1, C)
        nn = NO[fr(k)]
        inv = MI[k, 1:2]
        gc = (gn - m1.reshape(1, 1, 1, C) - nn * m2.reshape(1, 1, 1, C)) * inv.reshape(1, 1, 1, C)
        gc16 = jnp.where(valid > 0, gc, 0.0).astype(bf16)
        GG[0, k] = gc16[:, 1:5].reshape(POS, C)
        remote(GG.at[0, k], GG.at[1, k], s_pg.at[k], pg.at[k], (other, s, h))

        @pl.when(s > 0)
        def _():
            put_shifted(G, F * k, gc16.astype(f32))
            acc = None
            for ab in range(9):
                a, b = divmod(ab, 3)
                for c in range(3):
                    lhs = G[fr(k, a), b : b + R, :, C * c : C * c + C].reshape(POS, C)
                    t = 9 * (2 - a) + 3 * (2 - b) + 2 - c
                    d = lax.dot_general(
                        lhs, W[t * C : t * C + C, :], (((1,), (1,)), ((), ())), preferred_element_type=f32
                    )
                    acc = d if acc is None else acc + d
            u16 = (UR[fr(k), 1:5].astype(f32).reshape(POS, C) + acc).astype(bf16)
            gpre = u16.astype(f32) * LP[k]
            SBO[k] = gradient_summary(gpre, NP[k], GP[0:1])
            for b in bands:
                remote(SBO.at[k], SB.at[k, h], s_sb.at[k], sb.at[k], (dp, prv, b))
            UO[fr(k)] = u16.reshape(F, R, W16, C)
            send_edges(UO, 0, 3, UR, k, s_ur.at[k], ur.at[k], prv)
            remote(UO.at[fr(k)], UR.at[fr(k), pl.ds(1, R)], s_ur.at[k], ur.at[k], (dp, prv, h))

        @pl.when((s == 0) & ((dp == 1) | (k > 0)))
        def _():
            weight_grad(0, k)

        if i == 0:

            @pl.when((s == 0) & (dp == 0))
            def _():
                await_bytes(GG.at[1, 0], pg.at[0])
                weight_grad(1, 0)

    @pl.when((s == 0) & (dp == 0))
    def _():
        def term(i, carry):
            k = SPANS - 1 - i
            await_bytes(GG.at[1, k], pg.at[k])
            weight_grad(1, k)
            return carry

        lax.fori_loop(0, SPANS - 1, term, 0)

    for i in range(SPANS):
        backward(i)

    @pl.when((s > 0) | (dp == 1))
    def _():
        await_bytes(GG.at[1, 2], pg.at[2])
        await_bytes(GG.at[1, 1], pg.at[1])

    @pl.when((s > 0) & (dp == 0))
    def _():
        await_bytes(GG.at[1, 0], pg.at[0])

    def term(t, carry):
        late = (t >= 2 + dp).astype(jnp.int32)
        weight_grad(late, SPANS - 1 - (t - late * (2 + dp)))
        return carry

    lax.fori_loop(jnp.where(s > 0, 0, jnp.where(dp == 1, 3, 5)), 5, term, 0)

    @pl.when(dp == 1)
    def _():
        await_bytes(GG.at[1, 0], pg.at[0])

    for q in range(4):
        part(q, dp, 0)
        if q > 0:
            first_phase(q - 1)
    middle(dp, 0)
    first_phase(3)
    first_phase_rest()

    def norm_terms(k, total):
        gpre = (UR[fr(k), 1:5].astype(f32) * LO[fr(k), 1:5]).reshape(POS, C)
        both = jnp.concatenate(
            [
                jnp.sum(gpre * NO[fr(k), 1:5].reshape(POS, C), axis=0, keepdims=True),
                jnp.sum(gpre, axis=0, keepdims=True),
            ],
            axis=0,
        )
        return total + both

    NT[h] = lax.fori_loop(0, SPANS, norm_terms, jnp.zeros((2, C), f32))
    for b in bands[:-1]:
        remote(NT.at[h], NT.at[h], s_nt, nt, (dp, s, b))

    def total(r, *at):
        return sum(r[(j, *at)].astype(f32) for j in range(3))

    for i, (n, t0) in enumerate(cuts):
        span = pl.ds(t0, n)
        await_bytes(A1R.at[:, :, span], a1.at[i])
        for dy in range(1, 4):
            y = lax.rem(yy + dy, 4)
            A2S[dy - 1, span] = (tiles((4 * zz + y) * SHARE + 8 * t0, n) + total(A1R, y, span)).astype(bf16)
            remote(A2S.at[dy - 1, span], A2R.at[dy - 1, span], s_a2, a2, (dp, s, 4 * zz + y))
        n = min(n, TB - t0)
        span = pl.ds(t0, n)
        await_bytes(B1R.at[:, :, span], b1.at[i])
        for dz in range(1, 4):
            z = lax.rem(zz + dz, 4)
            row = (4 * z + yy) * SHARE + 8 * (TA + t0)
            B2S[dz - 1, span] = (tiles(row, n) + total(B1R, z, span)).astype(bf16)
            remote(B2S.at[dz - 1, span], B2R.at[dz - 1, span], s_b2, b2, (dp, s, 4 * z + yy))
    await_bytes(NT.at[pl.ds(0, NB - 1)], nt)
    NG[0] = jnp.sum(NT[...], axis=0)
    remote(NG.at[0], NG.at[1], s_ng, ngs, (other, s, h))
    mine_a = tiles(h * SHARE, TA) + total(A1R, yy)
    mine_b = tiles(h * SHARE + 8 * TA, TB) + total(B1R, zz)
    await_bytes(A2R, a2)
    out_k[0, 0 : 8 * TA] = rows(mine_a + total(A2R))
    await_bytes(B2R, b2)
    out_k[0, 8 * TA : SHARE] = rows(mine_b + total(B2R))
    await_bytes(NG.at[1], ngs)
    out_n[0] = NG[0] + NG[1]

    for k in range(SPANS):
        await_bytes(STO.at[k, pl.ds(0, NB - 1)], s_sto.at[k])
        await_edges(CF, k, s_ch.at[k])
        await_bytes(PX.at[fr(k)], s_px.at[k])
        await_bytes(GG.at[0, k], s_pg.at[k])

        @pl.when(s < LAYERS - 1)
        def _():
            await_bytes(STP.at[k], s_stn.at[k])
            await_edges(CP, k, s_c.at[k], R)

        @pl.when(s <= 1)
        def _():
            await_bytes(XN.at[fr(k)], s_x.at[k])

            await_edges(XP, k, s_xr.at[k])

        @pl.when(s == 1)
        def _():
            await_edges(XP, k, s_xn.at[k])

        @pl.when(s > 0)
        def _():
            await_edges(UR, k, s_ur.at[k], R)
            await_bytes(SB.at[k], s_sb.at[k])

        @pl.when(s == LAYERS - 1)
        def _():
            await_edges(XP, k, s_rl.at[k], R)
            await_edges(UR, k, s_og.at[k])
            await_bytes(SB.at[k, pl.ds(0, NB - 1)], s_sbo.at[k])

    @pl.when(s < LAYERS - 1)
    def _():
        await_bytes(GO, s_gp)

    await_bytes(NG.at[0], s_ng)
    await_bytes(NT.at[pl.ds(0, NB - 1)], s_nt)
    for i, (n, t0) in enumerate(cuts):
        await_bytes(A1R.at[:, :, pl.ds(t0, n)], s_a1.at[i])
        await_bytes(B1R.at[:, :, pl.ds(t0, min(n, TB - t0))], s_b1.at[i])
    await_bytes(A2R, s_a2)
    await_bytes(B2R, s_b2)


def per_device(video, kernels, gains, shifts, out_grad):
    dma = pltpu.SemaphoreType.DMA
    six = (F * SPANS, 6, W16, C)
    four = (F * SPANS, R, W16, C)
    wide = (F * SPANS + 2, 6, W16, 3 * C)
    scratch = [
        pltpu.VMEM((27 * C, C), bf16),
        pltpu.VMEM(six, bf16),
        pltpu.VMEM(six, bf16),
        pltpu.VMEM(four, bf16),
        pltpu.VMEM(four, bf16),
        pltpu.VMEM(six, bf16),
        pltpu.VMEM(four, bf16),
        pltpu.VMEM(six, f32),
        pltpu.VMEM((2,) + wide, bf16),
        pltpu.VMEM(six, bf16),
        pltpu.VMEM(wide, bf16),
        pltpu.VMEM((2, SPANS, POS, C), bf16),
        pltpu.VMEM(six, bf16),
        pltpu.VMEM(four, bf16),
        pltpu.VMEM((SPANS, NB, 1, C), f32),
        pltpu.VMEM((SPANS, NB, 1, C), f32),
        pltpu.VMEM((SPANS, NB, 1, C), f32),
        pltpu.VMEM((SPANS, 1, C), f32),
        pltpu.VMEM((2, C), f32),
        pltpu.VMEM((2, C), f32),
        pltpu.VMEM((SPANS, POS, C), f32),
        pltpu.VMEM((SPANS, POS, C), f32),
        pltpu.VMEM(six, f32),
        pltpu.VMEM(six, f32),
        pltpu.VMEM((SPANS, 2, C), f32),
        pltpu.VMEM((HALF, C), f32),
        pltpu.VMEM((4, 4, 14, 16, 128), bf16),
        pltpu.VMEM((3, 4, 14, 16, 128), bf16),
        pltpu.VMEM((4, 4, 13, 16, 128), bf16),
        pltpu.VMEM((3, 4, 13, 16, 128), bf16),
        pltpu.VMEM((3, 14, 16, 128), bf16),
        pltpu.VMEM((3, 14, 16, 128), bf16),
        pltpu.VMEM((3, 13, 16, 128), bf16),
        pltpu.VMEM((3, 13, 16, 128), bf16),
        pltpu.VMEM((2, 2, C), f32),
        pltpu.VMEM((NB, 2, C), f32),
    ]
    k3 = dma((SPANS,))
    two = dma((2,))
    sems = [pltpu.SemaphoreType.REGULAR, dma] + [k3] * 11 + [two, two] + [dma] * 5
    sems += [k3] * 14 + [two, two] + [dma] * 5
    anyspec = pl.BlockSpec(memory_space=pl.ANY)
    vm = pl.BlockSpec(memory_space=pltpu.VMEM)
    return pl.pallas_call(
        kernel,
        out_shape=(
            pltpu.VMEM((1, SHARE, C), f32),
            pltpu.VMEM((1, 2, C), f32),
        ),
        in_specs=[anyspec, anyspec, vm, vm, anyspec],
        out_specs=(vm, vm),
        scratch_shapes=scratch + sems,
        compiler_params=pltpu.CompilerParams(
            collective_id=0, has_side_effects=True, vmem_limit_bytes=60 * 2**20
        ),
    )(video, kernels, gains, shifts, out_grad)


def solution(mesh):
    return jax.shard_map(
        per_device,
        mesh=mesh,
        in_specs=(
            P("dp", None, "height", None, None),
            P("pipe", None, None),
            P("pipe", None),
            P("pipe", None),
            P("dp", None, "height", None, None),
        ),
        out_specs=(P("pipe", ("dp", "height"), None), P("pipe", None, None)),
        check_vma=False,
    )
```

```python
import functools

import jax
import jax.numpy as jnp
from jax import lax
from jax.experimental import pallas as pl
from jax.experimental.pallas import tpu as pltpu
from jax.sharding import PartitionSpec as P

GROUPS = 32
F = 4
SPANS = 3
NB = 16
LAYERS = 4
R = 4
W16 = 16
C = 256
POS = F * R * W16
GSIZE = float(POS * NB * (C // GROUPS))
HALF = 3456
SHARE = 216
EPS = 1e-05
f32 = jnp.float32
bf16 = jnp.bfloat16
MESH = pl.DeviceIdType.MESH


def group_mate(x, d):
    lane = lax.broadcasted_iota(jnp.int32, x.shape, 1)
    return jnp.where((lane & d) != 0, pltpu.roll(x, d, 1), pltpu.roll(x, C - d, 1))


def group_sum(x):
    for d in (1, 2, 4):
        x = x + group_mate(x, d)
    return x


def even(x):
    return (lax.broadcasted_iota(jnp.int32, x.shape, 1) & 1) == 0


def spread(x):
    return jnp.where(even(x), x, pltpu.roll(x, 1, 1))


def summary(mean_c, dev_c):
    both = jnp.concatenate([mean_c, dev_c], axis=0)
    count = float(POS)
    for d in (1, 2, 4):
        mate = group_mate(both, d)
        gap = both[0:1] - mate[0:1]
        both = jnp.concatenate(
            [0.5 * (both[0:1] + mate[0:1]), both[1:2] + mate[1:2] + (0.5 * count) * gap * gap], axis=0
        )
        count = 2.0 * count
    return both[0:1], jnp.where(even(mean_c), both[0:1], both[1:2])


def gradient_summary(gpre, normed, gain):
    sums = jnp.concatenate(
        [jnp.sum(gpre * normed, axis=0, keepdims=True), jnp.sum(gpre, axis=0, keepdims=True)], axis=0
    )
    sums = group_sum(sums * gain)
    return jnp.where(even(gain), sums[0:1], sums[1:2])


def combine(table):
    sums = jnp.sum(table, axis=0)
    mean = sums * (1.0 / NB)
    between = jnp.sum((table - mean[None]) ** 2, axis=0)
    dev = pltpu.roll(sums, C - 1, 1) + (GSIZE / NB) * between
    both = spread(jnp.concatenate([mean, lax.rsqrt(dev * (1.0 / GSIZE) + EPS)], axis=0))
    return both[0:1], both[1:2]


def sigmoid(v):
    return 0.5 * jnp.tanh(0.5 * v) + 0.5


def put_shifted(dst, frame, x):
    n = x.shape[1]
    v = x.reshape(F * n, W16, C)
    col = lax.broadcasted_iota(jnp.int32, v.shape, 1)
    left = jnp.where(col == 0, 0.0, pltpu.roll(v, 1, 1))
    right = jnp.where(col == W16 - 1, 0.0, pltpu.roll(v, W16 - 1, 1))
    for c, part in enumerate((left, v, right)):
        dst[pl.ds(frame, F), :, :, C * c : C * c + C] = part.astype(bf16).reshape(F, n, W16, C)


def kernel(
    video, kern, gains, shifts, ograd, out_k, out_n,
    W, XP, XR, XN, RL, CP, CO, CF, SS, PX, G, GG, UR, UO, STP, STO, SB, SBO, GO, GP, NP, LP, NO, LO, MI,
    WG, A1S, A1R, B1S, B1R, A2S, A2R, B2S, B2R, NG, NT,
    ready, w_sem, xpc, xph, rl, cp, stp, sto, cfh, ur, sb, px, pg, a1, b1, a2, b2, ngs, gps, nt,
    s_x, s_xn, s_xr, s_rl, s_c, s_ch, s_sto, s_stn, s_px, s_pg, s_ur, s_og, s_sb, s_sbo, s_a1, s_b1, s_a2, s_b2, s_ng, s_gp, s_nt,
):
    dp, s, h = lax.axis_index("dp"), lax.axis_index("pipe"), lax.axis_index("height")
    nxt, prv = lax.rem(s + 1, LAYERS), lax.rem(s + LAYERS - 1, LAYERS)
    up, dn = lax.rem(h + NB - 1, NB), lax.rem(h + 1, NB)
    other = 1 - dp
    zz, yy = lax.div(h, 4), lax.rem(h, 4)
    steps = [(i, j) for i in range(4) for j in range(4)]
    steps.sort(key=lambda o: -(min(o[0], 4 - o[0]) + min(o[1], 4 - o[1])))
    bands = [lax.rem(zz + i, 4) * 4 + lax.rem(yy + j, 4) for i, j in steps]

    def remote(src, dst, ssem, rsem, dev):
        pltpu.make_async_remote_copy(
            src_ref=src, dst_ref=dst, send_sem=ssem, recv_sem=rsem, device_id=dev, device_id_type=MESH
        ).start()

    def await_bytes(ref, sem):
        pltpu.make_async_copy(ref, ref, sem).wait()

    inside = (h > 0) & (h < NB - 1)

    def await_edges(ref, k, sem, rows=0):
        @pl.when(inside)
        def _():
            await_bytes(ref.at[fr(k), pl.ds(0, rows + 2)], sem)

        @pl.when(jnp.logical_not(inside))
        def _():
            await_bytes(ref.at[fr(k), pl.ds(0, rows + 1)], sem)

    def send_edges(src, first, last, dst, k, ssem, rsem, layer):
        @pl.when(h > 0)
        def _():
            remote(src.at[fr(k), pl.ds(first, 1)], dst.at[fr(k), pl.ds(5, 1)], ssem, rsem, (dp, layer, up))

        @pl.when(h < NB - 1)
        def _():
            remote(src.at[fr(k), pl.ds(last, 1)], dst.at[fr(k), pl.ds(0, 1)], ssem, rsem, (dp, layer, dn))

    def fr(k, first=0):
        return pl.ds(F * k + first, F)

    wcopy = pltpu.make_async_copy(kern.at[0], W, w_sem)
    wcopy.start()
    barrier = pltpu.get_barrier_semaphore()
    far = lax.rem(s + 2, LAYERS)

    @pl.when(s == LAYERS - 1)
    def _():
        @pl.when(h > 0)
        def _():
            pl.semaphore_signal(barrier, inc=1, device_id=(dp, far, up), device_id_type=MESH)

        @pl.when(h < NB - 1)
        def _():
            pl.semaphore_signal(barrier, inc=1, device_id=(dp, far, dn), device_id_type=MESH)

        pl.semaphore_signal(barrier, inc=1, device_id=(dp, far, h), device_id_type=MESH)

    for b in bands[:-1]:
        pl.semaphore_signal(barrier, inc=1, device_id=(dp, s, b), device_id_type=MESH)
    for p in (nxt, prv):
        pl.semaphore_signal(barrier, inc=1, device_id=(dp, p, h), device_id_type=MESH)
    pl.semaphore_signal(barrier, inc=1, device_id=(other, s, h), device_id_type=MESH)

    @pl.when(s <= 1)
    def _():
        for k in range(SPANS):
            pltpu.make_async_copy(video.at[0, fr(k)], XP.at[fr(k), pl.ds(1, R)], xpc.at[k]).start()

    @pl.when(s == LAYERS - 1)
    def _():
        for k in range(SPANS):
            pltpu.make_async_copy(ograd.at[0, fr(k)], UR.at[fr(k), pl.ds(1, R)], ur.at[k]).start()

    SS[:, 0:2] = jnp.zeros((2, 2, 6, W16, 3 * C), bf16)
    G[12:14] = jnp.zeros((2, 6, W16, 3 * C), bf16)
    GO[0:1] = gains[...]
    GO[1:2] = shifts[...]
    from_far = (h > 0).astype(jnp.int32) + (h < NB - 1).astype(jnp.int32) + 1
    pl.semaphore_wait(barrier, NB - 1 + 2 + 1 + jnp.where(s == 1, from_far, 0))
    for p in (nxt, prv):
        pl.semaphore_signal(ready, inc=1, device_id=(dp, p, h), device_id_type=MESH)

    @pl.when(s <= 1)
    def _():
        for k in range(SPANS):
            send_edges(video.at[0], 0, 3, XP, k, s_xr.at[k], xph.at[k], s)

    @pl.when(s == LAYERS - 1)
    def _():
        for k in reversed(range(SPANS)):
            send_edges(ograd.at[0], 0, 3, UR, k, s_og.at[k], ur.at[k], s)

    @pl.when(s < LAYERS - 1)
    def _():
        remote(GO, GP, s_gp, gps, (dp, nxt, h))

    @pl.when(s > 0)
    def _():
        await_bytes(GP, gps)

    row = lax.broadcasted_iota(jnp.int32, (1, 6, 1, 1), 1)
    valid = jnp.where(row == 0, (h > 0).astype(f32), jnp.where(row == 5, (h < NB - 1).astype(f32), 1.0))

    def normalized(conv, table_ref, k):
        mu, inv = combine(table_ref[k])
        own = (spread(table_ref[k, h]) - mu).reshape(1, 1, 1, C)
        above = (spread(table_ref[k, up]) - mu).reshape(1, 1, 1, C)
        below = (spread(table_ref[k, dn]) - mu).reshape(1, 1, 1, C)
        off = jnp.concatenate([above, own, own, own, own, below], axis=1)
        return (conv + off) * inv.reshape(1, 1, 1, C)

    gain4 = GO[0:1].reshape(1, 1, 1, C)
    shift4 = GO[1:2].reshape(1, 1, 1, C)

    def layer(k):
        await_bytes(XP.at[fr(k), pl.ds(1, R)], xpc.at[k])

        await_edges(XP, k, xph.at[k])

        @pl.when(s == 0)
        def _():
            x = jnp.where(valid > 0, XP[fr(k)].astype(f32), 0.0)
            XR[fr(k)] = x.astype(bf16)
            put_shifted(SS.at[0], 2 + F * k, x)

        @pl.when(s > 0)
        def _():
            await_bytes(STP.at[k], stp.at[k])
            await_edges(CP, k, cp.at[k], R)
            normed = normalized(CP[fr(k)].astype(f32), STP, k)
            pre = normed * GP[0:1].reshape(1, 1, 1, C) + GP[1:2].reshape(1, 1, 1, C)
            x = XP[fr(k)].astype(f32) + pre * sigmoid(pre)
            x16 = jnp.where(valid > 0, x, 0.0).astype(bf16)
            XR[fr(k)] = x16
            put_shifted(SS.at[0], 2 + F * k, x16.astype(f32))
            NP[k] = normed[:, 1:5].reshape(POS, C)

        @pl.when(k == 0)
        def _():
            wcopy.wait()

        acc = None
        for ab in range(9):
            a, b = divmod(ab, 3)
            lhs = SS[0, fr(k, a), b : b + R].reshape(POS, 3 * C)
            d = jnp.dot(lhs, W[ab * 768 : ab * 768 + 768, :], preferred_element_type=f32)
            acc = d if acc is None else acc + d
        mean = jnp.sum(acc, axis=0, keepdims=True) * (1.0 / POS)
        mean, STO[k, h] = summary(mean, jnp.sum((acc - mean) ** 2, axis=0, keepdims=True))
        cen = acc - mean

        @pl.when((s < LAYERS - 1) & (k == 0))
        def _():
            pl.semaphore_wait(ready, 2)

        @pl.when(s < LAYERS - 1)
        def _():
            for b in bands:
                remote(STO.at[k, h], STP.at[k, h], s_stn.at[k], stp.at[k], (dp, nxt, b))

        for b in bands[:-1]:
            remote(STO.at[k, h], STO.at[k, h], s_sto.at[k], sto.at[k], (dp, s, b))

        CF[fr(k), 1:5] = cen.reshape(F, R, W16, C)
        CO[fr(k)] = cen.astype(bf16).reshape(F, R, W16, C)

        @pl.when(s < LAYERS - 1)
        def _():
            send_edges(CO, 0, 3, CP, k, s_c.at[k], cp.at[k], nxt)
            remote(CO.at[fr(k)], CP.at[fr(k), pl.ds(1, R)], s_c.at[k], cp.at[k], (dp, nxt, h))

        send_edges(CF, 1, 4, CF, k, s_ch.at[k], cfh.at[k], s)
        remote(XR.at[fr(k)], PX.at[fr(k)], s_px.at[k], px.at[k], (other, s, h))

    def own_rows(k):
        await_bytes(STO.at[k, pl.ds(0, NB - 1)], sto.at[k])
        mu, inv = combine(STO[k])
        MI[k] = jnp.concatenate([mu, inv], axis=0)
        off = (spread(STO[k, h]) - mu).reshape(1, 1, 1, C)
        normed = (CF[fr(k), 1:5] + off) * inv.reshape(1, 1, 1, C)
        pre = normed * gain4 + shift4
        sig = sigmoid(pre)
        slope = sig * (1.0 + pre * (1.0 - sig))
        NO[fr(k), 1:5] = normed
        LO[fr(k), 1:5] = slope

        @pl.when(s <= 1)
        def _():
            XN[fr(k)] = (XR[fr(k), 1:5].astype(f32) + pre * sig).astype(bf16)

        @pl.when(s == 0)
        def _():
            remote(XN.at[fr(k)], RL.at[fr(k)], s_x.at[k], rl.at[k], (dp, prv, h))

        @pl.when(s == 1)
        def _():
            far = lax.rem(s + 2, LAYERS)
            send_edges(XN, 0, 3, XP, k, s_xn.at[k], xph.at[k], far)
            remote(XN.at[fr(k)], XP.at[fr(k), pl.ds(1, R)], s_x.at[k], xpc.at[k], (dp, far, h))

        @pl.when(s == LAYERS - 1)
        def _():
            await_edges(UR, k, ur.at[k], R)
            gpre = (UR[fr(k), 1:5].astype(f32) * slope).reshape(POS, C)
            nn = normed.reshape(POS, C)
            SB[k, h] = gradient_summary(gpre, nn, GO[0:1])
            for b in bands[:-1]:
                remote(SB.at[k, h], SB.at[k, h], s_sbo.at[k], sb.at[k], (dp, s, b))

    def own_halo(k):
        await_edges(CF, k, cfh.at[k])
        mu, inv = MI[k, 0:1], MI[k, 1:2]
        for r, b in ((0, up), (5, dn)):
            off = (spread(STO[k, b]) - mu).reshape(1, 1, 1, C)
            normed = (CF[fr(k), r : r + 1] + off) * inv.reshape(1, 1, 1, C)
            pre = normed * gain4 + shift4
            sig = sigmoid(pre)
            NO[fr(k), r : r + 1] = normed
            LO[fr(k), r : r + 1] = sig * (1.0 + pre * (1.0 - sig))

    @pl.when(s == LAYERS - 1)
    def _():
        pl.semaphore_wait(ready, 2)
        for k in range(SPANS):
            await_bytes(RL.at[fr(k)], rl.at[k])
            send_edges(RL, 0, 3, XP, k, s_rl.at[k], xph.at[k], prv)
            remote(RL.at[fr(k)], XP.at[fr(k), pl.ds(1, R)], s_rl.at[k], xpc.at[k], (dp, prv, h))

    def forward(k, carry):
        layer(k)
        return carry

    lax.fori_loop(0, SPANS, forward, 0)

    def own(k, carry):
        own_rows(k)
        return carry

    lax.fori_loop(0, SPANS, own, 0)

    def halo(i, carry):
        own_halo(SPANS - 1 - i)

        @pl.when(s > 0)
        def _():
            pre = NP[i] * GP[0:1] + GP[1:2]
            sig = sigmoid(pre)
            LP[i] = sig * (1.0 + pre * (1.0 - sig))

        return carry

    lax.fori_loop(0, SPANS, halo, 0)

    def partner(k, carry):
        await_bytes(PX.at[fr(k)], px.at[k])
        put_shifted(SS.at[1], 2 + F * k, PX[fr(k)].astype(f32))
        return carry

    lax.fori_loop(0, SPANS, partner, 0)
    WG[...] = jnp.zeros((HALF, C), f32)

    def add_rows(off, rows, lhs, side, k):
        WG[pl.ds(off, rows), :] += lax.dot_general(
            lhs, GG[side, k], (((0,), (0,)), ((), ())), preferred_element_type=f32
        )

    def part(q, side, k):
        ab = q + dp * (8 - 2 * q)
        a, b = lax.div(ab, 3), lax.rem(ab, 3)
        off = pl.multiple_of(ab * 768 - HALF * dp, 128)
        add_rows(off, 768, SS[side, fr(k, a), pl.ds(b, R)].reshape(POS, 3 * C), side, k)

    def middle(side, k):
        off = pl.multiple_of((HALF - 384) * (1 - dp), 128)
        full = SS[side, fr(k, 1), 1 : 1 + R].reshape(POS, 3 * C)
        add_rows(off, 384, jnp.where(dp == 0, full[:, 0:384], full[:, 384:768]), side, k)

    def weight_grad(side, k):
        for q in range(4):
            part(q, side, k)
        middle(side, k)

    TA, TB = 14, 13
    cuts = ((12, 0), (2, 12))

    def tiles(row, n):
        v = WG[pl.ds(pl.multiple_of(row, 8), 8 * n), :].reshape(n, 8, C)
        return jnp.concatenate([v[:, :, 0:128], v[:, :, 128:256]], axis=1)

    def rows(t):
        return jnp.concatenate([t[:, 0:8], t[:, 8:16]], axis=2).reshape(8 * t.shape[0], C)

    def first_phase(m):
        z = m + dp * (3 - 2 * m)
        for y in range(4):
            row = (4 * z + y) * SHARE
            A1S[z, y] = tiles(row, TA).astype(bf16)
            B1S[y, z] = tiles(row + 8 * TA, TB).astype(bf16)
        dz = lax.rem(z - zz + 4, 4)
        n, _ = cuts[0]

        @pl.when(dz != 0)
        def _():
            remote(
                A1S.at[z, :, pl.ds(0, n)], A1R.at[dz - 1, :, pl.ds(0, n)], s_a1.at[0], a1.at[0], (dp, s, 4 * z + yy)
            )

        for dy in range(1, 4):
            y = lax.rem(yy + dy, 4)
            remote(
                B1S.at[y, z, pl.ds(0, n)], B1R.at[dy - 1, z, pl.ds(0, n)], s_b1.at[0], b1.at[0], (dp, s, 4 * zz + y)
            )

    def first_phase_rest():
        n = cuts[0][0]
        for d in range(1, 4):
            z, y = lax.rem(zz + d, 4), lax.rem(yy + d, 4)
            rest = pl.ds(n, TA - n)
            remote(A1S.at[z, :, rest], A1R.at[d - 1, :, rest], s_a1.at[1], a1.at[1], (dp, s, 4 * z + yy))
            rest = pl.ds(n, TB - n)
            remote(B1S.at[y, :, rest], B1R.at[d - 1, :, rest], s_b1.at[1], b1.at[1], (dp, s, 4 * zz + y))

    def backward(i):
        k = SPANS - 1 - i

        @pl.when(s < LAYERS - 1)
        def _():
            await_bytes(SB.at[k], sb.at[k])

        @pl.when((s > 0) & (s < LAYERS - 1))
        def _():
            await_edges(UR, k, ur.at[k], R)

        @pl.when(s == 0)
        def _():
            await_bytes(UR.at[fr(k), pl.ds(1, R)], ur.at[k])

        @pl.when(s == LAYERS - 1)
        def _():
            await_bytes(SB.at[k, pl.ds(0, NB - 1)], sb.at[k])

        sums = jnp.sum(SB[k], axis=0)
        gain = GO[0:1]
        means = sums * (1.0 / GSIZE)
        m2, m1 = spread(means), jnp.where(even(means), pltpu.roll(means, C - 1, 1), means)
        upstream = UR[fr(k)].astype(f32)
        gn = upstream * LO[fr(k)] * gain.reshape(1, 1, 1, C)
        nn = NO[fr(k)]
        inv = MI[k, 1:2]
        gc = (gn - m1.reshape(1, 1, 1, C) - nn * m2.reshape(1, 1, 1, C)) * inv.reshape(1, 1, 1, C)
        gc16 = jnp.where(valid > 0, gc, 0.0).astype(bf16)
        GG[0, k] = gc16[:, 1:5].reshape(POS, C)
        remote(GG.at[0, k], GG.at[1, k], s_pg.at[k], pg.at[k], (other, s, h))

        @pl.when(s > 0)
        def _():
            put_shifted(G, F * k, gc16.astype(f32))
            acc = None
            for ab in range(9):
                a, b = divmod(ab, 3)
                for c in range(3):
                    lhs = G[fr(k, a), b : b + R, :, C * c : C * c + C].reshape(POS, C)
                    t = 9 * (2 - a) + 3 * (2 - b) + 2 - c
                    d = lax.dot_general(
                        lhs, W[t * C : t * C + C, :], (((1,), (1,)), ((), ())), preferred_element_type=f32
                    )
                    acc = d if acc is None else acc + d
            u16 = (UR[fr(k), 1:5].astype(f32).reshape(POS, C) + acc).astype(bf16)
            gpre = u16.astype(f32) * LP[k]
            SBO[k] = gradient_summary(gpre, NP[k], GP[0:1])
            for b in bands:
                remote(SBO.at[k], SB.at[k, h], s_sb.at[k], sb.at[k], (dp, prv, b))
            UO[fr(k)] = u16.reshape(F, R, W16, C)

            @pl.when(s > 1)
            def _():
                send_edges(UO, 0, 3, UR, k, s_ur.at[k], ur.at[k], prv)

            remote(UO.at[fr(k)], UR.at[fr(k), pl.ds(1, R)], s_ur.at[k], ur.at[k], (dp, prv, h))

        @pl.when((s == 0) & ((dp == 1) | (k > 0)))
        def _():
            weight_grad(0, k)

        if i == 0:

            @pl.when((s == 0) & (dp == 0))
            def _():
                await_bytes(GG.at[1, 0], pg.at[0])
                weight_grad(1, 0)

    @pl.when((s == 0) & (dp == 0))
    def _():
        def term(i, carry):
            k = SPANS - 1 - i
            await_bytes(GG.at[1, k], pg.at[k])
            weight_grad(1, k)
            return carry

        lax.fori_loop(0, SPANS - 1, term, 0)

    for i in range(SPANS):
        backward(i)

    @pl.when((s > 0) | (dp == 1))
    def _():
        await_bytes(GG.at[1, 2], pg.at[2])
        await_bytes(GG.at[1, 1], pg.at[1])

    @pl.when((s > 0) & (dp == 0))
    def _():
        await_bytes(GG.at[1, 0], pg.at[0])

    def term(t, carry):
        late = (t >= 2 + dp).astype(jnp.int32)
        weight_grad(late, SPANS - 1 - (t - late * (2 + dp)))
        return carry

    lax.fori_loop(jnp.where(s > 0, 0, jnp.where(dp == 1, 3, 5)), 5, term, 0)

    @pl.when(dp == 1)
    def _():
        await_bytes(GG.at[1, 0], pg.at[0])

    for q in range(4):
        part(q, dp, 0)
        if q > 0:
            first_phase(q - 1)
    middle(dp, 0)
    first_phase(3)
    first_phase_rest()

    def norm_terms(k, total):
        gpre = (UR[fr(k), 1:5].astype(f32) * LO[fr(k), 1:5]).reshape(POS, C)
        both = jnp.concatenate(
            [
                jnp.sum(gpre * NO[fr(k), 1:5].reshape(POS, C), axis=0, keepdims=True),
                jnp.sum(gpre, axis=0, keepdims=True),
            ],
            axis=0,
        )
        return total + both

    NT[h] = lax.fori_loop(0, SPANS, norm_terms, jnp.zeros((2, C), f32))
    for b in bands[:-1]:
        remote(NT.at[h], NT.at[h], s_nt, nt, (dp, s, b))

    def total(r, *at):
        return sum(r[(j, *at)].astype(f32) for j in range(3))

    for i, (n, t0) in enumerate(cuts):
        span = pl.ds(t0, n)
        await_bytes(A1R.at[:, :, span], a1.at[i])
        for dy in range(1, 4):
            y = lax.rem(yy + dy, 4)
            A2S[dy - 1, span] = (tiles((4 * zz + y) * SHARE + 8 * t0, n) + total(A1R, y, span)).astype(bf16)
            remote(A2S.at[dy - 1, span], A2R.at[dy - 1, span], s_a2, a2, (dp, s, 4 * zz + y))
        n = min(n, TB - t0)
        span = pl.ds(t0, n)
        await_bytes(B1R.at[:, :, span], b1.at[i])
        for dz in range(1, 4):
            z = lax.rem(zz + dz, 4)
            row = (4 * z + yy) * SHARE + 8 * (TA + t0)
            B2S[dz - 1, span] = (tiles(row, n) + total(B1R, z, span)).astype(bf16)
            remote(B2S.at[dz - 1, span], B2R.at[dz - 1, span], s_b2, b2, (dp, s, 4 * z + yy))
    await_bytes(NT.at[pl.ds(0, NB - 1)], nt)
    NG[0] = jnp.sum(NT[...], axis=0)
    remote(NG.at[0], NG.at[1], s_ng, ngs, (other, s, h))
    mine_a = tiles(h * SHARE, TA) + total(A1R, yy)
    mine_b = tiles(h * SHARE + 8 * TA, TB) + total(B1R, zz)
    await_bytes(A2R, a2)
    out_k[0, 0 : 8 * TA] = rows(mine_a + total(A2R))
    await_bytes(B2R, b2)
    out_k[0, 8 * TA : SHARE] = rows(mine_b + total(B2R))
    await_bytes(NG.at[1], ngs)
    out_n[0] = NG[0] + NG[1]

    for k in range(SPANS):
        await_bytes(STO.at[k, pl.ds(0, NB - 1)], s_sto.at[k])
        await_edges(CF, k, s_ch.at[k])
        await_bytes(PX.at[fr(k)], s_px.at[k])
        await_bytes(GG.at[0, k], s_pg.at[k])

        @pl.when(s < LAYERS - 1)
        def _():
            await_bytes(STP.at[k], s_stn.at[k])
            await_edges(CP, k, s_c.at[k], R)

        @pl.when(s <= 1)
        def _():
            await_bytes(XN.at[fr(k)], s_x.at[k])

            await_edges(XP, k, s_xr.at[k])

        @pl.when(s == 1)
        def _():
            await_edges(XP, k, s_xn.at[k])

        @pl.when(s > 0)
        def _():
            await_bytes(SB.at[k], s_sb.at[k])

        @pl.when(s > 1)
        def _():
            await_edges(UR, k, s_ur.at[k], R)

        @pl.when(s == 1)
        def _():
            await_bytes(UR.at[fr(k), pl.ds(1, R)], s_ur.at[k])

        @pl.when(s == LAYERS - 1)
        def _():
            await_edges(XP, k, s_rl.at[k], R)
            await_edges(UR, k, s_og.at[k])
            await_bytes(SB.at[k, pl.ds(0, NB - 1)], s_sbo.at[k])

    @pl.when(s < LAYERS - 1)
    def _():
        await_bytes(GO, s_gp)

    await_bytes(NG.at[0], s_ng)
    await_bytes(NT.at[pl.ds(0, NB - 1)], s_nt)
    for i, (n, t0) in enumerate(cuts):
        await_bytes(A1R.at[:, :, pl.ds(t0, n)], s_a1.at[i])
        await_bytes(B1R.at[:, :, pl.ds(t0, min(n, TB - t0))], s_b1.at[i])
    await_bytes(A2R, s_a2)
    await_bytes(B2R, s_b2)


def per_device(video, kernels, gains, shifts, out_grad):
    dma = pltpu.SemaphoreType.DMA
    six = (F * SPANS, 6, W16, C)
    four = (F * SPANS, R, W16, C)
    wide = (F * SPANS + 2, 6, W16, 3 * C)
    scratch = [
        pltpu.VMEM((27 * C, C), bf16),
        pltpu.VMEM(six, bf16),
        pltpu.VMEM(six, bf16),
        pltpu.VMEM(four, bf16),
        pltpu.VMEM(four, bf16),
        pltpu.VMEM(six, bf16),
        pltpu.VMEM(four, bf16),
        pltpu.VMEM(six, f32),
        pltpu.VMEM((2,) + wide, bf16),
        pltpu.VMEM(six, bf16),
        pltpu.VMEM(wide, bf16),
        pltpu.VMEM((2, SPANS, POS, C), bf16),
        pltpu.VMEM(six, bf16),
        pltpu.VMEM(four, bf16),
        pltpu.VMEM((SPANS, NB, 1, C), f32),
        pltpu.VMEM((SPANS, NB, 1, C), f32),
        pltpu.VMEM((SPANS, NB, 1, C), f32),
        pltpu.VMEM((SPANS, 1, C), f32),
        pltpu.VMEM((2, C), f32),
        pltpu.VMEM((2, C), f32),
        pltpu.VMEM((SPANS, POS, C), f32),
        pltpu.VMEM((SPANS, POS, C), f32),
        pltpu.VMEM(six, f32),
        pltpu.VMEM(six, f32),
        pltpu.VMEM((SPANS, 2, C), f32),
        pltpu.VMEM((HALF, C), f32),
        pltpu.VMEM((4, 4, 14, 16, 128), bf16),
        pltpu.VMEM((3, 4, 14, 16, 128), bf16),
        pltpu.VMEM((4, 4, 13, 16, 128), bf16),
        pltpu.VMEM((3, 4, 13, 16, 128), bf16),
        pltpu.VMEM((3, 14, 16, 128), bf16),
        pltpu.VMEM((3, 14, 16, 128), bf16),
        pltpu.VMEM((3, 13, 16, 128), bf16),
        pltpu.VMEM((3, 13, 16, 128), bf16),
        pltpu.VMEM((2, 2, C), f32),
        pltpu.VMEM((NB, 2, C), f32),
    ]
    k3 = dma((SPANS,))
    two = dma((2,))
    sems = [pltpu.SemaphoreType.REGULAR, dma] + [k3] * 11 + [two, two] + [dma] * 5
    sems += [k3] * 14 + [two, two] + [dma] * 5
    anyspec = pl.BlockSpec(memory_space=pl.ANY)
    vm = pl.BlockSpec(memory_space=pltpu.VMEM)
    return pl.pallas_call(
        kernel,
        out_shape=(
            pltpu.VMEM((1, SHARE, C), f32),
            pltpu.VMEM((1, 2, C), f32),
        ),
        in_specs=[anyspec, anyspec, vm, vm, anyspec],
        out_specs=(vm, vm),
        scratch_shapes=scratch + sems,
        compiler_params=pltpu.CompilerParams(
            collective_id=0, has_side_effects=True, vmem_limit_bytes=60 * 2**20
        ),
    )(video, kernels, gains, shifts, out_grad)


def solution(mesh):
    return jax.shard_map(
        per_device,
        mesh=mesh,
        in_specs=(
            P("dp", None, "height", None, None),
            P("pipe", None, None),
            P("pipe", None),
            P("pipe", None),
            P("dp", None, "height", None, None),
        ),
        out_specs=(P("pipe", ("dp", "height"), None), P("pipe", None, None)),
        check_vma=False,
    )
```

```python
import functools

import jax
import jax.numpy as jnp
from jax import lax
from jax.experimental import pallas as pl
from jax.experimental.pallas import tpu as pltpu
from jax.sharding import PartitionSpec as P

GROUPS = 32
F = 4
SPANS = 3
NB = 16
LAYERS = 4
R = 4
W16 = 16
C = 256
POS = F * R * W16
GSIZE = float(POS * NB * (C // GROUPS))
HALF = 3456
SHARE = 216
EPS = 1e-05
f32 = jnp.float32
bf16 = jnp.bfloat16
MESH = pl.DeviceIdType.MESH


def group_mate(x, d):
    lane = lax.broadcasted_iota(jnp.int32, x.shape, 1)
    return jnp.where((lane & d) != 0, pltpu.roll(x, d, 1), pltpu.roll(x, C - d, 1))


def group_sum(x):
    for d in (1, 2, 4):
        x = x + group_mate(x, d)
    return x


def even(x):
    return (lax.broadcasted_iota(jnp.int32, x.shape, 1) & 1) == 0


def spread(x):
    return jnp.where(even(x), x, pltpu.roll(x, 1, 1))


def summary(mean_c, dev_c):
    both = jnp.concatenate([mean_c, dev_c], axis=0)
    count = float(POS)
    for d in (1, 2, 4):
        mate = group_mate(both, d)
        gap = both[0:1] - mate[0:1]
        both = jnp.concatenate(
            [0.5 * (both[0:1] + mate[0:1]), both[1:2] + mate[1:2] + (0.5 * count) * gap * gap], axis=0
        )
        count = 2.0 * count
    return both[0:1], jnp.where(even(mean_c), both[0:1], both[1:2])


def gradient_summary(gpre, normed, gain):
    sums = jnp.concatenate(
        [jnp.sum(gpre * normed, axis=0, keepdims=True), jnp.sum(gpre, axis=0, keepdims=True)], axis=0
    )
    sums = group_sum(sums * gain)
    return jnp.where(even(gain), sums[0:1], sums[1:2])


def combine(table):
    sums = jnp.sum(table, axis=0)
    mean = sums * (1.0 / NB)
    between = jnp.sum((table - mean[None]) ** 2, axis=0)
    dev = pltpu.roll(sums, C - 1, 1) + (GSIZE / NB) * between
    both = spread(jnp.concatenate([mean, lax.rsqrt(dev * (1.0 / GSIZE) + EPS)], axis=0))
    return both[0:1], both[1:2]


def sigmoid(v):
    return 0.5 * jnp.tanh(0.5 * v) + 0.5


def put_shifted(dst, frame, x):
    n = x.shape[1]
    v = x.reshape(F * n, W16, C)
    col = lax.broadcasted_iota(jnp.int32, v.shape, 1)
    left = jnp.where(col == 0, 0.0, pltpu.roll(v, 1, 1))
    right = jnp.where(col == W16 - 1, 0.0, pltpu.roll(v, W16 - 1, 1))
    for c, part in enumerate((left, v, right)):
        dst[pl.ds(frame, F), :, :, C * c : C * c + C] = part.astype(bf16).reshape(F, n, W16, C)


def kernel(
    video, kern, gains, shifts, ograd, out_k, out_n,
    W, XP, XR, XN, RL, CP, CO, CF, SS, PX, G, GG, UR, UO, STP, STO, SB, SBO, GO, GP, NP, LP, NO, LO, MI,
    WG, A1S, A1R, B1S, B1R, A2S, A2R, B2S, B2R, NG, NT,
    ready, w_sem, xpc, xph, rl, cp, stp, sto, cfh, ur, sb, px, pg, a1, b1, a2, b2, ngs, gps, nt,
    s_x, s_xn, s_xr, s_rl, s_c, s_ch, s_sto, s_stn, s_px, s_pg, s_ur, s_og, s_sb, s_sbo, s_a1, s_b1, s_a2, s_b2, s_ng, s_gp, s_nt,
):
    dp, s, h = lax.axis_index("dp"), lax.axis_index("pipe"), lax.axis_index("height")
    nxt, prv = lax.rem(s + 1, LAYERS), lax.rem(s + LAYERS - 1, LAYERS)
    up, dn = lax.rem(h + NB - 1, NB), lax.rem(h + 1, NB)
    other = 1 - dp
    zz, yy = lax.div(h, 4), lax.rem(h, 4)
    steps = [(i, j) for i in range(4) for j in range(4)]
    steps.sort(key=lambda o: -(min(o[0], 4 - o[0]) + min(o[1], 4 - o[1])))
    bands = [lax.rem(zz + i, 4) * 4 + lax.rem(yy + j, 4) for i, j in steps]

    def remote(src, dst, ssem, rsem, dev):
        pltpu.make_async_remote_copy(
            src_ref=src, dst_ref=dst, send_sem=ssem, recv_sem=rsem, device_id=dev, device_id_type=MESH
        ).start()

    def await_bytes(ref, sem):
        pltpu.make_async_copy(ref, ref, sem).wait()

    inside = (h > 0) & (h < NB - 1)

    def await_edges(ref, k, sem, rows=0):
        @pl.when(inside)
        def _():
            await_bytes(ref.at[fr(k), pl.ds(0, rows + 2)], sem)

        @pl.when(jnp.logical_not(inside))
        def _():
            await_bytes(ref.at[fr(k), pl.ds(0, rows + 1)], sem)

    def send_edges(src, first, last, dst, k, ssem, rsem, layer):
        @pl.when(h > 0)
        def _():
            remote(src.at[fr(k), pl.ds(first, 1)], dst.at[fr(k), pl.ds(5, 1)], ssem, rsem, (dp, layer, up))

        @pl.when(h < NB - 1)
        def _():
            remote(src.at[fr(k), pl.ds(last, 1)], dst.at[fr(k), pl.ds(0, 1)], ssem, rsem, (dp, layer, dn))

    def fr(k, first=0):
        return pl.ds(F * k + first, F)

    wcopy = pltpu.make_async_copy(kern.at[0], W, w_sem)
    wcopy.start()
    barrier = pltpu.get_barrier_semaphore()
    far = lax.rem(s + 2, LAYERS)

    @pl.when(s == LAYERS - 1)
    def _():
        @pl.when(h > 0)
        def _():
            pl.semaphore_signal(barrier, inc=1, device_id=(dp, far, up), device_id_type=MESH)

        @pl.when(h < NB - 1)
        def _():
            pl.semaphore_signal(barrier, inc=1, device_id=(dp, far, dn), device_id_type=MESH)

        pl.semaphore_signal(barrier, inc=1, device_id=(dp, far, h), device_id_type=MESH)

    for b in bands[:-1]:
        pl.semaphore_signal(barrier, inc=1, device_id=(dp, s, b), device_id_type=MESH)
    for p in (nxt, prv):
        pl.semaphore_signal(barrier, inc=1, device_id=(dp, p, h), device_id_type=MESH)
    pl.semaphore_signal(barrier, inc=1, device_id=(other, s, h), device_id_type=MESH)

    @pl.when(s <= 1)
    def _():
        for k in range(SPANS):
            pltpu.make_async_copy(video.at[0, fr(k)], XP.at[fr(k), pl.ds(1, R)], xpc.at[k]).start()

    @pl.when(s == LAYERS - 1)
    def _():
        for k in range(SPANS):
            pltpu.make_async_copy(ograd.at[0, fr(k)], UR.at[fr(k), pl.ds(1, R)], ur.at[k]).start()

    SS[:, 0:2] = jnp.zeros((2, 2, 6, W16, 3 * C), bf16)
    G[12:14] = jnp.zeros((2, 6, W16, 3 * C), bf16)
    GO[0:1] = gains[...]
    GO[1:2] = shifts[...]
    from_far = (h > 0).astype(jnp.int32) + (h < NB - 1).astype(jnp.int32) + 1
    pl.semaphore_wait(barrier, NB - 1 + 2 + 1 + jnp.where(s == 1, from_far, 0))
    for p in (nxt, prv):
        pl.semaphore_signal(ready, inc=1, device_id=(dp, p, h), device_id_type=MESH)

    @pl.when(s <= 1)
    def _():
        for k in range(SPANS):
            send_edges(video.at[0], 0, 3, XP, k, s_xr.at[k], xph.at[k], s)

    @pl.when(s == LAYERS - 1)
    def _():
        for k in reversed(range(SPANS)):
            send_edges(ograd.at[0], 0, 3, UR, k, s_og.at[k], ur.at[k], s)

    @pl.when(s < LAYERS - 1)
    def _():
        remote(GO, GP, s_gp, gps, (dp, nxt, h))

    @pl.when(s > 0)
    def _():
        await_bytes(GP, gps)

    row = lax.broadcasted_iota(jnp.int32, (1, 6, 1, 1), 1)
    valid = jnp.where(row == 0, (h > 0).astype(f32), jnp.where(row == 5, (h < NB - 1).astype(f32), 1.0))

    def normalized(conv, table_ref, k):
        mu, inv = combine(table_ref[k])
        own = (spread(table_ref[k, h]) - mu).reshape(1, 1, 1, C)
        above = (spread(table_ref[k, up]) - mu).reshape(1, 1, 1, C)
        below = (spread(table_ref[k, dn]) - mu).reshape(1, 1, 1, C)
        off = jnp.concatenate([above, own, own, own, own, below], axis=1)
        return (conv + off) * inv.reshape(1, 1, 1, C)

    gain4 = GO[0:1].reshape(1, 1, 1, C)
    shift4 = GO[1:2].reshape(1, 1, 1, C)

    def layer(k):
        await_bytes(XP.at[fr(k), pl.ds(1, R)], xpc.at[k])

        await_edges(XP, k, xph.at[k])

        @pl.when(s == 0)
        def _():
            x = jnp.where(valid > 0, XP[fr(k)].astype(f32), 0.0)
            XR[fr(k)] = x.astype(bf16)
            put_shifted(SS.at[0], 2 + F * k, x)

        @pl.when(s > 0)
        def _():
            await_bytes(STP.at[k], stp.at[k])
            await_edges(CP, k, cp.at[k], R)
            normed = normalized(CP[fr(k)].astype(f32), STP, k)
            pre = normed * GP[0:1].reshape(1, 1, 1, C) + GP[1:2].reshape(1, 1, 1, C)
            x = XP[fr(k)].astype(f32) + pre * sigmoid(pre)
            x16 = jnp.where(valid > 0, x, 0.0).astype(bf16)
            XR[fr(k)] = x16
            put_shifted(SS.at[0], 2 + F * k, x16.astype(f32))
            NP[k] = normed[:, 1:5].reshape(POS, C)

        @pl.when(k == 0)
        def _():
            wcopy.wait()

        acc = None
        for ab in range(9):
            a, b = divmod(ab, 3)
            lhs = SS[0, fr(k, a), b : b + R].reshape(POS, 3 * C)
            d = jnp.dot(lhs, W[ab * 768 : ab * 768 + 768, :], preferred_element_type=f32)
            acc = d if acc is None else acc + d
        mean = jnp.sum(acc, axis=0, keepdims=True) * (1.0 / POS)
        mean, STO[k, h] = summary(mean, jnp.sum((acc - mean) ** 2, axis=0, keepdims=True))
        cen = acc - mean

        @pl.when((s < LAYERS - 1) & (k == 0))
        def _():
            pl.semaphore_wait(ready, 2)

        @pl.when(s < LAYERS - 1)
        def _():
            for b in bands:
                remote(STO.at[k, h], STP.at[k, h], s_stn.at[k], stp.at[k], (dp, nxt, b))

        for b in bands[:-1]:
            remote(STO.at[k, h], STO.at[k, h], s_sto.at[k], sto.at[k], (dp, s, b))

        CF[fr(k), 1:5] = cen.reshape(F, R, W16, C)
        CO[fr(k)] = cen.astype(bf16).reshape(F, R, W16, C)

        @pl.when(s < LAYERS - 1)
        def _():
            send_edges(CO, 0, 3, CP, k, s_c.at[k], cp.at[k], nxt)
            remote(CO.at[fr(k)], CP.at[fr(k), pl.ds(1, R)], s_c.at[k], cp.at[k], (dp, nxt, h))

        send_edges(CF, 1, 4, CF, k, s_ch.at[k], cfh.at[k], s)
        remote(XR.at[fr(k)], PX.at[fr(k)], s_px.at[k], px.at[k], (other, s, h))

    def own_rows(k):
        await_bytes(STO.at[k, pl.ds(0, NB - 1)], sto.at[k])
        mu, inv = combine(STO[k])
        MI[k] = jnp.concatenate([mu, inv], axis=0)
        off = (spread(STO[k, h]) - mu).reshape(1, 1, 1, C)
        normed = (CF[fr(k), 1:5] + off) * inv.reshape(1, 1, 1, C)
        pre = normed * gain4 + shift4
        sig = sigmoid(pre)
        slope = sig * (1.0 + pre * (1.0 - sig))
        NO[fr(k), 1:5] = normed
        LO[fr(k), 1:5] = slope

        @pl.when(s <= 1)
        def _():
            XN[fr(k)] = (XR[fr(k), 1:5].astype(f32) + pre * sig).astype(bf16)

        @pl.when(s == 0)
        def _():
            remote(XN.at[fr(k)], RL.at[fr(k)], s_x.at[k], rl.at[k], (dp, prv, h))

        @pl.when(s == 1)
        def _():
            far = lax.rem(s + 2, LAYERS)
            send_edges(XN, 0, 3, XP, k, s_xn.at[k], xph.at[k], far)
            remote(XN.at[fr(k)], XP.at[fr(k), pl.ds(1, R)], s_x.at[k], xpc.at[k], (dp, far, h))

        @pl.when(s == LAYERS - 1)
        def _():
            await_edges(UR, k, ur.at[k], R)
            gpre = (UR[fr(k), 1:5].astype(f32) * slope).reshape(POS, C)
            nn = normed.reshape(POS, C)
            SB[k, h] = gradient_summary(gpre, nn, GO[0:1])
            for b in bands[:-1]:
                remote(SB.at[k, h], SB.at[k, h], s_sbo.at[k], sb.at[k], (dp, s, b))

    def own_halo(k):
        await_edges(CF, k, cfh.at[k])
        mu, inv = MI[k, 0:1], MI[k, 1:2]
        for r, b in ((0, up), (5, dn)):
            off = (spread(STO[k, b]) - mu).reshape(1, 1, 1, C)
            normed = (CF[fr(k), r : r + 1] + off) * inv.reshape(1, 1, 1, C)
            pre = normed * gain4 + shift4
            sig = sigmoid(pre)
            NO[fr(k), r : r + 1] = normed
            LO[fr(k), r : r + 1] = sig * (1.0 + pre * (1.0 - sig))

    @pl.when(s == LAYERS - 1)
    def _():
        pl.semaphore_wait(ready, 2)
        for k in range(SPANS):
            await_bytes(RL.at[fr(k)], rl.at[k])
            send_edges(RL, 0, 3, XP, k, s_rl.at[k], xph.at[k], prv)
            remote(RL.at[fr(k)], XP.at[fr(k), pl.ds(1, R)], s_rl.at[k], xpc.at[k], (dp, prv, h))

    def forward(k, carry):
        layer(k)
        return carry

    lax.fori_loop(0, SPANS, forward, 0)

    def own(k, carry):
        own_rows(k)
        return carry

    lax.fori_loop(0, SPANS, own, 0)

    def halo(i, carry):
        own_halo(SPANS - 1 - i)

        @pl.when(s > 0)
        def _():
            pre = NP[i] * GP[0:1] + GP[1:2]
            sig = sigmoid(pre)
            LP[i] = sig * (1.0 + pre * (1.0 - sig))

        return carry

    lax.fori_loop(0, SPANS, halo, 0)

    def partner(k, carry):
        await_bytes(PX.at[fr(k)], px.at[k])
        put_shifted(SS.at[1], 2 + F * k, PX[fr(k)].astype(f32))
        return carry

    lax.fori_loop(0, SPANS, partner, 0)
    WG[...] = jnp.zeros((HALF, C), f32)

    def add_rows(off, rows, lhs, side, k):
        WG[pl.ds(off, rows), :] += lax.dot_general(
            lhs, GG[side, k], (((0,), (0,)), ((), ())), preferred_element_type=f32
        )

    def part(q, side, k):
        ab = q + dp * (8 - 2 * q)
        a, b = lax.div(ab, 3), lax.rem(ab, 3)
        off = pl.multiple_of(ab * 768 - HALF * dp, 128)
        add_rows(off, 768, SS[side, fr(k, a), pl.ds(b, R)].reshape(POS, 3 * C), side, k)

    def middle(side, k):
        off = pl.multiple_of((HALF - 384) * (1 - dp), 128)
        full = SS[side, fr(k, 1), 1 : 1 + R].reshape(POS, 3 * C)
        add_rows(off, 384, jnp.where(dp == 0, full[:, 0:384], full[:, 384:768]), side, k)

    def weight_grad(side, k):
        for q in range(4):
            part(q, side, k)
        middle(side, k)

    TA, TB = 14, 13
    cuts = ((12, 0), (2, 12))

    def tiles(row, n):
        v = WG[pl.ds(pl.multiple_of(row, 8), 8 * n), :].reshape(n, 8, C)
        return jnp.concatenate([v[:, :, 0:128], v[:, :, 128:256]], axis=1)

    def rows(t):
        return jnp.concatenate([t[:, 0:8], t[:, 8:16]], axis=2).reshape(8 * t.shape[0], C)

    def first_phase(m):
        z = m + dp * (3 - 2 * m)
        for y in range(4):
            row = (4 * z + y) * SHARE
            A1S[z, y] = tiles(row, TA).astype(bf16)
            B1S[y, z] = tiles(row + 8 * TA, TB).astype(bf16)
        dz = lax.rem(z - zz + 4, 4)
        n, _ = cuts[0]

        @pl.when(dz != 0)
        def _():
            remote(
                A1S.at[z, :, pl.ds(0, n)], A1R.at[dz - 1, :, pl.ds(0, n)], s_a1.at[0], a1.at[0], (dp, s, 4 * z + yy)
            )

        for dy in range(1, 4):
            y = lax.rem(yy + dy, 4)
            remote(
                B1S.at[y, z, pl.ds(0, n)], B1R.at[dy - 1, z, pl.ds(0, n)], s_b1.at[0], b1.at[0], (dp, s, 4 * zz + y)
            )

    def first_phase_rest():
        n = cuts[0][0]
        for d in range(1, 4):
            z, y = lax.rem(zz + d, 4), lax.rem(yy + d, 4)
            rest = pl.ds(n, TA - n)
            remote(A1S.at[z, :, rest], A1R.at[d - 1, :, rest], s_a1.at[1], a1.at[1], (dp, s, 4 * z + yy))
            rest = pl.ds(n, TB - n)
            remote(B1S.at[y, :, rest], B1R.at[d - 1, :, rest], s_b1.at[1], b1.at[1], (dp, s, 4 * zz + y))

    def backward(i):
        k = SPANS - 1 - i

        @pl.when(s < LAYERS - 1)
        def _():
            await_bytes(SB.at[k], sb.at[k])

        @pl.when((s > 0) & (s < LAYERS - 1))
        def _():
            await_edges(UR, k, ur.at[k], R)

        @pl.when(s == 0)
        def _():
            await_bytes(UR.at[fr(k), pl.ds(1, R)], ur.at[k])

        @pl.when(s == LAYERS - 1)
        def _():
            await_bytes(SB.at[k, pl.ds(0, NB - 1)], sb.at[k])

        sums = jnp.sum(SB[k], axis=0)
        gain = GO[0:1]
        means = sums * (1.0 / GSIZE)
        m2, m1 = spread(means), jnp.where(even(means), pltpu.roll(means, C - 1, 1), means)
        upstream = UR[fr(k)].astype(f32)
        gn = upstream * LO[fr(k)] * gain.reshape(1, 1, 1, C)
        nn = NO[fr(k)]
        inv = MI[k, 1:2]
        gc = (gn - m1.reshape(1, 1, 1, C) - nn * m2.reshape(1, 1, 1, C)) * inv.reshape(1, 1, 1, C)
        gc16 = jnp.where(valid > 0, gc, 0.0).astype(bf16)
        GG[0, k] = gc16[:, 1:5].reshape(POS, C)

        @pl.when(s == 0)
        def _():
            remote(GG.at[0, k], GG.at[1, k], s_pg.at[k], pg.at[k], (other, s, h))

        @pl.when(s > 0)
        def _():
            put_shifted(G, F * k, gc16.astype(f32))
            acc = None
            for ab in range(9):
                a, b = divmod(ab, 3)
                for c in range(3):
                    lhs = G[fr(k, a), b : b + R, :, C * c : C * c + C].reshape(POS, C)
                    t = 9 * (2 - a) + 3 * (2 - b) + 2 - c
                    d = lax.dot_general(
                        lhs, W[t * C : t * C + C, :], (((1,), (1,)), ((), ())), preferred_element_type=f32
                    )
                    acc = d if acc is None else acc + d
            u16 = (UR[fr(k), 1:5].astype(f32).reshape(POS, C) + acc).astype(bf16)
            gpre = u16.astype(f32) * LP[k]
            SBO[k] = gradient_summary(gpre, NP[k], GP[0:1])
            for b in bands:
                remote(SBO.at[k], SB.at[k, h], s_sb.at[k], sb.at[k], (dp, prv, b))
            UO[fr(k)] = u16.reshape(F, R, W16, C)

            @pl.when(s > 1)
            def _():
                send_edges(UO, 0, 3, UR, k, s_ur.at[k], ur.at[k], prv)

            remote(UO.at[fr(k)], UR.at[fr(k), pl.ds(1, R)], s_ur.at[k], ur.at[k], (dp, prv, h))
            remote(GG.at[0, k], GG.at[1, k], s_pg.at[k], pg.at[k], (other, s, h))

        @pl.when((s == 0) & ((dp == 1) | (k > 0)))
        def _():
            weight_grad(0, k)

        if i == 0:

            @pl.when((s == 0) & (dp == 0))
            def _():
                await_bytes(GG.at[1, 0], pg.at[0])
                weight_grad(1, 0)

    @pl.when((s == 0) & (dp == 0))
    def _():
        def term(i, carry):
            k = SPANS - 1 - i
            await_bytes(GG.at[1, k], pg.at[k])
            weight_grad(1, k)
            return carry

        lax.fori_loop(0, SPANS - 1, term, 0)

    for i in range(SPANS):
        backward(i)

    @pl.when((s > 0) | (dp == 1))
    def _():
        await_bytes(GG.at[1, 2], pg.at[2])
        await_bytes(GG.at[1, 1], pg.at[1])

    @pl.when((s > 0) & (dp == 0))
    def _():
        await_bytes(GG.at[1, 0], pg.at[0])

    def term(t, carry):
        late = (t >= 2 + dp).astype(jnp.int32)
        weight_grad(late, SPANS - 1 - (t - late * (2 + dp)))
        return carry

    lax.fori_loop(jnp.where(s > 0, 0, jnp.where(dp == 1, 3, 5)), 5, term, 0)

    @pl.when(dp == 1)
    def _():
        await_bytes(GG.at[1, 0], pg.at[0])

    for q in range(4):
        part(q, dp, 0)
        if q > 0:
            first_phase(q - 1)
    middle(dp, 0)
    first_phase(3)
    first_phase_rest()

    def norm_terms(k, total):
        gpre = (UR[fr(k), 1:5].astype(f32) * LO[fr(k), 1:5]).reshape(POS, C)
        both = jnp.concatenate(
            [
                jnp.sum(gpre * NO[fr(k), 1:5].reshape(POS, C), axis=0, keepdims=True),
                jnp.sum(gpre, axis=0, keepdims=True),
            ],
            axis=0,
        )
        return total + both

    NT[h] = lax.fori_loop(0, SPANS, norm_terms, jnp.zeros((2, C), f32))
    for b in bands[:-1]:
        remote(NT.at[h], NT.at[h], s_nt, nt, (dp, s, b))

    def total(r, *at):
        return sum(r[(j, *at)].astype(f32) for j in range(3))

    for i, (n, t0) in enumerate(cuts):
        span = pl.ds(t0, n)
        await_bytes(A1R.at[:, :, span], a1.at[i])
        for dy in range(1, 4):
            y = lax.rem(yy + dy, 4)
            A2S[dy - 1, span] = (tiles((4 * zz + y) * SHARE + 8 * t0, n) + total(A1R, y, span)).astype(bf16)
            remote(A2S.at[dy - 1, span], A2R.at[dy - 1, span], s_a2, a2, (dp, s, 4 * zz + y))
        n = min(n, TB - t0)
        span = pl.ds(t0, n)
        await_bytes(B1R.at[:, :, span], b1.at[i])
        for dz in range(1, 4):
            z = lax.rem(zz + dz, 4)
            row = (4 * z + yy) * SHARE + 8 * (TA + t0)
            B2S[dz - 1, span] = (tiles(row, n) + total(B1R, z, span)).astype(bf16)
            remote(B2S.at[dz - 1, span], B2R.at[dz - 1, span], s_b2, b2, (dp, s, 4 * z + yy))
    await_bytes(NT.at[pl.ds(0, NB - 1)], nt)
    NG[0] = jnp.sum(NT[...], axis=0)
    remote(NG.at[0], NG.at[1], s_ng, ngs, (other, s, h))
    mine_a = tiles(h * SHARE, TA) + total(A1R, yy)
    mine_b = tiles(h * SHARE + 8 * TA, TB) + total(B1R, zz)
    await_bytes(A2R, a2)
    out_k[0, 0 : 8 * TA] = rows(mine_a + total(A2R))
    await_bytes(B2R, b2)
    out_k[0, 8 * TA : SHARE] = rows(mine_b + total(B2R))
    await_bytes(NG.at[1], ngs)
    out_n[0] = NG[0] + NG[1]

    for k in range(SPANS):
        await_bytes(STO.at[k, pl.ds(0, NB - 1)], s_sto.at[k])
        await_edges(CF, k, s_ch.at[k])
        await_bytes(PX.at[fr(k)], s_px.at[k])
        await_bytes(GG.at[0, k], s_pg.at[k])

        @pl.when(s < LAYERS - 1)
        def _():
            await_bytes(STP.at[k], s_stn.at[k])
            await_edges(CP, k, s_c.at[k], R)

        @pl.when(s <= 1)
        def _():
            await_bytes(XN.at[fr(k)], s_x.at[k])

            await_edges(XP, k, s_xr.at[k])

        @pl.when(s == 1)
        def _():
            await_edges(XP, k, s_xn.at[k])

        @pl.when(s > 0)
        def _():
            await_bytes(SB.at[k], s_sb.at[k])

        @pl.when(s > 1)
        def _():
            await_edges(UR, k, s_ur.at[k], R)

        @pl.when(s == 1)
        def _():
            await_bytes(UR.at[fr(k), pl.ds(1, R)], s_ur.at[k])

        @pl.when(s == LAYERS - 1)
        def _():
            await_edges(XP, k, s_rl.at[k], R)
            await_edges(UR, k, s_og.at[k])
            await_bytes(SB.at[k, pl.ds(0, NB - 1)], s_sbo.at[k])

    @pl.when(s < LAYERS - 1)
    def _():
        await_bytes(GO, s_gp)

    await_bytes(NG.at[0], s_ng)
    await_bytes(NT.at[pl.ds(0, NB - 1)], s_nt)
    for i, (n, t0) in enumerate(cuts):
        await_bytes(A1R.at[:, :, pl.ds(t0, n)], s_a1.at[i])
        await_bytes(B1R.at[:, :, pl.ds(t0, min(n, TB - t0))], s_b1.at[i])
    await_bytes(A2R, s_a2)
    await_bytes(B2R, s_b2)


def per_device(video, kernels, gains, shifts, out_grad):
    dma = pltpu.SemaphoreType.DMA
    six = (F * SPANS, 6, W16, C)
    four = (F * SPANS, R, W16, C)
    wide = (F * SPANS + 2, 6, W16, 3 * C)
    scratch = [
        pltpu.VMEM((27 * C, C), bf16),
        pltpu.VMEM(six, bf16),
        pltpu.VMEM(six, bf16),
        pltpu.VMEM(four, bf16),
        pltpu.VMEM(four, bf16),
        pltpu.VMEM(six, bf16),
        pltpu.VMEM(four, bf16),
        pltpu.VMEM(six, f32),
        pltpu.VMEM((2,) + wide, bf16),
        pltpu.VMEM(six, bf16),
        pltpu.VMEM(wide, bf16),
        pltpu.VMEM((2, SPANS, POS, C), bf16),
        pltpu.VMEM(six, bf16),
        pltpu.VMEM(four, bf16),
        pltpu.VMEM((SPANS, NB, 1, C), f32),
        pltpu.VMEM((SPANS, NB, 1, C), f32),
        pltpu.VMEM((SPANS, NB, 1, C), f32),
        pltpu.VMEM((SPANS, 1, C), f32),
        pltpu.VMEM((2, C), f32),
        pltpu.VMEM((2, C), f32),
        pltpu.VMEM((SPANS, POS, C), f32),
        pltpu.VMEM((SPANS, POS, C), f32),
        pltpu.VMEM(six, f32),
        pltpu.VMEM(six, f32),
        pltpu.VMEM((SPANS, 2, C), f32),
        pltpu.VMEM((HALF, C), f32),
        pltpu.VMEM((4, 4, 14, 16, 128), bf16),
        pltpu.VMEM((3, 4, 14, 16, 128), bf16),
        pltpu.VMEM((4, 4, 13, 16, 128), bf16),
        pltpu.VMEM((3, 4, 13, 16, 128), bf16),
        pltpu.VMEM((3, 14, 16, 128), bf16),
        pltpu.VMEM((3, 14, 16, 128), bf16),
        pltpu.VMEM((3, 13, 16, 128), bf16),
        pltpu.VMEM((3, 13, 16, 128), bf16),
        pltpu.VMEM((2, 2, C), f32),
        pltpu.VMEM((NB, 2, C), f32),
    ]
    k3 = dma((SPANS,))
    two = dma((2,))
    sems = [pltpu.SemaphoreType.REGULAR, dma] + [k3] * 11 + [two, two] + [dma] * 5
    sems += [k3] * 14 + [two, two] + [dma] * 5
    anyspec = pl.BlockSpec(memory_space=pl.ANY)
    vm = pl.BlockSpec(memory_space=pltpu.VMEM)
    return pl.pallas_call(
        kernel,
        out_shape=(
            pltpu.VMEM((1, SHARE, C), f32),
            pltpu.VMEM((1, 2, C), f32),
        ),
        in_specs=[anyspec, anyspec, vm, vm, anyspec],
        out_specs=(vm, vm),
        scratch_shapes=scratch + sems,
        compiler_params=pltpu.CompilerParams(
            collective_id=0, has_side_effects=True, vmem_limit_bytes=60 * 2**20
        ),
    )(video, kernels, gains, shifts, out_grad)


def solution(mesh):
    return jax.shard_map(
        per_device,
        mesh=mesh,
        in_specs=(
            P("dp", None, "height", None, None),
            P("pipe", None, None),
            P("pipe", None),
            P("pipe", None),
            P("dp", None, "height", None, None),
        ),
        out_specs=(P("pipe", ("dp", "height"), None), P("pipe", None, None)),
        check_vma=False,
    )
```
